32 devices in a mesh: dp: 8 (over z, core), comp: 4 (over y, x).
Axes of the slice: x: 2, y: 2, z: 4, core: 2. Of those that a mesh axis runs over, the one named last changes fastest.
Arguments:
- points: bfloat16 [65536, 768], P(('dp', 'comp')), may hold values from -6 to 6
- candidates: int32 [512, 4], P(('dp', 'comp')), may hold values from 0 to 127, as said below
- means: bfloat16 [16384, 768], P(('dp', 'comp')), may hold values from -0.59765625 to 0.59765625
- inv_var: bfloat16 [16384, 768], P(('dp', 'comp')), may hold values from 0.5 to 1.5
- log_weight: bfloat16 [16384], P(('dp', 'comp')), may hold values from -12 to -9
Outputs:
- counts: float32 [16384], P(('dp', 'comp'))
- first_moment: float32 [16384, 768], P(('dp', 'comp'))
- second_moment: float32 [16384, 768], P(('dp', 'comp'))
- loglik: float32 [65536], P(('dp', 'comp'))
The draws below stay inside these ranges and needn't reach their ends.
Inputs may be any that keep to these rules, and one draw needn't show every extreme that they name: `candidates`: each row block names 4 different component blocks; all blocks b named by the row blocks of device index i along dp+comp satisfy (b // 4) % 4 == i % 4, that is, one owner group serves each device's rows.
All inputs are finite; a program needn't handle non-finite values.
Results may differ from the reference program's by a relative error of at most 0.028.
Values may be sent and summed in bfloat16 or wider, within the bound.
No kernel may reach another device: no remote copies, remote signals or barrier semaphores. Data moves between devices by JAX's collectives and lax.ppermute only.
A program may use at most 128 MiB of HBM per device.

```python
import math
import jax
import jax.numpy as jnp
from jax import lax

D = 768
CB = 128
RB = 128
CANDS = 4
BLK_OWN = 32
RB_DEV = 16
OWNERS = 4
SLABS = 8
BPD = 4
NB = 128
K = 16384
ROWS = 65536


def draw_candidates(key, part):
    total = RB_DEV * SLABS * OWNERS
    spacing = BLK_OWN // CANDS
    first_draw = jax.random.randint(jax.random.fold_in(key, 1), (total,), 0, BLK_OWN)
    second_draw = jax.random.randint(jax.random.fold_in(key, 2), (total,), 0, BLK_OWN)
    base_ids = first_draw * second_draw // BLK_OWN
    position = jnp.arange(total, dtype=jnp.int32) % RB_DEV
    base_ids = jnp.where(position == 0, BLK_OWN - 1, jnp.where(position == 1, 0, base_ids))
    offsets = jax.random.randint(jax.random.fold_in(key, 3), (total, CANDS), 0, spacing)
    slot_index = jnp.arange(CANDS, dtype=jnp.int32)[None, :]
    offsets = jnp.where(slot_index == 0, 0, offsets)
    group_ids = (base_ids[:, None] + slot_index * spacing + offsets) % BLK_OWN
    owner_index = jnp.arange(total, dtype=jnp.int32) // RB_DEV % OWNERS
    holder = group_ids // BPD
    return ((holder * OWNERS + owner_index[:, None]) * BPD + group_ids % BPD).astype(jnp.int32)


def level_of(key, dims, cuts, low, top_value):
    loudness = 1.0
    for axis_at, shards_of in cuts:
        draws = jax.random.uniform(jax.random.fold_in(jax.random.fold_in(key, 6), axis_at), (shards_of,), jnp.float32, low / len(cuts), top_value / len(cuts))
        loudness = loudness * jnp.repeat(jnp.exp(draws), dims[axis_at] // shards_of).reshape((-1,) + (1,) * (len(dims) - 1 - axis_at))
    return loudness


def bell_draw(rng, shape, scale, limit, shards=(), kind=jnp.bfloat16):
    result = jax.random.normal(rng, shape, jnp.float32) * scale
    if len(shards) > 0:
        result = level_of(rng, shape, shards, -0.22, 0.18) * result
    return jnp.clip(result, min=-limit, max=limit).astype(kind)


def setup_inputs(seed: int = 0) -> dict:
    key_of = jax.random.split(jax.random.key(seed), 6)
    return {
        "points": bell_draw(key_of[0], (ROWS, D), 1.0, 6.0, ((0, 32),)),
        "candidates": draw_candidates(jax.random.fold_in(key_of[5], 71), 0),
        "means": bell_draw(key_of[2], (K, D), 0.1, 0.59765625, ((0, 32),)),
        "inv_var": jnp.clip(1.0 + 0.1 * jax.random.normal(key_of[3], (K, D), jnp.float32), 0.5, 1.5).astype(jnp.bfloat16),
        "log_weight": jnp.clip(-12.0 + 3.0 * jax.random.uniform(key_of[4], (K,), jnp.float32) ** level_of(key_of[4], (K,), ((0, 32),), -0.2, 0.2), -12.0, -9.0).astype(jnp.bfloat16),
    }


def component_consts(mean_values, inv_values, log_values):
    mean_f = mean_values.astype(jnp.float32)
    inv_f = inv_values.astype(jnp.float32)
    return (log_values.astype(jnp.float32) + 0.5 * jnp.sum(jnp.log(inv_f), axis=1)
            - 0.5 * jnp.sum(inv_f * mean_f * mean_f, axis=1) - 0.5 * D * math.log(2.0 * math.pi))


def block_terms(row_block, chosen_ids, scaled, inverse, constants):
    row_f = row_block.astype(jnp.float32)
    squares = (row_f * row_f).astype(jnp.bfloat16)
    square_f = squares.astype(jnp.float32)
    chosen_scaled = scaled[chosen_ids].astype(jnp.float32)
    chosen_inverse = inverse[chosen_ids].astype(jnp.float32)
    chosen_consts = constants[chosen_ids]
    linear = jnp.einsum('grd,gskd->grsk', row_f, chosen_scaled, precision=lax.Precision.HIGHEST)
    quadratic = jnp.einsum('grd,gskd->grsk', square_f, chosen_inverse, precision=lax.Precision.HIGHEST)
    densities = chosen_consts[:, None] + linear - 0.5 * quadratic
    row_peak = jnp.max(densities, axis=(2, 3))
    normalizer = row_peak + jnp.log(jnp.sum(jnp.exp(densities - row_peak[:, :, None, None]), axis=(2, 3)))
    responsibility = jnp.exp(densities - normalizer[:, :, None, None]).astype(jnp.bfloat16)
    weights = responsibility.astype(jnp.float32)
    counts = jnp.sum(weights, axis=1)
    first_moment = jnp.einsum('grsk,grd->gskd', weights, row_f, precision=lax.Precision.HIGHEST)
    second_moment = jnp.einsum('grsk,grd->gskd', weights, square_f, precision=lax.Precision.HIGHEST)
    return normalizer, counts, first_moment, second_moment


def reference(points, candidates, means, inv_var, log_weight):
    scaled = (inv_var.astype(jnp.float32) * means.astype(jnp.float32)).astype(jnp.bfloat16).reshape(NB, CB, D)
    inverse = inv_var.reshape(NB, CB, D)
    constants = component_consts(means, inv_var, log_weight).reshape(NB, CB)
    device_rows = points.reshape(SLABS * OWNERS, RB_DEV, RB, D)
    device_ids = candidates.reshape(SLABS * OWNERS, RB_DEV, CANDS).astype(jnp.int32)
    owner_seq = jnp.arange(SLABS * OWNERS, dtype=jnp.int32) % OWNERS
    group_index = jnp.arange(BLK_OWN, dtype=jnp.int32)

    def per_device(running, inputs):
        row_block, chosen_ids, owner_index = inputs
        normalizer, counts, first_part, second_part = block_terms(row_block, chosen_ids, scaled, inverse, constants)
        local_ids = ((chosen_ids // (OWNERS * BPD)) * BPD + chosen_ids % BPD).reshape(-1)
        part_counts = jnp.zeros((BLK_OWN, CB), jnp.float32).at[local_ids].add(counts.reshape(-1, CB))
        part_first = jnp.zeros((BLK_OWN, CB, D), jnp.float32).at[local_ids].add(first_part.reshape(-1, CB, D))
        part_second = jnp.zeros((BLK_OWN, CB, D), jnp.float32).at[local_ids].add(second_part.reshape(-1, CB, D))
        rounded = lax.optimization_barrier((part_counts.astype(jnp.bfloat16), part_first.astype(jnp.bfloat16),
                                            part_second.astype(jnp.bfloat16)))
        global_ids = ((group_index // BPD) * OWNERS + owner_index) * BPD + group_index % BPD
        running = (running[0].at[global_ids].add(rounded[0].astype(jnp.float32)),
                   running[1].at[global_ids].add(rounded[1].astype(jnp.float32)),
                   running[2].at[global_ids].add(rounded[2].astype(jnp.float32)))
        return running, normalizer.reshape(-1)

    initial = (jnp.zeros((NB, CB), jnp.float32), jnp.zeros((NB, CB, D), jnp.float32),
               jnp.zeros((NB, CB, D), jnp.float32))
    totals, normalizers = lax.scan(per_device, initial, (device_rows, device_ids, owner_seq))
    loglik = normalizers.reshape(-1) / D
    return (totals[0].reshape(K), totals[1].reshape(K, D), totals[2].reshape(K, D), loglik)
```

```python
import functools
import math

import jax
import jax.numpy as jnp
from jax import lax
from jax.experimental import pallas as pl
from jax.experimental.pallas import tpu as pltpu
from jax.sharding import PartitionSpec as P

CB = 128
RB = 128
CANDS = 4
VMEM_LIMIT = 56 * 1024 * 1024
NT = (((1,), (1,)), ((), ()))


def component_consts(mean_values, inv_values, log_values):
    feature_count = mean_values.shape[1]
    mean_f = mean_values.astype(jnp.float32)
    inv_f = inv_values.astype(jnp.float32)
    return (
        log_values.astype(jnp.float32)
        + 0.5 * jnp.sum(jnp.log(inv_f), axis=1)
        - 0.5 * jnp.sum(inv_f * mean_f * mean_f, axis=1)
        - 0.5 * feature_count * math.log(2.0 * math.pi)
    )


def square_of(x):
    x_f = x.astype(jnp.float32)
    return (x_f * x_f).astype(jnp.bfloat16)


def density_body(shards, held, pos_ref, nat_ref, x_ref, const_ref, *rest):
    weight_refs = rest[:shards]
    resp_ref, norm_ref, count_ref, weights, sems = rest[shards:]
    step = pl.program_id(0)

    @pl.when(step == 0)
    def _():
        copies = [
            pltpu.make_async_copy(weight_refs[j], weights.at[j], sems.at[j]) for j in range(shards)
        ]
        for copy in copies:
            copy.start()
        for copy in copies:
            copy.wait()

    x = x_ref[...]
    half = (square_of(x).astype(jnp.float32) * -0.5).astype(jnp.bfloat16)
    densities = []
    for slot in range(CANDS):
        pos = pos_ref[step, slot]
        shard, block = lax.div(pos, held), lax.rem(pos, held)
        linear = lax.dot_general(
            weights[shard, 0, block], x, NT, preferred_element_type=jnp.float32
        )
        quadratic = lax.dot_general(
            weights[shard, 1, block], half, NT, preferred_element_type=jnp.float32
        )
        densities.append(linear + quadratic + const_ref[nat_ref[step, slot]])
    peak = functools.reduce(jnp.maximum, [jnp.max(d, axis=0, keepdims=True) for d in densities])
    terms = [jnp.exp(d - peak) for d in densities]
    total = functools.reduce(jnp.add, [jnp.sum(t, axis=0, keepdims=True) for t in terms])
    norm_ref[0] = peak + jnp.log(total)
    inverse_total = 1.0 / total
    ones = jnp.ones((8, RB), jnp.bfloat16)
    for slot in range(CANDS):
        resp = (terms[slot] * inverse_total).astype(jnp.bfloat16)
        resp_ref[0, slot] = resp
        counts = lax.dot_general(ones, resp, NT, preferred_element_type=jnp.float32)
        count_ref[0, slot : slot + 1] = counts[0:1]


def responsibilities(rows, pos, nat, consts, weights):
    count = rows.shape[0] // RB
    feature_count = rows.shape[1]
    shards, held = len(weights), weights[0].shape[1]
    pairs = count * CANDS
    grid_spec = pltpu.PrefetchScalarGridSpec(
        num_scalar_prefetch=2,
        grid=(count,),
        in_specs=[
            pl.BlockSpec((RB, feature_count), lambda i, *_: (i, 0)),
            pl.BlockSpec(consts.shape, lambda i, *_: (0, 0, 0)),
        ]
        + [pl.BlockSpec(memory_space=pl.ANY)] * shards,
        out_specs=[
            pl.BlockSpec((1, CANDS, CB, RB), lambda i, *_: (i, 0, 0, 0)),
            pl.BlockSpec((1, 1, RB), lambda i, *_: (i, 0, 0)),
            pl.BlockSpec((1, CANDS, CB), lambda i, *_: (i, 0, 0)),
        ],
        scratch_shapes=[
            pltpu.VMEM((shards,) + weights[0].shape, jnp.bfloat16),
            pltpu.SemaphoreType.DMA((shards,)),
        ],
    )
    return pl.pallas_call(
        functools.partial(density_body, shards, held),
        grid_spec=grid_spec,
        out_shape=[
            jax.ShapeDtypeStruct((count, CANDS, CB, RB), jnp.bfloat16),
            jax.ShapeDtypeStruct((count, 1, RB), jnp.float32),
            jax.ShapeDtypeStruct((count, CANDS, CB), jnp.float32),
        ],
        compiler_params=pltpu.CompilerParams(
            dimension_semantics=("arbitrary",), vmem_limit_bytes=VMEM_LIMIT
        ),
        cost_estimate=pl.CostEstimate(
            flops=pairs * 4 * CB * RB * feature_count,
            bytes_accessed=shards * weights[0].size * 2 + rows.size * 4,
            transcendentals=pairs * CB * RB,
        ),
        name="responsibilities",
    )(pos, nat, rows, consts, *weights)


def moment_body(first, shards, held, counts, pos_ref, *rest):
    parts = len(counts)
    row_refs, resp_refs = rest[:parts], rest[parts : 2 * parts]
    out_refs = rest[2 * parts : 2 * parts + shards]
    rows, resp, sums, sems = rest[2 * parts + shards :]
    copies = []
    start = 0
    for j in range(parts):
        here = pl.ds(start, counts[j])
        copies.append(
            (
                pltpu.make_async_copy(row_refs[j], rows.at[here], sems.at[0, j]),
                pltpu.make_async_copy(resp_refs[j], resp.at[here], sems.at[1, j]),
            )
        )
        start += counts[j]
    for pair in copies:
        for copy in pair:
            copy.start()
    sums[...] = jnp.zeros_like(sums)
    start = 0
    for j in range(parts):
        for copy in copies[j]:
            copy.wait()

        @pl.loop(start, start + counts[j])
        def _(i):
            for slot in range(CANDS):
                local = pos_ref[i, slot] - first * held

                @pl.when(jnp.logical_and(local >= 0, local < shards * held))
                def _():
                    x = rows[i]
                    weight = resp[i, slot]
                    sums[local, 0] += jnp.dot(weight, x, preferred_element_type=jnp.float32)
                    sums[local, 1] += jnp.dot(
                        weight, square_of(x), preferred_element_type=jnp.float32
                    )

        start += counts[j]
    for j in range(shards):
        for b in range(held):
            for m in range(2):
                out_refs[j][m, b] = sums[j * held + b, m].astype(jnp.bfloat16)


def moments(rows, resp, pos, held, first, shards):
    counts = tuple(r.shape[0] for r in rows)
    feature_count = rows[0].shape[2]
    total = sum(counts)
    any_spec = pl.BlockSpec(memory_space=pl.ANY)
    pairs = total * shards * held // 8
    return pl.pallas_call(
        functools.partial(moment_body, first, shards, held, counts),
        in_specs=[pl.BlockSpec(memory_space=pltpu.SMEM)] + [any_spec] * (2 * len(counts)),
        out_specs=[pl.BlockSpec(memory_space=pltpu.VMEM)] * shards,
        out_shape=[jax.ShapeDtypeStruct((2, held, CB, feature_count), jnp.bfloat16)] * shards,
        scratch_shapes=[
            pltpu.VMEM((total, RB, feature_count), jnp.bfloat16),
            pltpu.VMEM((total, CANDS, CB, RB), jnp.bfloat16),
            pltpu.VMEM((shards * held, 2, CB, feature_count), jnp.float32),
            pltpu.SemaphoreType.DMA((2, len(counts))),
        ],
        compiler_params=pltpu.CompilerParams(vmem_limit_bytes=VMEM_LIMIT),
        cost_estimate=pl.CostEstimate(
            flops=pairs * 4 * CB * RB * feature_count,
            bytes_accessed=total * RB * (feature_count + CANDS * CB) * 2,
            transcendentals=0,
        ),
        name="moments",
    )(pos, *rows, *resp)


def in_blocks(rows):
    return rows.reshape(rows.shape[0] // RB, RB, rows.shape[1])


def summed_counts(counts, ids, group_blocks):
    spread = (jnp.arange(group_blocks, dtype=jnp.int32)[:, None] == ids.reshape(1, -1)).astype(
        jnp.float32
    )
    return jnp.dot(spread, counts.reshape(-1, CB), precision=lax.Precision.HIGHEST)


def plain_plan(points, ids, weights, consts):
    dp_size = lax.axis_size("dp")
    held, feature_count = weights.shape[1], weights.shape[3]
    group_blocks = dp_size * held
    all_weights = lax.all_gather(weights, "dp", axis=0)
    all_consts = lax.all_gather(consts, "dp", axis=0, tiled=True)
    const_columns = all_consts.reshape(group_blocks, CB, 1)
    resp, norm, counts = responsibilities(
        points, ids, ids, const_columns, [all_weights[j] for j in range(dp_size)]
    )
    sums = []
    for j in range(dp_size):
        sums += moments([in_blocks(points)], [resp], ids, held, j, 1)
    total = lax.psum_scatter(jnp.stack(sums), "dp", scatter_dimension=0).astype(jnp.float32)
    count_sum = lax.psum_scatter(
        summed_counts(counts, ids, group_blocks), "dp", scatter_dimension=0, tiled=True
    )
    total = total.reshape(2, held * CB, feature_count)
    return count_sum.reshape(-1), total[0], total[1], norm.reshape(-1)


def line_pairs(links):
    return [(2 * a + c, 2 * b + c) for a, b in links for c in (0, 1)]


INWARD = line_pairs(((0, 1), (3, 2)))
OUTWARD = line_pairs(((1, 0), (2, 3)))
MIDDLE = line_pairs(((1, 2), (2, 1)))
CORES = [(2, 3), (3, 2), (4, 5), (5, 4)]


def move(value, pairs):
    return lax.ppermute(value, "dp", pairs)


def after(value, *others):
    return lax.optimization_barrier((value,) + others)[0]


def line_plan(points, ids, weights, consts):
    held, feature_count = weights.shape[1], weights.shape[3]
    group_blocks = 8 * held
    index = lax.axis_index("dp")
    chip, core = index // 2, index % 2
    row_blocks = points.shape[0] // RB
    late_blocks = row_blocks // 4
    cut = (row_blocks - late_blocks) * RB

    outer = move(weights, INWARD)
    across = move(weights, MIDDLE)
    early_rows = move(after(points[:cut], outer), INWARD)
    far = move(outer, MIDDLE)
    late_rows = move(after(points[cut:], early_rows), INWARD)
    shared = [move(w, CORES) for w in (weights, outer, across, far)]
    near = [weights, outer, across, far]
    shards = [w for pair in zip(near, shared) for w in pair]

    small = jnp.concatenate([consts, ids.reshape(-1).astype(jnp.float32)])
    all_small = lax.all_gather(small, "dp", axis=0)
    const_columns = all_small[:, : consts.shape[0]].reshape(group_blocks, CB, 1)
    all_ids = all_small[:, consts.shape[0] :].astype(jnp.int32)
    end_chip = jnp.where(chip < 2, 0, 3)
    end_ids = lax.dynamic_index_in_dim(all_ids, 2 * end_chip + core, 0, keepdims=False)
    end_ids = end_ids.reshape(row_blocks, CANDS)

    def place(nat):
        holder = nat // held
        z = jnp.where(chip < 2, holder // 2, 3 - holder // 2)
        z = jnp.where(z == 0, 1, jnp.where(z == 1, 0, z))
        other = (holder % 2 + core) % 2
        return (z * 2 + other) * held + nat % held

    early_ids, late_ids = end_ids[: row_blocks - late_blocks], end_ids[row_blocks - late_blocks :]
    runs = [(points, ids), (early_rows, early_ids), (late_rows, late_ids)]
    results = [responsibilities(r, place(i), i, const_columns, shards) for r, i in runs]
    rows = [in_blocks(r) for r, _ in runs]
    resp = [r[0] for r in results]
    all_nat = jnp.concatenate([i for _, i in runs])
    all_pos = place(all_nat)

    def both_cores(place_of):
        other = moments(rows, resp, all_pos, held, 2 * place_of + 1, 1)[0]
        received = move(other, CORES)
        own = moments(rows, resp, all_pos, held, 2 * place_of, 1)[0]
        return own.astype(jnp.float32) + received.astype(jnp.float32)

    far_sum = move(both_cores(3).astype(jnp.bfloat16), MIDDLE)
    across_sum = move(both_cores(2).astype(jnp.bfloat16), MIDDLE)
    outer_sum = (both_cores(1) + far_sum.astype(jnp.float32)).astype(jnp.bfloat16)
    end_sum = move(outer_sum, OUTWARD)
    own_sum = both_cores(0) + across_sum.astype(jnp.float32)
    is_end = jnp.logical_or(chip == 0, chip == 3)
    total = jnp.where(is_end, end_sum.astype(jnp.float32), own_sum)
    total = total.reshape(2, held * CB, feature_count)

    counts = jnp.concatenate([r[2] for r in results])
    counts = jnp.where(is_end, 0.0, summed_counts(counts, all_nat, group_blocks))
    counts = lax.psum(counts, "dp")
    counts = lax.dynamic_slice_in_dim(counts, index * held, held, 0)

    end_norm = jnp.concatenate([results[1][1], results[2][1]]).reshape(-1)
    norm = jnp.where(is_end, move(end_norm, OUTWARD), results[0][1].reshape(-1))
    return counts.reshape(-1), total[0], total[1], norm


def on_device(points, candidates, means, inv_var, log_weight):
    feature_count = points.shape[1]
    owner_count = lax.axis_size("comp")
    held = means.shape[0] // CB
    scaled = (inv_var.astype(jnp.float32) * means.astype(jnp.float32)).astype(jnp.bfloat16)
    weights = jnp.stack([scaled, inv_var]).reshape(2, held, CB, feature_count)
    consts = component_consts(means, inv_var, log_weight)
    ids = candidates // (owner_count * held) * held + candidates % held
    plan = line_plan if lax.axis_size("dp") == 8 else plain_plan
    counts, first, second, norm = plan(points, ids, weights, consts)
    return counts, first, second, norm / feature_count


def solution(mesh):
    return jax.shard_map(
        on_device,
        mesh=mesh,
        in_specs=(
            P(("dp", "comp"), None),
            P(("dp", "comp"), None),
            P(("dp", "comp"), None),
            P(("dp", "comp"), None),
            P(("dp", "comp")),
        ),
        out_specs=(
            P(("dp", "comp")),
            P(("dp", "comp"), None),
            P(("dp", "comp"), None),
            P(("dp", "comp")),
        ),
        check_vma=False,
    )
```

```python
import functools
import math

import jax
import jax.numpy as jnp
from jax import lax
from jax.experimental import pallas as pl
from jax.experimental.pallas import tpu as pltpu
from jax.sharding import PartitionSpec as P

CB = 128
RB = 128
CANDS = 4
META = 16
VMEM_LIMIT = 12 * 1024 * 1024
NT = (((1,), (1,)), ((), ()))
TN = (((0,), (0,)), ((), ()))


def square_of(x):
    x_f = x.astype(jnp.float32)
    return (x_f * x_f).astype(jnp.bfloat16)


def in_vmem(value):
    return pltpu.with_memory_space_constraint(value, pltpu.VMEM)


def shard_body(means_ref, inv_ref, log_ref, out_ref):
    owned, feature_count = means_ref.shape
    ones = jnp.ones((META, feature_count), jnp.float32)
    row = lax.broadcasted_iota(jnp.int32, (META, CB), 0)
    out_ref[2 * owned : 2 * owned + META, :] = jnp.zeros((META, feature_count), jnp.bfloat16)
    for block in range(owned // CB):
        here = slice(block * CB, (block + 1) * CB)
        inverse = inv_ref[here, :]
        mean_f = means_ref[here, :].astype(jnp.float32)
        inv_f = inverse.astype(jnp.float32)
        scaled = inv_f * mean_f
        out_ref[here, :] = scaled.astype(jnp.bfloat16)
        out_ref[owned + block * CB : owned + (block + 1) * CB, :] = inverse
        terms = 0.5 * jnp.log(inv_f) - 0.5 * (scaled * mean_f)
        rest = lax.dot_general(
            ones, terms, NT, precision=lax.Precision.HIGHEST, preferred_element_type=jnp.float32
        )
        rest += log_ref[:, here].astype(jnp.float32)
        rest -= 0.5 * feature_count * math.log(2.0 * math.pi)
        high = rest.astype(jnp.bfloat16).astype(jnp.float32)
        rest -= high
        middle = rest.astype(jnp.bfloat16).astype(jnp.float32)
        low = rest - middle
        pieces = jnp.where(row == 0, high, jnp.where(row == 1, middle, low))
        out_ref[2 * owned : 2 * owned + META, here] = pieces.astype(jnp.bfloat16)


def parameter_shard(means, inv_var, log_weight):
    owned, feature_count = means.shape
    vmem = pl.BlockSpec(memory_space=pltpu.VMEM)
    return pl.pallas_call(
        shard_body,
        in_specs=[vmem, vmem, vmem],
        out_specs=vmem,
        out_shape=pltpu.VMEM((2 * owned + META, feature_count), jnp.bfloat16),
        compiler_params=pltpu.CompilerParams(vmem_limit_bytes=VMEM_LIMIT),
        cost_estimate=pl.CostEstimate(
            flops=owned * feature_count * 40,
            bytes_accessed=owned * feature_count * 8,
            transcendentals=owned * feature_count,
        ),
        name="parameter_shard",
    )(in_vmem(means), in_vmem(inv_var), log_weight.reshape(1, owned))


def density_body(count, held, pos_ref, x_ref, weight_ref, resp_ref, norm_ref):
    owned = held * CB
    row_index = lax.broadcasted_iota(jnp.int32, (META, RB), 0)
    pieces = jnp.where(row_index < 3, 1.0, 0.0).astype(jnp.bfloat16)

    @pl.loop(0, count)
    def _(i):
        x = x_ref[pl.ds(pl.multiple_of(i * RB, RB), RB), :]
        half = (square_of(x).astype(jnp.float32) * -0.5).astype(jnp.bfloat16)
        densities = []
        for slot in range(CANDS):
            pos = pos_ref[i, slot]
            shard, start = lax.div(pos, held), lax.rem(pos, held) * CB
            start = pl.multiple_of(start, CB)
            linear = lax.dot_general(
                weight_ref[shard, pl.ds(start, CB), :], x, NT, preferred_element_type=jnp.float32
            )
            quadratic = lax.dot_general(
                weight_ref[shard, pl.ds(owned + start, CB), :],
                half,
                NT,
                preferred_element_type=jnp.float32,
            )
            constant = lax.dot_general(
                weight_ref[shard, 2 * owned : 2 * owned + META, pl.ds(start, CB)],
                pieces,
                TN,
                preferred_element_type=jnp.float32,
            )
            densities.append(linear + quadratic + constant)
        peak = functools.reduce(
            jnp.maximum, [jnp.max(d, axis=0, keepdims=True) for d in densities]
        )
        terms = [jnp.exp(d - peak) for d in densities]
        total = functools.reduce(jnp.add, [jnp.sum(t, axis=0, keepdims=True) for t in terms])
        norm_ref[i] = peak + jnp.log(total)
        inverse_total = 1.0 / total
        for slot in range(CANDS):
            resp_ref[i, slot] = (terms[slot] * inverse_total).astype(jnp.bfloat16)


def responsibilities(rows, pos, weights, held):
    count = rows.shape[0] // RB
    feature_count = rows.shape[1]
    vmem = pl.BlockSpec(memory_space=pltpu.VMEM)
    pairs = count * CANDS
    return pl.pallas_call(
        functools.partial(density_body, count, held),
        in_specs=[pl.BlockSpec(memory_space=pltpu.SMEM), vmem, vmem],
        out_specs=[vmem, vmem],
        out_shape=[
            pltpu.VMEM((count, CANDS, CB, RB), jnp.bfloat16),
            pltpu.VMEM((count, 1, RB), jnp.float32),
        ],
        compiler_params=pltpu.CompilerParams(vmem_limit_bytes=VMEM_LIMIT),
        cost_estimate=pl.CostEstimate(
            flops=pairs * 4 * CB * RB * feature_count,
            bytes_accessed=pairs * CB * feature_count * 4 + rows.size * 2,
            transcendentals=pairs * CB * RB,
        ),
        name="responsibilities",
    )(pos, in_vmem(rows), in_vmem(weights))


def pair_lists(pos, runs, group_blocks):
    run_of = []
    for index, count in enumerate(runs):
        run_of += [index] * (count * CANDS)
    run_of = jnp.array(run_of, jnp.int32)
    key = pos.reshape(-1) * len(runs) + run_of
    number = jnp.arange(key.shape[0], dtype=jnp.int32)
    before = jnp.logical_or(
        key[None, :] < key[:, None],
        jnp.logical_and(key[None, :] == key[:, None], number[None, :] < number[:, None]),
    )
    rank = jnp.sum(before.astype(jnp.int32), axis=1)
    order = jnp.sum(jnp.where(rank[None, :] == number[:, None], number[None, :], 0), axis=1)
    bounds = jnp.arange(group_blocks * len(runs) + 1, dtype=jnp.int32)
    starts = jnp.sum((key[None, :] < bounds[:, None]).astype(jnp.int32), axis=1)
    return order, starts


def moment_body(shards, held, runs, order_ref, start_ref, *rest):
    parts, outs = len(runs), len(shards)
    row_refs, resp_refs = rest[:parts], rest[parts : 2 * parts]
    out_refs = rest[2 * parts : 2 * parts + outs]
    sums, count_sum = rest[2 * parts + outs :]
    owned = held * CB
    meta = slice(2 * owned, 2 * owned + META)
    ones = jnp.ones((META, 2 * RB), jnp.bfloat16)

    def block_sums(pos):
        sums[...] = jnp.zeros_like(sums)
        count_sum[...] = jnp.zeros_like(count_sum)
        base = 0
        for run in range(parts):
            entry = pos * parts + run
            low, high = start_ref[entry], start_ref[entry + 1]

            @pl.loop(0, lax.div(high - low + 1, 2))
            def _(step, base=base, run=run, low=low, high=high):
                one = low + 2 * step
                two = jnp.minimum(one + 1, high - 1)
                valid = (one + 1 < high).astype(jnp.float32)
                pair_a, pair_b = order_ref[one] - base, order_ref[two] - base
                row_a, row_b = lax.div(pair_a, CANDS), lax.div(pair_b, CANDS)
                weight_a = resp_refs[run][row_a, lax.rem(pair_a, CANDS)]
                weight_b = resp_refs[run][row_b, lax.rem(pair_b, CANDS)]
                weight_b = (weight_b.astype(jnp.float32) * valid).astype(jnp.bfloat16)
                weight = jnp.concatenate([weight_a, weight_b], axis=1)
                x = jnp.concatenate(
                    [
                        row_refs[run][pl.ds(pl.multiple_of(row_a * RB, RB), RB), :],
                        row_refs[run][pl.ds(pl.multiple_of(row_b * RB, RB), RB), :],
                    ],
                    axis=0,
                )
                sums[0] += jnp.dot(weight, x, preferred_element_type=jnp.float32)
                sums[1] += jnp.dot(weight, square_of(x), preferred_element_type=jnp.float32)
                count_sum[...] += lax.dot_general(
                    ones, weight, NT, preferred_element_type=jnp.float32
                )

            base += runs[run] * CANDS

    for shard, out_ref in zip(shards, out_refs):
        out_ref[meta, :] = jnp.zeros((META, out_ref.shape[1]), jnp.bfloat16)

        @pl.loop(0, held)
        def _(block, shard=shard, out_ref=out_ref):
            block_sums(shard * held + block)
            start = pl.multiple_of(block * CB, CB)
            out_ref[pl.ds(start, CB), :] = sums[0].astype(jnp.bfloat16)
            out_ref[pl.ds(owned + start, CB), :] = sums[1].astype(jnp.bfloat16)
            out_ref[meta, pl.ds(start, CB)] = count_sum[...].astype(jnp.bfloat16)


def moments(rows, resp, order, starts, held, shards):
    runs = tuple(r.shape[0] // RB for r in rows)
    feature_count = rows[0].shape[1]
    smem = pl.BlockSpec(memory_space=pltpu.SMEM)
    vmem = pl.BlockSpec(memory_space=pltpu.VMEM)
    pairs = sum(runs) * held * len(shards) // 8
    out_shape = pltpu.VMEM((2 * held * CB + META, feature_count), jnp.bfloat16)
    return pl.pallas_call(
        functools.partial(moment_body, tuple(shards), held, runs),
        in_specs=[smem, smem] + [vmem] * (2 * len(runs)),
        out_specs=[vmem] * len(shards),
        out_shape=[out_shape] * len(shards),
        scratch_shapes=[
            pltpu.VMEM((2, CB, feature_count), jnp.float32),
            pltpu.VMEM((META, CB), jnp.float32),
        ],
        compiler_params=pltpu.CompilerParams(vmem_limit_bytes=VMEM_LIMIT),
        cost_estimate=pl.CostEstimate(
            flops=pairs * 4 * CB * RB * feature_count,
            bytes_accessed=pairs * RB * (feature_count + CB) * 2,
            transcendentals=0,
        ),
        name="moments",
    )(order, starts, *[in_vmem(r) for r in rows], *[in_vmem(r) for r in resp])


def plain_plan(points, ids, weights, held):
    dp_size = lax.axis_size("dp")
    all_weights = lax.all_gather(weights, "dp", axis=0)
    resp, norm = responsibilities(points, ids, all_weights, held)
    order, starts = pair_lists(ids, (points.shape[0] // RB,), dp_size * held)
    sums = []
    for j in range(dp_size):
        sums += moments([points], [resp], order, starts, held, [j])
    total = lax.psum_scatter(jnp.concatenate(sums), "dp", scatter_dimension=0, tiled=True)
    return (lambda a, b: total[a, b].astype(jnp.float32)), norm.reshape(-1)


def line_pairs(links):
    return [(2 * a + c, 2 * b + c) for a, b in links for c in (0, 1)]


INWARD = line_pairs(((0, 1), (3, 2)))
OUTWARD = line_pairs(((1, 0), (2, 3)))
MIDDLE = line_pairs(((1, 2), (2, 1)))
CORES = [(2, 3), (3, 2), (4, 5), (5, 4)]


def move(value, pairs):
    return lax.ppermute(value, "dp", pairs)


def after(value, *others):
    return lax.optimization_barrier((value,) + others)[0]


def line_plan(points, ids, weights, held):
    group_blocks = 8 * held
    index = lax.axis_index("dp")
    chip, core = index // 2, index % 2
    row_blocks = points.shape[0] // RB
    cuts = (0, row_blocks // 2, row_blocks - row_blocks // 8, row_blocks)
    pieces = [points[a * RB : b * RB] for a, b in zip(cuts[:-1], cuts[1:])]

    outer = move(weights, INWARD)
    weights_then, *pieces = lax.optimization_barrier((weights, *pieces))
    across = move(weights_then, MIDDLE)
    moved = [move(after(pieces[0], outer), INWARD)]
    far = move(outer, MIDDLE)
    moved.append(move(after(pieces[1], moved[0]), INWARD))
    moved.append(move(after(pieces[2], moved[0], far), INWARD))
    near = [weights_then, outer, across, far]
    shards = [w for pair in ((w, move(w, CORES)) for w in near) for w in pair]
    all_weights = jnp.stack(shards)

    def place(nat):
        holder = nat // held
        z = jnp.where(chip < 2, holder // 2, 3 - holder // 2)
        z = jnp.where(z == 0, 1, jnp.where(z == 1, 0, z))
        other = (holder % 2 + core) % 2
        return (z * 2 + other) * held + nat % held

    end_pos = place(move(ids, INWARD))
    own_pos = place(ids)
    rows = [points] + moved
    runs = (row_blocks,) + tuple(b - a for a, b in zip(cuts[:-1], cuts[1:]))
    order, starts = pair_lists(jnp.concatenate([own_pos, end_pos]), runs, group_blocks)
    run_pos = [own_pos] + [end_pos[a:b] for a, b in zip(cuts[:-1], cuts[1:])]
    results = []
    for run_rows, pos in zip(rows, run_pos):
        if results:
            pos = after(pos, results[-1][1])
        results.append(responsibilities(run_rows, pos, all_weights, held))
    resp = [r[0] for r in results]

    def both_cores(own, other):
        return own.astype(jnp.float32) + move(other, CORES).astype(jnp.float32)

    def sums_of(position, *earlier):
        return moments(rows, resp, after(order, *earlier), starts, held, [position])[0]

    far_other = sums_of(7)
    far_own = sums_of(6, far_other)
    far_part = both_cores(far_own, far_other).astype(jnp.bfloat16)
    far_sum = move(far_part, MIDDLE)
    across_other = sums_of(5, far_part)
    across_own = sums_of(4, across_other)
    across_part = both_cores(across_own, across_other).astype(jnp.bfloat16)
    across_sum = move(across_part, MIDDLE)
    outer_other = sums_of(3, across_part)
    own_other = sums_of(1, outer_other)
    outer_own = sums_of(2, own_other)
    own_own = sums_of(0, outer_own)
    outer_part = both_cores(outer_own, outer_other)
    own_part = both_cores(own_own, own_other)
    outer_sum = (outer_part + far_sum.astype(jnp.float32)).astype(jnp.bfloat16)
    end_sum = move(outer_sum, OUTWARD)
    is_end = jnp.logical_or(chip == 0, chip == 3)

    def total(rows_of, columns):
        own = own_part[rows_of, columns] + across_sum[rows_of, columns].astype(jnp.float32)
        return jnp.where(is_end, end_sum[rows_of, columns].astype(jnp.float32), own)

    end_norm = jnp.concatenate([r[1].reshape(-1) for r in results[1:]])
    norm = jnp.where(is_end, move(end_norm, OUTWARD), results[0][1].reshape(-1))
    return total, norm


def on_device(points, candidates, means, inv_var, log_weight):
    feature_count = points.shape[1]
    owner_count = lax.axis_size("comp")
    owned = means.shape[0]
    held = owned // CB
    ids = candidates // (owner_count * held) * held + candidates % held
    weights = parameter_shard(means, inv_var, log_weight)
    plan = line_plan if lax.axis_size("dp") == 8 else plain_plan
    total, norm = plan(points, ids, weights, held)
    every = slice(0, feature_count)
    counts = total(2 * owned, slice(0, owned))
    first, second = total(slice(0, owned), every), total(slice(owned, 2 * owned), every)
    return counts, first, second, norm / feature_count


def solution(mesh):
    return jax.shard_map(
        on_device,
        mesh=mesh,
        in_specs=(
            P(("dp", "comp"), None),
            P(("dp", "comp"), None),
            P(("dp", "comp"), None),
            P(("dp", "comp"), None),
            P(("dp", "comp")),
        ),
        out_specs=(
            P(("dp", "comp")),
            P(("dp", "comp"), None),
            P(("dp", "comp"), None),
            P(("dp", "comp")),
        ),
        check_vma=False,
    )
```

```python
import functools
import math

import jax
import jax.numpy as jnp
from jax import lax
from jax.experimental import pallas as pl
from jax.experimental.pallas import tpu as pltpu
from jax.sharding import PartitionSpec as P

CB = 128
RB = 128
CANDS = 4
META = 16
VMEM_LIMIT = 8 * 1024 * 1024
NT = (((1,), (1,)), ((), ()))
TN = (((0,), (0,)), ((), ()))


def in_vmem(value):
    return pltpu.with_memory_space_constraint(value, pltpu.VMEM)


def shard_body(cuts, means_ref, inv_ref, log_ref, points_ref, out_ref, *rest):
    piece_refs, sems = rest[:-1], rest[-1]
    copies = [
        pltpu.make_async_copy(points_ref.at[pl.ds(cuts[j], piece.shape[0])], piece, sems.at[j])
        for j, piece in enumerate(piece_refs)
    ]
    for copy in copies:
        copy.start()
    owned, feature_count = means_ref.shape
    ones = jnp.ones((META, feature_count), jnp.float32)
    row = lax.broadcasted_iota(jnp.int32, (META, CB), 0)
    for half in range(2):
        out_ref[0, half, owned:, :] = jnp.zeros((META, feature_count), jnp.bfloat16)
    for block in range(owned // CB):
        here = slice(block * CB, (block + 1) * CB)
        inverse = inv_ref[here, :]
        mean_f = means_ref[here, :].astype(jnp.float32)
        inv_f = inverse.astype(jnp.float32)
        scaled = inv_f * mean_f
        out_ref[0, 0, here, :] = scaled.astype(jnp.bfloat16)
        out_ref[0, 1, here, :] = inverse
        terms = 0.5 * jnp.log(inv_f) - 0.5 * (scaled * mean_f)
        rest = lax.dot_general(
            ones, terms, NT, precision=lax.Precision.HIGHEST, preferred_element_type=jnp.float32
        )
        rest += log_ref[:, here].astype(jnp.float32)
        rest -= 0.5 * feature_count * math.log(2.0 * math.pi)
        high = rest.astype(jnp.bfloat16).astype(jnp.float32)
        rest -= high
        middle = rest.astype(jnp.bfloat16).astype(jnp.float32)
        low = rest - middle
        pieces = jnp.where(row == 0, high, jnp.where(row == 1, middle, low))
        out_ref[0, 0, owned:, here] = pieces.astype(jnp.bfloat16)
    for copy in copies:
        copy.wait()


def parameter_shard(means, inv_var, log_weight, points, cuts):
    owned, feature_count = means.shape
    vmem = pl.BlockSpec(memory_space=pltpu.VMEM)
    anywhere = pl.BlockSpec(memory_space=pl.ANY)
    lengths = [b - a for a, b in zip(cuts[:-1], cuts[1:])]
    return pl.pallas_call(
        functools.partial(shard_body, cuts),
        in_specs=[vmem, vmem, vmem, anywhere],
        out_specs=[vmem] + [anywhere] * len(lengths),
        out_shape=[pltpu.VMEM((1, 2, owned + META, feature_count), jnp.bfloat16)]
        + [jax.ShapeDtypeStruct((length, feature_count), points.dtype) for length in lengths],
        scratch_shapes=[pltpu.SemaphoreType.DMA((max(len(lengths), 1),))],
        compiler_params=pltpu.CompilerParams(vmem_limit_bytes=VMEM_LIMIT),
        cost_estimate=pl.CostEstimate(
            flops=owned * feature_count * 40,
            bytes_accessed=owned * feature_count * 8,
            transcendentals=owned * feature_count,
        ),
        name="parameter_shard",
    )(in_vmem(means), in_vmem(inv_var), log_weight.reshape(1, owned), points)


def density_body(count, held, shards, arrays, pos_ref, x_ref, *rest):
    weight_refs = rest[:arrays]
    resp_ref, norm_ref, chosen, metas, sems, meta_sems = rest[arrays:]
    owned = held * CB
    per_array = shards // arrays
    row_index = lax.broadcasted_iota(jnp.int32, (META, RB), 0)
    pieces = jnp.where(row_index < 3, 1.0, 0.0).astype(jnp.bfloat16)

    def block_copy(array, entry, start, half, slot):
        return pltpu.make_async_copy(
            weight_refs[array].at[entry, :, pl.ds(start, CB), :],
            chosen.at[half, :, pl.ds(slot * CB, CB), :],
            sems.at[half, slot],
        )

    def fetch(i, half):
        for slot in range(CANDS):
            pos = pos_ref[i, slot]
            shard = lax.div(pos, held)
            start = pl.multiple_of(lax.rem(pos, held) * CB, CB)
            if arrays == 1:
                block_copy(0, shard, start, half, slot).start()
            for array in range(arrays if arrays > 1 else 0):

                @pl.when(shard == array)
                def _(array=array, start=start, slot=slot):
                    block_copy(array, 0, start, half, slot).start()

    fetch(0, 0)
    meta_copies = [
        pltpu.make_async_copy(
            weight_refs[shard // per_array].at[shard % per_array, 0, pl.ds(owned, META), :],
            metas.at[shard],
            meta_sems.at[shard],
        )
        for shard in range(shards)
    ]
    for copy in meta_copies:
        copy.start()
    for copy in meta_copies:
        copy.wait()

    @pl.loop(0, count)
    def _(i):
        half = lax.rem(i, 2)

        @pl.when(i + 1 < count)
        def _():
            fetch(i + 1, 1 - half)

        x = x_ref[pl.ds(pl.multiple_of(i * RB, RB), RB), :]
        constants = []
        for slot in range(CANDS):
            pos = pos_ref[i, slot]
            start = pl.multiple_of(lax.rem(pos, held) * CB, CB)
            constants.append(metas[lax.div(pos, held), :, pl.ds(start, CB)])
        densities = lax.dot_general(
            jnp.concatenate(constants, axis=1), pieces, TN, preferred_element_type=jnp.float32
        )
        for slot in range(CANDS):
            block_copy(0, 0, 0, half, slot).wait()
        densities += lax.dot_general(chosen[half, 0], x, NT, preferred_element_type=jnp.float32)
        densities += lax.dot_general(
            chosen[half, 1], x * x * -0.5, NT, preferred_element_type=jnp.float32
        )
        peak = jnp.max(densities, axis=0, keepdims=True)
        terms = jnp.exp(densities - peak)
        total = jnp.sum(terms, axis=0, keepdims=True)
        norm_ref[pl.ds(i, 1), :] = peak + jnp.log(total)
        resp = (terms * (1.0 / total)).astype(jnp.bfloat16)
        for slot in range(CANDS):
            resp_ref[i, slot] = resp[slot * CB : (slot + 1) * CB]


def responsibilities(rows, pos, weights, held):
    count = rows.shape[0] // RB
    feature_count = rows.shape[1]
    arrays = len(weights)
    shards = sum(w.shape[0] for w in weights)
    vmem = pl.BlockSpec(memory_space=pltpu.VMEM)
    pairs = count * CANDS
    return pl.pallas_call(
        functools.partial(density_body, count, held, shards, arrays),
        in_specs=[pl.BlockSpec(memory_space=pltpu.SMEM), vmem]
        + [pl.BlockSpec(memory_space=pl.ANY)] * arrays,
        out_specs=[vmem, vmem],
        out_shape=[
            pltpu.VMEM((count, CANDS, CB, RB), jnp.bfloat16),
            pltpu.VMEM((count, RB), jnp.float32),
        ],
        scratch_shapes=[
            pltpu.VMEM((2, 2, CANDS * CB, feature_count), jnp.bfloat16),
            pltpu.VMEM((shards, META, feature_count), jnp.bfloat16),
            pltpu.SemaphoreType.DMA((2, CANDS)),
            pltpu.SemaphoreType.DMA((shards,)),
        ],
        compiler_params=pltpu.CompilerParams(vmem_limit_bytes=VMEM_LIMIT),
        cost_estimate=pl.CostEstimate(
            flops=pairs * 4 * CB * RB * feature_count,
            bytes_accessed=pairs * CB * feature_count * 4 + rows.size * 2,
            transcendentals=pairs * CB * RB,
        ),
        name="responsibilities",
    )(pos, in_vmem(rows), *weights)


def pair_lists(pos, runs, group_blocks):
    run_of = []
    for index, count in enumerate(runs):
        run_of += [index] * (count * CANDS)
    run_of = jnp.array(run_of, jnp.int32)
    key = pos.reshape(-1) * len(runs) + run_of
    number = jnp.arange(key.shape[0], dtype=jnp.int32)
    before = jnp.logical_or(
        key[None, :] < key[:, None],
        jnp.logical_and(key[None, :] == key[:, None], number[None, :] < number[:, None]),
    )
    rank = jnp.sum(before.astype(jnp.int32), axis=1)
    order = jnp.sum(jnp.where(rank[None, :] == number[:, None], number[None, :], 0), axis=1)
    bounds = jnp.arange(group_blocks * len(runs) + 1, dtype=jnp.int32)
    starts = jnp.sum((key[None, :] < bounds[:, None]).astype(jnp.int32), axis=1)
    return order, starts


def moment_body(shards, held, runs, order_ref, start_ref, *rest):
    parts, outs = len(runs), len(shards)
    row_refs, resp_refs = rest[:parts], rest[parts : 2 * parts]
    out_refs = rest[2 * parts : 2 * parts + outs]
    sums, weight_sum = rest[2 * parts + outs :]
    owned = held * CB
    meta = slice(2 * owned, 2 * owned + META)
    feature_count = row_refs[0].shape[1]
    ones = jnp.ones((META, RB), jnp.float32)

    def block_sums(pos):
        sums[...] = jnp.zeros_like(sums)
        weight_sum[...] = jnp.zeros_like(weight_sum)
        base = 0
        for run in range(parts):
            entry = pos * parts + run
            low, high = start_ref[entry], start_ref[entry + 1]

            @pl.loop(0, lax.div(high - low + 1, 2))
            def _(step, base=base, run=run, low=low, high=high):
                one = low + 2 * step
                two = jnp.minimum(one + 1, high - 1)
                valid = jnp.full((CB, RB), (one + 1 < high).astype(jnp.float32))
                pair_a, pair_b = order_ref[one] - base, order_ref[two] - base
                row_a, row_b = lax.div(pair_a, CANDS), lax.div(pair_b, CANDS)
                weight_a = resp_refs[run][row_a, lax.rem(pair_a, CANDS)]
                weight_b = resp_refs[run][row_b, lax.rem(pair_b, CANDS)]
                weight_b = weight_b * valid.astype(jnp.bfloat16)
                weight = jnp.concatenate([weight_a, weight_b], axis=1)
                x = jnp.concatenate(
                    [
                        row_refs[run][pl.ds(pl.multiple_of(row_a * RB, RB), RB), :],
                        row_refs[run][pl.ds(pl.multiple_of(row_b * RB, RB), RB), :],
                    ],
                    axis=0,
                )
                sums[...] += jnp.dot(
                    weight,
                    jnp.concatenate([x, x * x], axis=1),
                    preferred_element_type=jnp.float32,
                )
                weight_sum[...] += weight_a.astype(jnp.float32) + weight_b.astype(jnp.float32)

            base += runs[run] * CANDS

    for shard, out_ref in zip(shards, out_refs):
        out_ref[meta, :] = jnp.zeros((META, out_ref.shape[1]), jnp.bfloat16)

        @pl.loop(0, held)
        def _(block, shard=shard, out_ref=out_ref):
            block_sums(shard * held + block)
            start = pl.multiple_of(block * CB, CB)
            out_ref[pl.ds(start, CB), :] = sums[:, :feature_count].astype(jnp.bfloat16)
            out_ref[pl.ds(owned + start, CB), :] = sums[:, feature_count:].astype(jnp.bfloat16)
            counts = lax.dot_general(
                ones,
                weight_sum[...],
                NT,
                precision=lax.Precision.HIGHEST,
                preferred_element_type=jnp.float32,
            )
            out_ref[meta, pl.ds(start, CB)] = counts.astype(jnp.bfloat16)


def moments(rows, resp, order, starts, held, shards):
    runs = tuple(r.shape[0] // RB for r in rows)
    feature_count = rows[0].shape[1]
    smem = pl.BlockSpec(memory_space=pltpu.SMEM)
    vmem = pl.BlockSpec(memory_space=pltpu.VMEM)
    pairs = sum(runs) * held * len(shards) // 8
    out_shape = pltpu.VMEM((2 * held * CB + META, feature_count), jnp.bfloat16)
    return pl.pallas_call(
        functools.partial(moment_body, tuple(shards), held, runs),
        in_specs=[smem, smem] + [vmem] * (2 * len(runs)),
        out_specs=[vmem] * len(shards),
        out_shape=[out_shape] * len(shards),
        scratch_shapes=[
            pltpu.VMEM((CB, 2 * feature_count), jnp.float32),
            pltpu.VMEM((CB, RB), jnp.float32),
        ],
        compiler_params=pltpu.CompilerParams(vmem_limit_bytes=VMEM_LIMIT),
        cost_estimate=pl.CostEstimate(
            flops=pairs * 4 * CB * RB * feature_count,
            bytes_accessed=pairs * RB * (feature_count + CB) * 2,
            transcendentals=0,
        ),
        name="moments",
    )(order, starts, *[in_vmem(r) for r in rows], *[in_vmem(r) for r in resp])


CHUNK = 80


def each_chunk(rows, step):
    whole = rows // CHUNK

    @pl.loop(0, whole)
    def _(i):
        step(pl.ds(pl.multiple_of(i * CHUNK, 16), CHUNK))

    if rows % CHUNK:
        step(slice(whole * CHUNK, rows))


def add_body(*refs):
    def step(here):
        terms = [ref[here, :].astype(jnp.float32) for ref in refs[:-1]]
        refs[-1][here, :] = functools.reduce(jnp.add, terms).astype(jnp.bfloat16)

    each_chunk(refs[-1].shape[0], step)


def join_body(*refs):
    start = 0
    for ref in refs[:-1]:
        refs[-1][start : start + ref.shape[0], :] = ref[...]
        start += ref.shape[0]


def small_step(body, shape, dtype, name, *operands):
    vmem = pl.BlockSpec(memory_space=pltpu.VMEM)
    return pl.pallas_call(
        body,
        in_specs=[vmem] * len(operands),
        out_specs=vmem,
        out_shape=pltpu.VMEM(shape, dtype),
        compiler_params=pltpu.CompilerParams(vmem_limit_bytes=VMEM_LIMIT),
        cost_estimate=pl.CostEstimate(
            flops=math.prod(shape), bytes_accessed=2 * math.prod(shape), transcendentals=0
        ),
        name=name,
    )(*[in_vmem(value) for value in operands])


def added(*terms):
    return small_step(add_body, terms[0].shape, jnp.bfloat16, "add_sums", *terms)


def joined(*norms):
    shape = (sum(n.shape[0] for n in norms), RB)
    return small_step(join_body, shape, jnp.float32, "join_norms", *norms)


def result_body(owned, end_ref, *refs):
    own_norm, end_norm, end_sum = refs[:3]
    terms, (count_ref, first_ref, second_ref, loglik_ref) = refs[3:-4], refs[-4:]
    is_end = end_ref[0] > 0
    block = pl.program_id(0)
    feature_count = first_ref.shape[1]

    def total(rows):
        inner = functools.reduce(jnp.add, [t[rows, :].astype(jnp.float32) for t in terms])
        return jnp.where(is_end, end_sum[rows, :].astype(jnp.float32), inner)

    start = pl.multiple_of(block * CB, CB)
    first_ref[...] = total(pl.ds(start, CB))
    second_ref[...] = total(pl.ds(owned + start, CB))
    count_ref[...] = total(slice(2 * owned, 2 * owned + META))[0:1, :owned]
    norm = jnp.where(is_end, end_norm[...], own_norm[...])
    loglik_ref[...] = norm * (1.0 / feature_count)


def results_of(is_end, own_norm, end_norm, end_sum, *terms):
    rows, feature_count = end_sum.shape
    owned = (rows - META) // 2
    vmem = pl.BlockSpec(memory_space=pltpu.VMEM)
    operands = (own_norm, end_norm, end_sum) + terms
    return pl.pallas_call(
        functools.partial(result_body, owned),
        grid=(owned // CB,),
        in_specs=[pl.BlockSpec(memory_space=pltpu.SMEM)] + [vmem] * len(operands),
        out_specs=[
            pl.BlockSpec((1, owned), lambda i: (0, 0)),
            pl.BlockSpec((CB, feature_count), lambda i: (i, 0)),
            pl.BlockSpec((CB, feature_count), lambda i: (i, 0)),
            pl.BlockSpec(own_norm.shape, lambda i: (0, 0)),
        ],
        out_shape=[
            jax.ShapeDtypeStruct((1, owned), jnp.float32),
            jax.ShapeDtypeStruct((owned, feature_count), jnp.float32),
            jax.ShapeDtypeStruct((owned, feature_count), jnp.float32),
            jax.ShapeDtypeStruct(own_norm.shape, jnp.float32),
        ],
        compiler_params=pltpu.CompilerParams(vmem_limit_bytes=VMEM_LIMIT),
        name="results",
    )(is_end.astype(jnp.int32).reshape(1), *[in_vmem(value) for value in operands])


def plain_plan(points, ids, parameters, held):
    weights = parameter_shard(*parameters, points, (0,))[0]
    dp_size = lax.axis_size("dp")
    all_weights = lax.all_gather(weights, "dp", axis=0, tiled=True)
    resp, norm = responsibilities(points, ids, [all_weights], held)
    order, starts = pair_lists(ids, (points.shape[0] // RB,), dp_size * held)
    sums = []
    for j in range(dp_size):
        sums += moments([points], [resp], order, starts, held, [j])
    total = lax.psum_scatter(jnp.concatenate(sums), "dp", scatter_dimension=0, tiled=True)
    total = total.astype(jnp.float32)
    owned = held * CB
    counts, first, second = total[2 * owned, :owned], total[:owned], total[owned : 2 * owned]
    return counts, first, second, norm.reshape(-1) / points.shape[1]


def line_pairs(links):
    return [(2 * a + c, 2 * b + c) for a, b in links for c in (0, 1)]


INWARD = line_pairs(((0, 1), (3, 2)))
OUTWARD = line_pairs(((1, 0), (2, 3)))
MIDDLE = line_pairs(((1, 2), (2, 1)))
CORES = [(2, 3), (3, 2), (4, 5), (5, 4)]


def move(value, pairs):
    return lax.ppermute(value, "dp", pairs)


def after(value, *others):
    return lax.optimization_barrier((value,) + others)[0]


def line_plan(points, ids, parameters, held):
    group_blocks = 8 * held
    index = lax.axis_index("dp")
    chip, core = index // 2, index % 2
    row_blocks = points.shape[0] // RB
    cuts = (0, row_blocks // 2, row_blocks - row_blocks // 8, row_blocks)
    weights, *pieces = parameter_shard(*parameters, points, [cut * RB for cut in cuts])

    outer = move(weights, INWARD)
    across = move(weights, MIDDLE)
    own_shared = move(weights, CORES)
    moved = [move(after(pieces[0], outer), INWARD)]
    far = move(outer, MIDDLE)
    outer_shared = move(outer, CORES)
    across_shared = move(across, CORES)
    moved.append(move(after(pieces[1], moved[0]), INWARD))
    moved.append(move(after(pieces[2], moved[0], far), INWARD))
    far_shared = move(far, CORES)
    shards = [weights, own_shared, outer, outer_shared, across, across_shared, far, far_shared]

    def place(nat):
        holder = nat // held
        z = jnp.where(chip < 2, holder // 2, 3 - holder // 2)
        z = jnp.where(z == 0, 1, jnp.where(z == 1, 0, z))
        other = (holder % 2 + core) % 2
        return (z * 2 + other) * held + nat % held

    end_pos = place(after(move(ids, INWARD), moved[0]))
    own_pos = place(ids)
    rows = [points] + moved
    runs = (row_blocks,) + tuple(b - a for a, b in zip(cuts[:-1], cuts[1:]))
    order, starts = pair_lists(jnp.concatenate([own_pos, end_pos]), runs, group_blocks)
    run_pos = [own_pos] + [end_pos[a:b] for a, b in zip(cuts[:-1], cuts[1:])]
    results = []
    for run_rows, pos in zip(rows, run_pos):
        if results:
            pos = after(pos, results[-1][1])
        results.append(responsibilities(run_rows, pos, shards, held))
    resp = [r[0] for r in results]

    def sums_of(position, *earlier):
        return moments(rows, resp, after(order, *earlier), starts, held, [position])[0]

    end_norm = move(joined(*[r[1] for r in results[1:]]), OUTWARD)
    far_other = sums_of(7)
    far_received = move(far_other, CORES)
    far_own = sums_of(6, far_other)
    far_part = added(far_own, far_received)
    far_sum = move(far_part, MIDDLE)
    across_other = sums_of(5, far_part, end_norm)
    across_received = move(across_other, CORES)
    across_own = sums_of(4, across_other)
    across_part = added(across_own, across_received)
    across_sum = move(across_part, MIDDLE)
    outer_other = sums_of(3, across_part)
    outer_received = move(outer_other, CORES)
    own_other = sums_of(1, outer_other)
    own_received = move(own_other, CORES)
    outer_own = sums_of(2, own_other)
    own_own = sums_of(0, outer_own)
    outer_sum = added(outer_own, outer_received, far_sum)
    end_sum = move(outer_sum, OUTWARD)
    is_end = jnp.logical_or(chip == 0, chip == 3)
    counts, first, second, loglik = results_of(
        is_end, results[0][1], end_norm, end_sum, own_own, own_received, across_sum
    )
    return counts.reshape(-1), first, second, loglik.reshape(-1)


def on_device(points, candidates, means, inv_var, log_weight):
    feature_count = points.shape[1]
    owner_count = lax.axis_size("comp")
    owned = means.shape[0]
    held = owned // CB
    ids = candidates // (owner_count * held) * held + candidates % held
    plan = line_plan if lax.axis_size("dp") == 8 else plain_plan
    return plan(points, ids, (means, inv_var, log_weight), held)


def solution(mesh):
    return jax.shard_map(
        on_device,
        mesh=mesh,
        in_specs=(
            P(("dp", "comp"), None),
            P(("dp", "comp"), None),
            P(("dp", "comp"), None),
            P(("dp", "comp"), None),
            P(("dp", "comp")),
        ),
        out_specs=(
            P(("dp", "comp")),
            P(("dp", "comp"), None),
            P(("dp", "comp"), None),
            P(("dp", "comp")),
        ),
        check_vma=False,
    )
```

```python
import functools
import math

import jax
import jax.numpy as jnp
from jax import lax
from jax.experimental import pallas as pl
from jax.experimental.pallas import tpu as pltpu
from jax.sharding import PartitionSpec as P

CB = 128
RB = 128
CANDS = 4
META = 16
VMEM_LIMIT = 8 * 1024 * 1024
NT = (((1,), (1,)), ((), ()))
TN = (((0,), (0,)), ((), ()))


def in_vmem(value):
    return pltpu.with_memory_space_constraint(value, pltpu.VMEM)


def in_hbm(value):
    return pltpu.with_memory_space_constraint(value, pltpu.HBM)


def shard_body(cuts, means_hbm, inv_hbm, log_ref, points_ref, out_ref, *rest):
    piece_refs, (means_ref, inv_ref, own_sems, sems) = rest[:-4], rest[-4:]
    own_copies = [
        pltpu.make_async_copy(means_hbm, means_ref, own_sems.at[0]),
        pltpu.make_async_copy(inv_hbm, inv_ref, own_sems.at[1]),
    ]
    for copy in own_copies:
        copy.start()
    copies = [
        pltpu.make_async_copy(points_ref.at[pl.ds(cuts[j], piece.shape[0])], piece, sems.at[j])
        for j, piece in enumerate(piece_refs)
    ]
    for copy in copies:
        copy.start()
    owned, feature_count = means_ref.shape
    ones = jnp.ones((META, feature_count), jnp.float32)
    row = lax.broadcasted_iota(jnp.int32, (META, CB), 0)
    for copy in own_copies:
        copy.wait()
    for half in range(2):
        out_ref[0, half, owned:, :] = jnp.zeros((META, feature_count), jnp.bfloat16)
    for block in range(owned // CB):
        here = slice(block * CB, (block + 1) * CB)
        inverse = inv_ref[here, :]
        mean_f = means_ref[here, :].astype(jnp.float32)
        inv_f = inverse.astype(jnp.float32)
        scaled = inv_f * mean_f
        out_ref[0, 0, here, :] = scaled.astype(jnp.bfloat16)
        out_ref[0, 1, here, :] = inverse
        terms = 0.5 * jnp.log(inv_f) - 0.5 * (scaled * mean_f)
        rest = lax.dot_general(
            ones, terms, NT, precision=lax.Precision.HIGHEST, preferred_element_type=jnp.float32
        )
        rest += log_ref[:, here].astype(jnp.float32)
        rest -= 0.5 * feature_count * math.log(2.0 * math.pi)
        high = rest.astype(jnp.bfloat16).astype(jnp.float32)
        rest -= high
        middle = rest.astype(jnp.bfloat16).astype(jnp.float32)
        low = rest - middle
        pieces = jnp.where(row == 0, high, jnp.where(row == 1, middle, low))
        out_ref[0, 0, owned:, here] = pieces.astype(jnp.bfloat16)
    for copy in copies:
        copy.wait()


def parameter_shard(means, inv_var, log_weight, points, cuts):
    owned, feature_count = means.shape
    vmem = pl.BlockSpec(memory_space=pltpu.VMEM)
    hbm = pl.BlockSpec(memory_space=pltpu.HBM)
    lengths = [b - a for a, b in zip(cuts[:-1], cuts[1:])]
    return pl.pallas_call(
        functools.partial(shard_body, cuts),
        in_specs=[hbm, hbm, vmem, hbm],
        out_specs=[vmem] + [hbm] * len(lengths),
        out_shape=[pltpu.VMEM((1, 2, owned + META, feature_count), jnp.bfloat16)]
        + [pltpu.HBM((length, feature_count), points.dtype) for length in lengths],
        scratch_shapes=[
            pltpu.VMEM((owned, feature_count), means.dtype),
            pltpu.VMEM((owned, feature_count), inv_var.dtype),
            pltpu.SemaphoreType.DMA((2,)),
            pltpu.SemaphoreType.DMA((max(len(lengths), 1),)),
        ],
        compiler_params=pltpu.CompilerParams(vmem_limit_bytes=VMEM_LIMIT),
        cost_estimate=pl.CostEstimate(
            flops=owned * feature_count * 40,
            bytes_accessed=owned * feature_count * 8,
            transcendentals=owned * feature_count,
        ),
        name="parameter_shard",
    )(in_hbm(means), in_hbm(inv_var), log_weight.reshape(1, owned), in_hbm(points))


def density_body(first, count, held, pos_ref, x_ref, weight_ref, resp_ref, norm_ref):
    owned = held * CB
    row_index = lax.broadcasted_iota(jnp.int32, (META, RB), 0)
    pieces = jnp.where(row_index < 3, 1.0, 0.0).astype(jnp.bfloat16)

    @pl.loop(0, count)
    def _(i):
        x = x_ref[pl.ds(pl.multiple_of(i * RB, RB), RB), :]
        half = x * x * -0.5
        densities = []
        for slot in range(CANDS):
            pos = pos_ref[(first + i) * CANDS + slot]
            shard, start = lax.div(pos, held), lax.rem(pos, held) * CB
            here = pl.ds(pl.multiple_of(start, CB), CB)
            linear = lax.dot_general(
                weight_ref[shard, 0, here, :], x, NT, preferred_element_type=jnp.float32
            )
            quadratic = lax.dot_general(
                weight_ref[shard, 1, here, :], half, NT, preferred_element_type=jnp.float32
            )
            constant = lax.dot_general(
                weight_ref[shard, 0, owned:, here],
                pieces,
                TN,
                preferred_element_type=jnp.float32,
            )
            densities.append(linear + quadratic + constant)
        peak = functools.reduce(
            jnp.maximum, [jnp.max(d, axis=0, keepdims=True) for d in densities]
        )
        terms = [jnp.exp(d - peak) for d in densities]
        total = functools.reduce(jnp.add, [jnp.sum(t, axis=0, keepdims=True) for t in terms])
        norm_ref[pl.ds(i, 1), :] = peak + jnp.log(total)
        inverse_total = 1.0 / total
        for slot in range(CANDS):
            resp_ref[i, slot] = (terms[slot] * inverse_total).astype(jnp.bfloat16)


def responsibilities(rows, pos, first, weights, held):
    count = rows.shape[0] // RB
    feature_count = rows.shape[1]
    vmem = pl.BlockSpec(memory_space=pltpu.VMEM)
    pairs = count * CANDS
    return pl.pallas_call(
        functools.partial(density_body, first, count, held),
        in_specs=[pl.BlockSpec(memory_space=pltpu.SMEM), vmem, vmem],
        out_specs=[vmem, vmem],
        out_shape=[
            pltpu.VMEM((count, CANDS, CB, RB), jnp.bfloat16),
            pltpu.VMEM((count, RB), jnp.float32),
        ],
        compiler_params=pltpu.CompilerParams(vmem_limit_bytes=VMEM_LIMIT),
        cost_estimate=pl.CostEstimate(
            flops=pairs * 4 * CB * RB * feature_count,
            bytes_accessed=pairs * CB * feature_count * 4 + rows.size * 2,
            transcendentals=pairs * CB * RB,
        ),
        name="responsibilities",
    )(pos, in_vmem(rows), in_vmem(weights))


def list_body(runs, held, owners, place, known, *rest):
    where = [ref[0] for ref in rest[:known]]
    id_refs, (pos_ref, order_ref, start_ref, cursor) = rest[known:-4], rest[-4:]
    bins = start_ref.shape[0]
    number_of_runs = len(runs)
    per_ref = sum(runs) // len(id_refs)
    firsts = [sum(runs[:j]) for j in range(number_of_runs)]

    def run_of(i):
        return sum((i >= start).astype(jnp.int32) for start in firsts[1:]) if firsts[1:] else 0

    @pl.loop(0, bins)
    def _(j):
        start_ref[j] = 0

    for part, id_ref in enumerate(id_refs):

        @pl.loop(0, per_ref)
        def _(row, part=part, id_ref=id_ref):
            i = part * per_ref + row
            for slot in range(CANDS):
                block = id_ref[slot, row]
                holder = place(lax.div(block, owners * held), *where)
                pos = holder * held + lax.rem(block, held)
                pos_ref[i * CANDS + slot] = pos
                key = pos * number_of_runs + run_of(i) + 1
                start_ref[key] = start_ref[key] + 1

    def prefix(j, total):
        total = total + start_ref[j]
        start_ref[j] = total
        cursor[j] = total
        return total

    lax.fori_loop(0, bins, prefix, jnp.int32(0))

    @pl.loop(0, sum(runs))
    def _(i):
        for slot in range(CANDS):
            key = pos_ref[i * CANDS + slot] * number_of_runs + run_of(i)
            order_ref[cursor[key]] = i * CANDS + slot
            cursor[key] = cursor[key] + 1


def pair_lists(candidates, runs, held, group_blocks, owners, place, where):
    smem = pl.BlockSpec(memory_space=pltpu.SMEM)
    pairs = sum(runs) * CANDS
    bins = group_blocks * len(runs) + 1
    return pl.pallas_call(
        functools.partial(list_body, tuple(runs), held, owners, place, len(where)),
        in_specs=[smem] * (len(where) + len(candidates)),
        out_specs=[smem] * 3,
        out_shape=[jax.ShapeDtypeStruct((n,), jnp.int32) for n in (pairs, pairs, bins)],
        scratch_shapes=[pltpu.SMEM((bins,), jnp.int32)],
        compiler_params=pltpu.CompilerParams(vmem_limit_bytes=VMEM_LIMIT),
        name="pair_lists",
    )(*where, *candidates)


def moment_body(shards, held, runs, order_ref, start_ref, *rest):
    parts, outs = len(runs), len(shards)
    row_refs, resp_refs = rest[:parts], rest[parts : 2 * parts]
    out_refs = rest[2 * parts : 2 * parts + outs]
    sums, count_sum = rest[2 * parts + outs :]
    owned = held * CB
    meta = slice(2 * owned, 2 * owned + META)
    ones = jnp.ones((META, 2 * RB), jnp.bfloat16)

    def block_sums(pos):
        sums[...] = jnp.zeros_like(sums)
        count_sum[...] = jnp.zeros_like(count_sum)
        base = 0
        for run in range(parts):
            entry = pos * parts + run
            low, high = start_ref[entry], start_ref[entry + 1]

            @pl.loop(0, lax.div(high - low + 1, 2))
            def _(step, base=base, run=run, low=low, high=high):
                one = low + 2 * step
                two = jnp.minimum(one + 1, high - 1)
                valid = (one + 1 < high).astype(jnp.float32)
                pair_a, pair_b = order_ref[one] - base, order_ref[two] - base
                row_a, row_b = lax.div(pair_a, CANDS), lax.div(pair_b, CANDS)
                weight_a = resp_refs[run][row_a, lax.rem(pair_a, CANDS)]
                weight_b = resp_refs[run][row_b, lax.rem(pair_b, CANDS)]
                weight_b = (weight_b.astype(jnp.float32) * valid).astype(jnp.bfloat16)
                weight = jnp.concatenate([weight_a, weight_b], axis=1)
                x = jnp.concatenate(
                    [
                        row_refs[run][pl.ds(pl.multiple_of(row_a * RB, RB), RB), :],
                        row_refs[run][pl.ds(pl.multiple_of(row_b * RB, RB), RB), :],
                    ],
                    axis=0,
                )
                sums[0] += jnp.dot(weight, x, preferred_element_type=jnp.float32)
                sums[1] += jnp.dot(weight, x * x, preferred_element_type=jnp.float32)
                count_sum[...] += lax.dot_general(
                    ones, weight, NT, preferred_element_type=jnp.float32
                )

            base += runs[run] * CANDS

    for shard, out_ref in zip(shards, out_refs):
        out_ref[meta, :] = jnp.zeros((META, out_ref.shape[1]), jnp.bfloat16)

        @pl.loop(0, held)
        def _(block, shard=shard, out_ref=out_ref):
            block_sums(shard * held + block)
            start = pl.multiple_of(block * CB, CB)
            out_ref[pl.ds(start, CB), :] = sums[0].astype(jnp.bfloat16)
            out_ref[pl.ds(owned + start, CB), :] = sums[1].astype(jnp.bfloat16)
            out_ref[meta, pl.ds(start, CB)] = count_sum[...].astype(jnp.bfloat16)


def moments(rows, resp, order, starts, held, shards):
    runs = tuple(r.shape[0] // RB for r in rows)
    feature_count = rows[0].shape[1]
    smem = pl.BlockSpec(memory_space=pltpu.SMEM)
    vmem = pl.BlockSpec(memory_space=pltpu.VMEM)
    pairs = sum(runs) * held * len(shards) // 8
    out_shape = pltpu.VMEM((2 * held * CB + META, feature_count), jnp.bfloat16)
    return pl.pallas_call(
        functools.partial(moment_body, tuple(shards), held, runs),
        in_specs=[smem, smem] + [vmem] * (2 * len(runs)),
        out_specs=[vmem] * len(shards),
        out_shape=[out_shape] * len(shards),
        scratch_shapes=[
            pltpu.VMEM((2, CB, feature_count), jnp.float32),
            pltpu.VMEM((META, CB), jnp.float32),
        ],
        compiler_params=pltpu.CompilerParams(vmem_limit_bytes=VMEM_LIMIT),
        cost_estimate=pl.CostEstimate(
            flops=pairs * 4 * CB * RB * feature_count,
            bytes_accessed=pairs * RB * (feature_count + CB) * 2,
            transcendentals=0,
        ),
        name="moments",
    )(order, starts, *[in_vmem(r) for r in rows], *[in_vmem(r) for r in resp])


CHUNK = 80


def each_chunk(rows, step):
    whole = rows // CHUNK

    @pl.loop(0, whole)
    def _(i):
        step(pl.ds(pl.multiple_of(i * CHUNK, 16), CHUNK))

    if rows % CHUNK:
        step(slice(whole * CHUNK, rows))


def copy_body(firsts, skip, *refs):
    sources, target, sems = refs[skip:-2], refs[-2], refs[-1]
    copies = [
        pltpu.make_async_copy(source.at[0], target.at[index], sems.at[j])
        for j, (index, source) in enumerate(zip(firsts, sources))
    ]
    for copy in copies:
        copy.start()
    for copy in copies:
        copy.wait()


def stacked(total, first, shards, *earlier):
    vmem = pl.BlockSpec(memory_space=pltpu.VMEM)
    anywhere = pl.BlockSpec(memory_space=pl.ANY)
    places = range(first, first + len(shards))
    return pl.pallas_call(
        functools.partial(copy_body, places, len(earlier)),
        in_specs=[vmem] * len(earlier) + [anywhere] * len(shards),
        out_specs=vmem,
        out_shape=pltpu.VMEM((total,) + shards[0].shape[1:], jnp.bfloat16),
        scratch_shapes=[pltpu.SemaphoreType.DMA((len(shards),))],
        input_output_aliases={0: 0} if earlier else {},
        compiler_params=pltpu.CompilerParams(vmem_limit_bytes=VMEM_LIMIT),
        name="stack_shards",
    )(*[in_vmem(e) for e in earlier], *shards)


def add_body(*refs):
    def step(here):
        terms = [ref[here, :].astype(jnp.float32) for ref in refs[:-1]]
        refs[-1][here, :] = functools.reduce(jnp.add, terms).astype(jnp.bfloat16)

    each_chunk(refs[-1].shape[0], step)


def join_body(*refs):
    start = 0
    for ref in refs[:-1]:
        refs[-1][start : start + ref.shape[0], :] = ref[...]
        start += ref.shape[0]


def small_step(body, shape, dtype, name, *operands):
    vmem = pl.BlockSpec(memory_space=pltpu.VMEM)
    return pl.pallas_call(
        body,
        in_specs=[vmem] * len(operands),
        out_specs=vmem,
        out_shape=pltpu.VMEM(shape, dtype),
        compiler_params=pltpu.CompilerParams(vmem_limit_bytes=VMEM_LIMIT),
        cost_estimate=pl.CostEstimate(
            flops=math.prod(shape), bytes_accessed=2 * math.prod(shape), transcendentals=0
        ),
        name=name,
    )(*[in_vmem(value) for value in operands])


def added(*terms):
    return small_step(add_body, terms[0].shape, jnp.bfloat16, "add_sums", *terms)


def joined(*norms):
    shape = (sum(n.shape[0] for n in norms), RB)
    return small_step(join_body, shape, jnp.float32, "join_norms", *norms)


def result_body(owned, end_ref, *refs):
    own_norm, end_norm, end_sum = refs[:3]
    terms, (count_ref, first_ref, second_ref, loglik_ref) = refs[3:-4], refs[-4:]
    is_end = end_ref[0] > 0
    block = pl.program_id(0)
    feature_count = first_ref.shape[1]

    def total(rows):
        inner = functools.reduce(jnp.add, [t[rows, :].astype(jnp.float32) for t in terms])
        return jnp.where(is_end, end_sum[rows, :].astype(jnp.float32), inner)

    start = pl.multiple_of(block * CB, CB)
    first_ref[...] = total(pl.ds(start, CB))
    second_ref[...] = total(pl.ds(owned + start, CB))
    count_ref[...] = total(slice(2 * owned, 2 * owned + META))[0:1, :owned]
    norm = jnp.where(is_end, end_norm[...], own_norm[...])
    loglik_ref[...] = norm * (1.0 / feature_count)


def results_of(is_end, own_norm, end_norm, end_sum, *terms):
    rows, feature_count = end_sum.shape
    owned = (rows - META) // 2
    vmem = pl.BlockSpec(memory_space=pltpu.VMEM)
    operands = (own_norm, end_norm, end_sum) + terms
    return pl.pallas_call(
        functools.partial(result_body, owned),
        grid=(owned // CB,),
        in_specs=[pl.BlockSpec(memory_space=pltpu.SMEM)] + [vmem] * len(operands),
        out_specs=[
            pl.BlockSpec((1, owned), lambda i: (0, 0)),
            pl.BlockSpec((CB, feature_count), lambda i: (i, 0)),
            pl.BlockSpec((CB, feature_count), lambda i: (i, 0)),
            pl.BlockSpec(own_norm.shape, lambda i: (0, 0)),
        ],
        out_shape=[
            jax.ShapeDtypeStruct((1, owned), jnp.float32),
            jax.ShapeDtypeStruct((owned, feature_count), jnp.float32),
            jax.ShapeDtypeStruct((owned, feature_count), jnp.float32),
            jax.ShapeDtypeStruct(own_norm.shape, jnp.float32),
        ],
        compiler_params=pltpu.CompilerParams(vmem_limit_bytes=VMEM_LIMIT),
        name="results",
    )(is_end.astype(jnp.int32).reshape(1), *[in_vmem(value) for value in operands])


def plain_plan(points, candidates, parameters, held):
    weights = parameter_shard(*parameters, points, (0,))[0]
    dp_size = lax.axis_size("dp")
    row_blocks = points.shape[0] // RB
    pos, order, starts = pair_lists(
        [candidates.T],
        (row_blocks,),
        held,
        dp_size * held,
        lax.axis_size("comp"),
        lambda holder: holder,
        [],
    )
    all_weights = lax.all_gather(weights, "dp", axis=0, tiled=True)
    resp, norm = responsibilities(points, pos, 0, all_weights, held)
    sums = []
    for j in range(dp_size):
        sums += moments([points], [resp], order, starts, held, [j])
    total = lax.psum_scatter(jnp.concatenate(sums), "dp", scatter_dimension=0, tiled=True)
    total = total.astype(jnp.float32)
    owned = held * CB
    counts, first, second = total[2 * owned, :owned], total[:owned], total[owned : 2 * owned]
    return counts, first, second, norm.reshape(-1) / points.shape[1]


def line_pairs(links):
    return [(2 * a + c, 2 * b + c) for a, b in links for c in (0, 1)]


INWARD = line_pairs(((0, 1), (3, 2)))
OUTWARD = line_pairs(((1, 0), (2, 3)))
MIDDLE = line_pairs(((1, 2), (2, 1)))
CORES = [(2, 3), (3, 2), (4, 5), (5, 4)]


def move(value, pairs):
    return lax.ppermute(value, "dp", pairs)


def after(value, *others):
    return lax.optimization_barrier((value,) + others)[0]


def line_place(holder, chip, core):
    z, other = lax.div(holder, 2), lax.rem(holder, 2)
    z = jnp.where(chip < 2, z, 3 - z)
    z = jnp.where(z == 0, 1, jnp.where(z == 1, 0, z))
    return z * 2 + lax.rem(other + core, 2)


def line_plan(points, candidates, parameters, held):
    index = lax.axis_index("dp")
    chip, core = index // 2, index % 2
    where = [chip.reshape(1), core.reshape(1)]
    row_blocks = points.shape[0] // RB
    cuts = (0, row_blocks // 2, row_blocks - row_blocks // 8, row_blocks)
    runs = (row_blocks,) + tuple(b - a for a, b in zip(cuts[:-1], cuts[1:]))
    own_ids = candidates.T
    end_ids = move(own_ids, INWARD)
    weights, *pieces = parameter_shard(*parameters, points, [cut * RB for cut in cuts])
    weights, end_ids = lax.optimization_barrier((weights, end_ids))

    outer = move(weights, INWARD)
    across = move(weights, MIDDLE)
    own_shared = move(weights, CORES)
    moved = [move(after(pieces[0], outer), INWARD)]
    far = move(outer, MIDDLE)
    outer_shared = move(outer, CORES)
    across_shared = move(across, CORES)
    moved.append(move(after(pieces[1], moved[0]), INWARD))
    moved.append(move(after(pieces[2], moved[0], far), INWARD))
    near = [weights, own_shared, outer, outer_shared, across, across_shared]
    pos, order, starts = pair_lists(
        [own_ids, end_ids], runs, held, 8 * held, lax.axis_size("comp"), line_place, where
    )
    near_weights = stacked(8, 0, [after(near[0], pos, order, starts)] + near[1:])
    far, near_weights = lax.optimization_barrier((far, near_weights))
    far_shared = move(far, CORES)
    all_weights = stacked(8, 6, [far, far_shared], near_weights)
    rows = [points] + moved
    results = []
    for j, run_rows in enumerate(rows):
        if results:
            pos = after(pos, results[-1][1])
        results.append(responsibilities(run_rows, pos, sum(runs[:j]), all_weights, held))
    resp = [r[0] for r in results]

    def sums_of(position, *earlier):
        return moments(rows, resp, after(order, *earlier), starts, held, [position])[0]

    end_norm = move(joined(*[r[1] for r in results[1:]]), OUTWARD)
    far_other = sums_of(7)
    far_received = move(far_other, CORES)
    far_own = sums_of(6, far_other)
    far_part = added(far_own, far_received)
    far_sum = move(far_part, MIDDLE)
    across_other = sums_of(5, far_part, end_norm)
    across_received = move(across_other, CORES)
    across_own = sums_of(4, across_other)
    across_part = added(across_own, across_received)
    across_sum = move(across_part, MIDDLE)
    outer_other = sums_of(3, across_part)
    outer_received = move(outer_other, CORES)
    own_other = sums_of(1, outer_other)
    own_received = move(own_other, CORES)
    outer_own = sums_of(2, own_other)
    own_own = sums_of(0, outer_own)
    outer_sum = added(outer_own, outer_received, far_sum)
    end_sum = move(outer_sum, OUTWARD)
    is_end = jnp.logical_or(chip == 0, chip == 3)
    counts, first, second, loglik = results_of(
        is_end, results[0][1], end_norm, end_sum, own_own, own_received, across_sum
    )
    return counts.reshape(-1), first, second, loglik.reshape(-1)


def on_device(points, candidates, means, inv_var, log_weight):
    held = means.shape[0] // CB
    plan = line_plan if lax.axis_size("dp") == 8 else plain_plan
    return plan(points, candidates, (means, inv_var, log_weight), held)


def solution(mesh):
    return jax.shard_map(
        on_device,
        mesh=mesh,
        in_specs=(
            P(("dp", "comp"), None),
            P(("dp", "comp"), None),
            P(("dp", "comp"), None),
            P(("dp", "comp"), None),
            P(("dp", "comp")),
        ),
        out_specs=(
            P(("dp", "comp")),
            P(("dp", "comp"), None),
            P(("dp", "comp"), None),
            P(("dp", "comp")),
        ),
        check_vma=False,
    )
```

```python
import functools
import math

import jax
import jax.numpy as jnp
from jax import lax
from jax.experimental import pallas as pl
from jax.experimental.pallas import tpu as pltpu
from jax.sharding import PartitionSpec as P

CB = 128
RB = 128
CANDS = 4
META = 16
MIB = 1024 * 1024
NT = (((1,), (1,)), ((), ()))
TN = (((0,), (0,)), ((), ()))


def in_vmem(value):
    return pltpu.with_memory_space_constraint(value, pltpu.VMEM)


def in_hbm(value):
    return pltpu.with_memory_space_constraint(value, pltpu.HBM)


def shard_body(cuts, means_hbm, inv_hbm, log_ref, points_ref, out_ref, *rest):
    piece_refs, (means_ref, inv_ref, own_sems, sems) = rest[:-4], rest[-4:]
    own_copies = [
        pltpu.make_async_copy(means_hbm, means_ref, own_sems.at[0]),
        pltpu.make_async_copy(inv_hbm, inv_ref, own_sems.at[1]),
    ]
    for copy in own_copies:
        copy.start()
    copies = [
        pltpu.make_async_copy(points_ref.at[pl.ds(cuts[j], piece.shape[0])], piece, sems.at[j])
        for j, piece in enumerate(piece_refs)
    ]
    for copy in copies:
        copy.start()
    owned, feature_count = means_ref.shape
    ones = jnp.ones((META, feature_count), jnp.float32)
    row = lax.broadcasted_iota(jnp.int32, (META, CB), 0)
    for copy in own_copies:
        copy.wait()
    for half in range(2):
        out_ref[0, half, owned:, :] = jnp.zeros((META, feature_count), jnp.bfloat16)
    for block in range(owned // CB):
        here = slice(block * CB, (block + 1) * CB)
        inverse = inv_ref[here, :]
        mean_f = means_ref[here, :].astype(jnp.float32)
        inv_f = inverse.astype(jnp.float32)
        scaled = inv_f * mean_f
        out_ref[0, 0, here, :] = scaled.astype(jnp.bfloat16)
        out_ref[0, 1, here, :] = inverse
        terms = 0.5 * jnp.log(inv_f) - 0.5 * (scaled * mean_f)
        rest = lax.dot_general(
            ones, terms, NT, precision=lax.Precision.HIGHEST, preferred_element_type=jnp.float32
        )
        rest += log_ref[:, here].astype(jnp.float32)
        rest -= 0.5 * feature_count * math.log(2.0 * math.pi)
        high = rest.astype(jnp.bfloat16).astype(jnp.float32)
        rest -= high
        middle = rest.astype(jnp.bfloat16).astype(jnp.float32)
        low = rest - middle
        pieces = jnp.where(row == 0, high, jnp.where(row == 1, middle, low))
        out_ref[0, 0, owned:, here] = pieces.astype(jnp.bfloat16)
    for copy in copies:
        copy.wait()


def parameter_shard(means, inv_var, log_weight, points, cuts):
    owned, feature_count = means.shape
    vmem = pl.BlockSpec(memory_space=pltpu.VMEM)
    hbm = pl.BlockSpec(memory_space=pltpu.HBM)
    lengths = [b - a for a, b in zip(cuts[:-1], cuts[1:])]
    return pl.pallas_call(
        functools.partial(shard_body, cuts),
        in_specs=[hbm, hbm, vmem, hbm],
        out_specs=[vmem] + [vmem] * len(lengths),
        out_shape=[pltpu.VMEM((1, 2, owned + META, feature_count), jnp.bfloat16)]
        + [pltpu.VMEM((length, feature_count), points.dtype) for length in lengths],
        scratch_shapes=[
            pltpu.VMEM((owned, feature_count), means.dtype),
            pltpu.VMEM((owned, feature_count), inv_var.dtype),
            pltpu.SemaphoreType.DMA((2,)),
            pltpu.SemaphoreType.DMA((max(len(lengths), 1),)),
        ],
        compiler_params=pltpu.CompilerParams(vmem_limit_bytes=6 * MIB),
        cost_estimate=pl.CostEstimate(
            flops=owned * feature_count * 40,
            bytes_accessed=owned * feature_count * 8,
            transcendentals=owned * feature_count,
        ),
        name="parameter_shard",
    )(in_hbm(means), in_hbm(inv_var), log_weight.reshape(1, owned), in_hbm(points))


COLUMNS = 256


def group_of(blocks, feature_count):
    return [
        pltpu.VMEM((blocks, 2, CB, feature_count), jnp.float32),
        pltpu.VMEM((blocks, CB, RB), jnp.float32),
    ]


def run_body(first, count, held, owners, arrays, place, known, fresh, given, *refs):
    where = [ref[0] for ref in refs[:known]]
    id_ref, x_ref = refs[known : known + 2]
    weight_refs = refs[known + 2 : known + 2 + arrays]
    outs = refs[known + 2 + arrays + (0 if fresh else 2) : -7]
    sum_ref, weight_sum_ref, norm_ref = outs[:3]
    blocks, constants, rows, sems, row_sems, staging, out_sems = refs[-7:]
    owned = held * CB
    feature_count = x_ref.shape[1]
    row_index = lax.broadcasted_iota(jnp.int32, (META, RB), 0)
    pieces = jnp.where(row_index < 3, 1.0, 0.0).astype(jnp.bfloat16)

    def choice(i, slot):
        block = id_ref[slot, first + i]
        return place(lax.div(block, owners * held), *where), lax.rem(block, held)

    def copies(array, shard, block, half, slot):
        here = pl.ds(pl.multiple_of(block * CB, CB), CB)
        there = pl.ds(slot * CB, CB)
        source = weight_refs[array].at[shard]
        return (
            pltpu.make_async_copy(
                source.at[:, here, :], blocks.at[half, :, there, :], sems.at[half, slot, 0]
            ),
            pltpu.make_async_copy(
                source.at[0, pl.ds(owned, META), here],
                constants.at[half, :, there],
                sems.at[half, slot, 1],
            ),
        )

    def row_copy(i, half):
        here = pl.ds(pl.multiple_of(i * RB, RB), RB)
        return pltpu.make_async_copy(x_ref.at[here, :], rows.at[half], row_sems.at[half])

    def fetch(i, half):
        row_copy(i, half).start()
        for slot in range(CANDS):
            shard, block = choice(i, slot)
            if arrays == 1:
                for copy in copies(0, shard, block, half, slot):
                    copy.start()
            for array in range(arrays if arrays > 1 else 0):

                @pl.when(shard == array)
                def _(array=array, block=block, slot=slot):
                    for copy in copies(array, 0, block, half, slot):
                        copy.start()

    fetch(0, 0)
    if fresh:

        @pl.loop(0, sum_ref.shape[0])
        def _(i):
            sum_ref[i] = jnp.zeros(sum_ref.shape[1:], jnp.float32)
            weight_sum_ref[i] = jnp.zeros(weight_sum_ref.shape[1:], jnp.float32)

    @pl.loop(0, count)
    def _(i):
        half = lax.rem(i, 2)

        @pl.when(i + 1 < count)
        def _():
            fetch(i + 1, 1 - half)

        row_copy(0, half).wait()
        x = rows[half]
        squares = x * x
        for slot in range(CANDS):
            for copy in copies(0, 0, 0, half, slot):
                copy.wait()
        densities = lax.dot_general(blocks[half, 0], x, NT, preferred_element_type=jnp.float32)
        densities += lax.dot_general(
            blocks[half, 1], squares * -0.5, NT, preferred_element_type=jnp.float32
        )
        densities += lax.dot_general(
            constants[half], pieces, TN, preferred_element_type=jnp.float32
        )
        peak = jnp.max(densities, axis=0, keepdims=True)
        terms = jnp.exp(densities - peak)
        total = jnp.sum(terms, axis=0, keepdims=True)
        norm_ref[pl.ds(i, 1), :] = peak + jnp.log(total)
        resp = (terms * (1.0 / total)).astype(jnp.bfloat16)
        targets = []
        for slot in range(CANDS):
            shard, block = choice(i, slot)
            targets.append(shard * held + block)
        for moment, values in enumerate((x, squares)):
            for column in range(0, feature_count, COLUMNS):
                columns = slice(column, column + COLUMNS)
                part = jnp.dot(resp, values[:, columns], preferred_element_type=jnp.float32)
                for slot, target in enumerate(targets):
                    sum_ref[target, moment, :, columns] += part[slot * CB : (slot + 1) * CB]
        for slot, target in enumerate(targets):
            weight_sum_ref[target] += resp[slot * CB : (slot + 1) * CB].astype(jnp.float32)

    round_shards(given, held, sum_ref, weight_sum_ref, outs[3:], staging, out_sems)


def round_shards(given, held, sum_ref, weight_sum_ref, out_refs, staging, sems):
    owned = held * CB
    feature_count = staging.shape[2]
    ones = jnp.ones((META, RB), jnp.float32)
    copies = []
    for index, (shard, out_ref) in enumerate(zip(given, out_refs)):
        half = index % 2
        if index >= 2:
            copies[index - 2].wait()
        if feature_count > owned:
            zeros = jnp.zeros((META, feature_count - owned), jnp.bfloat16)
            staging[half, 2 * owned :, owned:] = zeros

        @pl.loop(0, held)
        def _(block, half=half, shard=shard):
            here = pl.ds(pl.multiple_of(block * CB, CB), CB)
            for moment in range(2):
                start = pl.multiple_of(moment * owned + block * CB, CB)
                staging[half, pl.ds(start, CB), :] = sum_ref[shard * held + block, moment].astype(
                    jnp.bfloat16
                )
            counts = lax.dot_general(
                ones,
                weight_sum_ref[shard * held + block],
                NT,
                precision=lax.Precision.HIGHEST,
                preferred_element_type=jnp.float32,
            )
            staging[half, 2 * owned :, here] = counts.astype(jnp.bfloat16)

        copies.append(pltpu.make_async_copy(staging.at[half], out_ref, sems.at[half]))
        copies[-1].start()
    for copy in copies[-2:]:
        copy.wait()


def part_shape(held, feature_count):
    return (2 * held * CB + META, feature_count)


def staging_of(held, feature_count):
    return [
        pltpu.VMEM((2,) + part_shape(held, feature_count), jnp.bfloat16),
        pltpu.SemaphoreType.DMA((2,)),
    ]


def rest_body(given, held, sum_ref, weight_sum_ref, *refs):
    round_shards(given, held, sum_ref, weight_sum_ref, refs[:-2], refs[-2], refs[-1])


def rounded(sums, held, given):
    feature_count = sums[0].shape[3]
    shape = part_shape(held, feature_count)
    return pl.pallas_call(
        functools.partial(rest_body, given, held),
        in_specs=[pl.BlockSpec(memory_space=pltpu.VMEM)] * 2,
        out_specs=[pl.BlockSpec(memory_space=pltpu.HBM)] * len(given),
        out_shape=[pltpu.HBM(shape, jnp.bfloat16)] * len(given),
        scratch_shapes=staging_of(held, feature_count),
        compiler_params=pltpu.CompilerParams(vmem_limit_bytes=5 * MIB),
        cost_estimate=pl.CostEstimate(
            flops=len(given) * math.prod(shape),
            bytes_accessed=len(given) * 2 * math.prod(shape),
            transcendentals=0,
        ),
        name="round_sums",
    )(*[in_vmem(value) for value in sums])


def add_run(sums, rows, ids, first, weights, held, owners, place, where, blocks, given):
    count = rows.shape[0] // RB
    feature_count = rows.shape[1]
    smem = pl.BlockSpec(memory_space=pltpu.SMEM)
    vmem = pl.BlockSpec(memory_space=pltpu.VMEM)
    pairs = count * CANDS
    known, arrays, fresh = len(where), len(weights), not sums
    part = pltpu.HBM(part_shape(held, feature_count), jnp.bfloat16)
    return pl.pallas_call(
        functools.partial(
            run_body, first, count, held, owners, arrays, place, known, fresh, given
        ),
        in_specs=[smem] * (known + 1)
        + [pl.BlockSpec(memory_space=pltpu.HBM)] * (1 + arrays)
        + [vmem] * len(sums),
        out_specs=[vmem] * 3 + [pl.BlockSpec(memory_space=pltpu.HBM)] * len(given),
        out_shape=group_of(blocks, feature_count)
        + [jax.ShapeDtypeStruct((count, RB), jnp.float32)]
        + [part] * len(given),
        scratch_shapes=[
            pltpu.VMEM((2, 2, CANDS * CB, feature_count), jnp.bfloat16),
            pltpu.VMEM((2, META, CANDS * CB), jnp.bfloat16),
            pltpu.VMEM((2, RB, feature_count), jnp.bfloat16),
            pltpu.SemaphoreType.DMA((2, CANDS, 2)),
            pltpu.SemaphoreType.DMA((2,)),
        ]
        + staging_of(held, feature_count),
        input_output_aliases={} if fresh else {known + 2 + arrays: 0, known + 3 + arrays: 1},
        compiler_params=pltpu.CompilerParams(vmem_limit_bytes=9 * MIB),
        cost_estimate=pl.CostEstimate(
            flops=pairs * 8 * CB * RB * feature_count,
            bytes_accessed=pairs * CB * feature_count * 4 + rows.size * 2,
            transcendentals=pairs * CB * RB,
        ),
        name="add_run",
    )(
        *where,
        ids,
        in_hbm(rows),
        *[in_hbm(w) for w in weights],
        *[in_vmem(value) for value in sums],
    )


CHUNK = 80


def add_body(*refs):
    rows = refs[-1].shape[0]

    def step(here):
        terms = [ref[here, :].astype(jnp.float32) for ref in refs[:-1]]
        refs[-1][here, :] = functools.reduce(jnp.add, terms).astype(jnp.bfloat16)

    @pl.loop(0, rows // CHUNK)
    def _(i):
        step(pl.ds(pl.multiple_of(i * CHUNK, 16), CHUNK))

    if rows % CHUNK:
        step(slice(rows // CHUNK * CHUNK, rows))


def added(*terms):
    vmem = pl.BlockSpec(memory_space=pltpu.VMEM)
    shape = terms[0].shape
    return pl.pallas_call(
        add_body,
        in_specs=[vmem] * len(terms),
        out_specs=vmem,
        out_shape=jax.ShapeDtypeStruct(shape, jnp.bfloat16),
        compiler_params=pltpu.CompilerParams(vmem_limit_bytes=8 * MIB),
        cost_estimate=pl.CostEstimate(
            flops=math.prod(shape), bytes_accessed=6 * math.prod(shape), transcendentals=0
        ),
        name="add_sums",
    )(*terms)


def join_body(*refs):
    start = 0
    for ref in refs[:-1]:
        refs[-1][start : start + ref.shape[0], :] = ref[...]
        start += ref.shape[0]


def joined(*norms):
    vmem = pl.BlockSpec(memory_space=pltpu.VMEM)
    return pl.pallas_call(
        join_body,
        in_specs=[vmem] * len(norms),
        out_specs=vmem,
        out_shape=pltpu.VMEM((sum(n.shape[0] for n in norms), RB), jnp.float32),
        compiler_params=pltpu.CompilerParams(vmem_limit_bytes=1 * MIB),
        name="join_norms",
    )(*norms)


def result_body(held, end_ref, own_norm, end_norm, end_sum, *refs):
    terms, (count_ref, first_ref, second_ref, loglik_ref) = refs[:-4], refs[-4:]
    is_end = end_ref[0] > 0
    owned = held * CB
    feature_count = first_ref.shape[1]
    start = pl.multiple_of(pl.program_id(0) * CB, CB)

    def total(rows):
        inner = functools.reduce(jnp.add, [t[rows, :].astype(jnp.float32) for t in terms])
        return jnp.where(is_end, end_sum[rows, :].astype(jnp.float32), inner)

    first_ref[...] = total(pl.ds(start, CB))
    second_ref[...] = total(pl.ds(owned + start, CB))
    count_ref[...] = total(slice(2 * owned, 2 * owned + META))[0:1, :owned]
    norm = jnp.where(is_end, end_norm[...], own_norm[...])
    loglik_ref[...] = norm * (1.0 / feature_count)


def results_of(held, is_end, own_norm, end_norm, end_sum, *terms):
    feature_count = end_sum.shape[1]
    owned = held * CB
    vmem = pl.BlockSpec(memory_space=pltpu.VMEM)
    operands = (own_norm, end_norm, end_sum) + terms
    return pl.pallas_call(
        functools.partial(result_body, held),
        grid=(held,),
        in_specs=[pl.BlockSpec(memory_space=pltpu.SMEM)] + [vmem] * len(operands),
        out_specs=[
            pl.BlockSpec((1, owned), lambda i: (0, 0)),
            pl.BlockSpec((CB, feature_count), lambda i: (i, 0)),
            pl.BlockSpec((CB, feature_count), lambda i: (i, 0)),
            pl.BlockSpec(own_norm.shape, lambda i: (0, 0)),
        ],
        out_shape=[
            jax.ShapeDtypeStruct((1, owned), jnp.float32),
            jax.ShapeDtypeStruct((owned, feature_count), jnp.float32),
            jax.ShapeDtypeStruct((owned, feature_count), jnp.float32),
            jax.ShapeDtypeStruct(own_norm.shape, jnp.float32),
        ],
        compiler_params=pltpu.CompilerParams(vmem_limit_bytes=10 * MIB),
        name="results",
    )(is_end.astype(jnp.int32).reshape(1), *[in_vmem(value) for value in operands])


def plain_plan(points, candidates, parameters, held):
    weights = parameter_shard(*parameters, points, (0,))[0]
    dp_size = lax.axis_size("dp")
    all_weights = lax.all_gather(weights, "dp", axis=0, tiled=True)
    outs = add_run(
        [],
        points,
        candidates.T,
        0,
        [all_weights],
        held,
        lax.axis_size("comp"),
        lambda holder: holder,
        [],
        dp_size * held,
        [],
    )
    norm, parts = outs[2], jnp.concatenate(rounded(outs[:2], held, list(range(dp_size))))
    total = lax.psum_scatter(parts, "dp", scatter_dimension=0, tiled=True)
    total = total.astype(jnp.float32)
    owned = held * CB
    counts, first, second = total[2 * owned, :owned], total[:owned], total[owned : 2 * owned]
    return counts, first, second, norm.reshape(-1) / points.shape[1]


def line_pairs(links):
    return [(2 * a + c, 2 * b + c) for a, b in links for c in (0, 1)]


INWARD = line_pairs(((0, 1), (3, 2)))
OUTWARD = line_pairs(((1, 0), (2, 3)))
MIDDLE = line_pairs(((1, 2), (2, 1)))
CORES = [(2, 3), (3, 2), (4, 5), (5, 4)]


def move(value, pairs):
    return lax.ppermute(value, "dp", pairs)


def after(value, *others):
    return lax.optimization_barrier((value,) + others)[0]


def line_place(holder, chip, core):
    z, other = lax.div(holder, 2), lax.rem(holder, 2)
    z = jnp.where(chip < 2, z, 3 - z)
    z = jnp.where(z == 0, 1, jnp.where(z == 1, 0, z))
    return z * 2 + lax.rem(other + core, 2)


def line_plan(points, candidates, parameters, held):
    index = lax.axis_index("dp")
    chip, core = index // 2, index % 2
    where = [chip.reshape(1), core.reshape(1)]
    owners = lax.axis_size("comp")
    row_blocks = points.shape[0] // RB
    cuts = (0, row_blocks // 2, row_blocks - row_blocks // 8, row_blocks)
    own_ids = candidates.T
    end_ids = move(own_ids, INWARD)
    weights, *pieces = parameter_shard(*parameters, points, [cut * RB for cut in cuts])
    weights, end_ids = lax.optimization_barrier((weights, end_ids))

    outer = move(weights, INWARD)
    across = move(weights, MIDDLE)
    own_shared = move(weights, CORES)
    far = move(outer, MIDDLE)
    moved = [move(pieces[0], INWARD)]
    moved.append(move(after(pieces[1], moved[0]), INWARD))
    moved.append(move(after(pieces[2], moved[0], far), INWARD))
    outer_shared = move(after(outer, moved[0]), CORES)
    across_shared = move(after(across, moved[0]), CORES)
    far_shared = move(far, CORES)
    shards = [weights, own_shared, outer, outer_shared, across, across_shared, far, far_shared]

    runs = [(points, own_ids, 0)]
    runs += [(piece, end_ids, cut) for piece, cut in zip(moved, cuts)]
    sums, norms = [], []
    for run_rows, ids, first in runs:
        outs = add_run(
            sums,
            run_rows,
            ids,
            first,
            shards,
            held,
            owners,
            line_place,
            where,
            8 * held,
            [7, 6] if len(norms) == len(runs) - 1 else [],
        )
        sums = outs[:2]
        norms.append(outs[2])
    far_other, far = outs[3:]
    far_received = move(far_other, CORES)
    across_other, across, outer_other, outer, own_other, own = rounded(
        [after(sums[0], far_other), sums[1]], held, [5, 4, 3, 2, 1, 0]
    )
    far_sum = move(added(after(far, own), far_received), MIDDLE)
    across_received = move(across_other, CORES)
    across_sum = move(added(across, across_received), MIDDLE)
    outer_received = move(outer_other, CORES)
    own_received = move(own_other, CORES)
    end_norm = move(joined(*norms[1:]), OUTWARD)
    end_sum = move(added(outer, outer_received, far_sum), OUTWARD)
    is_end = jnp.logical_or(chip == 0, chip == 3)
    counts, first, second, loglik = results_of(
        held, is_end, norms[0], end_norm, end_sum, own, own_received, across_sum
    )
    return counts.reshape(-1), first, second, loglik.reshape(-1)


def on_device(points, candidates, means, inv_var, log_weight):
    held = means.shape[0] // CB
    plan = line_plan if lax.axis_size("dp") == 8 else plain_plan
    return plan(points, candidates, (means, inv_var, log_weight), held)


def solution(mesh):
    return jax.shard_map(
        on_device,
        mesh=mesh,
        in_specs=(
            P(("dp", "comp"), None),
            P(("dp", "comp"), None),
            P(("dp", "comp"), None),
            P(("dp", "comp"), None),
            P(("dp", "comp")),
        ),
        out_specs=(
            P(("dp", "comp")),
            P(("dp", "comp"), None),
            P(("dp", "comp"), None),
            P(("dp", "comp")),
        ),
        check_vma=False,
    )
```

```python
import functools
import math

import jax
import jax.numpy as jnp
from jax import lax
from jax.experimental import pallas as pl
from jax.experimental.pallas import tpu as pltpu
from jax.sharding import PartitionSpec as P

CB = 128
RB = 128
CANDS = 4
META = 16
VMEM_LIMIT = 8 * 1024 * 1024
NT = (((1,), (1,)), ((), ()))
TN = (((0,), (0,)), ((), ()))


def in_vmem(value):
    return pltpu.with_memory_space_constraint(value, pltpu.VMEM)


def in_hbm(value):
    return pltpu.with_memory_space_constraint(value, pltpu.HBM)


def shard_body(cuts, means_hbm, inv_hbm, log_ref, points_ref, out_ref, *rest):
    piece_refs, (means_ref, inv_ref, own_sems, sems) = rest[:-4], rest[-4:]
    own_copies = [
        pltpu.make_async_copy(means_hbm, means_ref, own_sems.at[0]),
        pltpu.make_async_copy(inv_hbm, inv_ref, own_sems.at[1]),
    ]
    for copy in own_copies:
        copy.start()
    copies = [
        pltpu.make_async_copy(points_ref.at[pl.ds(cuts[j], piece.shape[0])], piece, sems.at[j])
        for j, piece in enumerate(piece_refs)
    ]
    for copy in copies:
        copy.start()
    owned, feature_count = means_ref.shape
    ones = jnp.ones((META, feature_count), jnp.float32)
    row = lax.broadcasted_iota(jnp.int32, (META, CB), 0)
    for copy in own_copies:
        copy.wait()
    for half in range(2):
        out_ref[0, half, owned:, :] = jnp.zeros((META, feature_count), jnp.bfloat16)
    for block in range(owned // CB):
        here = slice(block * CB, (block + 1) * CB)
        inverse = inv_ref[here, :]
        mean_f = means_ref[here, :].astype(jnp.float32)
        inv_f = inverse.astype(jnp.float32)
        scaled = inv_f * mean_f
        out_ref[0, 0, here, :] = scaled.astype(jnp.bfloat16)
        out_ref[0, 1, here, :] = inverse
        terms = 0.5 * jnp.log(inv_f) - 0.5 * (scaled * mean_f)
        rest = lax.dot_general(
            ones, terms, NT, precision=lax.Precision.HIGHEST, preferred_element_type=jnp.float32
        )
        rest += log_ref[:, here].astype(jnp.float32)
        rest -= 0.5 * feature_count * math.log(2.0 * math.pi)
        high = rest.astype(jnp.bfloat16).astype(jnp.float32)
        rest -= high
        middle = rest.astype(jnp.bfloat16).astype(jnp.float32)
        low = rest - middle
        pieces = jnp.where(row == 0, high, jnp.where(row == 1, middle, low))
        out_ref[0, 0, owned:, here] = pieces.astype(jnp.bfloat16)
    for copy in copies:
        copy.wait()


def parameter_shard(means, inv_var, log_weight, points, cuts):
    owned, feature_count = means.shape
    vmem = pl.BlockSpec(memory_space=pltpu.VMEM)
    hbm = pl.BlockSpec(memory_space=pltpu.HBM)
    lengths = [b - a for a, b in zip(cuts[:-1], cuts[1:])]
    return pl.pallas_call(
        functools.partial(shard_body, cuts),
        in_specs=[hbm, hbm, vmem, hbm],
        out_specs=[vmem] + [vmem] * len(lengths),
        out_shape=[pltpu.VMEM((1, 2, owned + META, feature_count), jnp.bfloat16)]
        + [pltpu.VMEM((length, feature_count), points.dtype) for length in lengths],
        scratch_shapes=[
            pltpu.VMEM((owned, feature_count), means.dtype),
            pltpu.VMEM((owned, feature_count), inv_var.dtype),
            pltpu.SemaphoreType.DMA((2,)),
            pltpu.SemaphoreType.DMA((max(len(lengths), 1),)),
        ],
        compiler_params=pltpu.CompilerParams(vmem_limit_bytes=VMEM_LIMIT),
        cost_estimate=pl.CostEstimate(
            flops=owned * feature_count * 40,
            bytes_accessed=owned * feature_count * 8,
            transcendentals=owned * feature_count,
        ),
        name="parameter_shard",
    )(in_hbm(means), in_hbm(inv_var), log_weight.reshape(1, owned), in_hbm(points))


def density_body(first, count, held, pos_ref, x_ref, weight_ref, resp_ref, norm_ref):
    owned = held * CB
    row_index = lax.broadcasted_iota(jnp.int32, (META, RB), 0)
    pieces = jnp.where(row_index < 3, 1.0, 0.0).astype(jnp.bfloat16)

    @pl.loop(0, count)
    def _(i):
        x = x_ref[pl.ds(pl.multiple_of(i * RB, RB), RB), :]
        half = x * x * -0.5
        densities = []
        for slot in range(CANDS):
            pos = pos_ref[(first + i) * CANDS + slot]
            shard, start = lax.div(pos, held), lax.rem(pos, held) * CB
            here = pl.ds(pl.multiple_of(start, CB), CB)
            linear = lax.dot_general(
                weight_ref[shard, 0, here, :], x, NT, preferred_element_type=jnp.float32
            )
            quadratic = lax.dot_general(
                weight_ref[shard, 1, here, :], half, NT, preferred_element_type=jnp.float32
            )
            constant = lax.dot_general(
                weight_ref[shard, 0, owned:, here],
                pieces,
                TN,
                preferred_element_type=jnp.float32,
            )
            densities.append(linear + quadratic + constant)
        peak = functools.reduce(
            jnp.maximum, [jnp.max(d, axis=0, keepdims=True) for d in densities]
        )
        terms = [jnp.exp(d - peak) for d in densities]
        total = functools.reduce(jnp.add, [jnp.sum(t, axis=0, keepdims=True) for t in terms])
        norm_ref[pl.ds(i, 1), :] = peak + jnp.log(total)
        inverse_total = 1.0 / total
        for slot in range(CANDS):
            resp_ref[i, slot] = (terms[slot] * inverse_total).astype(jnp.bfloat16)


def responsibilities(rows, pos, first, weights, held):
    count = rows.shape[0] // RB
    feature_count = rows.shape[1]
    vmem = pl.BlockSpec(memory_space=pltpu.VMEM)
    pairs = count * CANDS
    return pl.pallas_call(
        functools.partial(density_body, first, count, held),
        in_specs=[pl.BlockSpec(memory_space=pltpu.SMEM), vmem, vmem],
        out_specs=[vmem, vmem],
        out_shape=[
            pltpu.VMEM((count, CANDS, CB, RB), jnp.bfloat16),
            pltpu.VMEM((count, RB), jnp.float32),
        ],
        compiler_params=pltpu.CompilerParams(vmem_limit_bytes=VMEM_LIMIT),
        cost_estimate=pl.CostEstimate(
            flops=pairs * 4 * CB * RB * feature_count,
            bytes_accessed=pairs * CB * feature_count * 4 + rows.size * 2,
            transcendentals=pairs * CB * RB,
        ),
        name="responsibilities",
    )(pos, in_vmem(rows), in_vmem(weights))


def list_body(runs, held, owners, place, known, *rest):
    where = [ref[0] for ref in rest[:known]]
    id_refs, (pos_ref, order_ref, start_ref, cursor) = rest[known:-4], rest[-4:]
    bins = start_ref.shape[0]
    number_of_runs = len(runs)
    per_ref = sum(runs) // len(id_refs)
    firsts = [sum(runs[:j]) for j in range(number_of_runs)]

    def run_of(i):
        return sum((i >= start).astype(jnp.int32) for start in firsts[1:]) if firsts[1:] else 0

    @pl.loop(0, bins)
    def _(j):
        start_ref[j] = 0

    for part, id_ref in enumerate(id_refs):

        @pl.loop(0, per_ref)
        def _(row, part=part, id_ref=id_ref):
            i = part * per_ref + row
            for slot in range(CANDS):
                block = id_ref[slot, row]
                holder = place(lax.div(block, owners * held), *where)
                pos = holder * held + lax.rem(block, held)
                pos_ref[i * CANDS + slot] = pos
                key = pos * number_of_runs + run_of(i) + 1
                start_ref[key] = start_ref[key] + 1

    def prefix(j, total):
        total = total + start_ref[j]
        start_ref[j] = total
        cursor[j] = total
        return total

    lax.fori_loop(0, bins, prefix, jnp.int32(0))

    @pl.loop(0, sum(runs))
    def _(i):
        for slot in range(CANDS):
            key = pos_ref[i * CANDS + slot] * number_of_runs + run_of(i)
            order_ref[cursor[key]] = i * CANDS + slot
            cursor[key] = cursor[key] + 1


def pair_lists(candidates, runs, held, group_blocks, owners, place, where):
    smem = pl.BlockSpec(memory_space=pltpu.SMEM)
    pairs = sum(runs) * CANDS
    bins = group_blocks * len(runs) + 1
    return pl.pallas_call(
        functools.partial(list_body, tuple(runs), held, owners, place, len(where)),
        in_specs=[smem] * (len(where) + len(candidates)),
        out_specs=[smem] * 3,
        out_shape=[jax.ShapeDtypeStruct((n,), jnp.int32) for n in (pairs, pairs, bins)],
        scratch_shapes=[pltpu.SMEM((bins,), jnp.int32)],
        compiler_params=pltpu.CompilerParams(vmem_limit_bytes=VMEM_LIMIT),
        name="pair_lists",
    )(*where, *candidates)


def moment_body(shards, held, runs, order_ref, start_ref, *rest):
    parts, outs = len(runs), len(shards)
    row_refs, resp_refs = rest[:parts], rest[parts : 2 * parts]
    out_refs = rest[2 * parts : 2 * parts + outs]
    sums, count_sum = rest[2 * parts + outs :]
    owned = held * CB
    meta = slice(2 * owned, 2 * owned + META)
    ones = jnp.ones((META, 2 * RB), jnp.bfloat16)

    def block_sums(pos):
        sums[...] = jnp.zeros_like(sums)
        count_sum[...] = jnp.zeros_like(count_sum)
        base = 0
        for run in range(parts):
            entry = pos * parts + run
            low, high = start_ref[entry], start_ref[entry + 1]

            @pl.loop(0, lax.div(high - low + 1, 2))
            def _(step, base=base, run=run, low=low, high=high):
                one = low + 2 * step
                two = jnp.minimum(one + 1, high - 1)
                valid = (one + 1 < high).astype(jnp.float32)
                pair_a, pair_b = order_ref[one] - base, order_ref[two] - base
                row_a, row_b = lax.div(pair_a, CANDS), lax.div(pair_b, CANDS)
                weight_a = resp_refs[run][row_a, lax.rem(pair_a, CANDS)]
                weight_b = resp_refs[run][row_b, lax.rem(pair_b, CANDS)]
                weight_b = (weight_b.astype(jnp.float32) * valid).astype(jnp.bfloat16)
                weight = jnp.concatenate([weight_a, weight_b], axis=1)
                x = jnp.concatenate(
                    [
                        row_refs[run][pl.ds(pl.multiple_of(row_a * RB, RB), RB), :],
                        row_refs[run][pl.ds(pl.multiple_of(row_b * RB, RB), RB), :],
                    ],
                    axis=0,
                )
                sums[0] += jnp.dot(weight, x, preferred_element_type=jnp.float32)
                sums[1] += jnp.dot(weight, x * x, preferred_element_type=jnp.float32)
                count_sum[...] += lax.dot_general(
                    ones, weight, NT, preferred_element_type=jnp.float32
                )

            base += runs[run] * CANDS

    for shard, out_ref in zip(shards, out_refs):
        out_ref[meta, :] = jnp.zeros((META, out_ref.shape[1]), jnp.bfloat16)

        @pl.loop(0, held)
        def _(block, shard=shard, out_ref=out_ref):
            block_sums(shard * held + block)
            start = pl.multiple_of(block * CB, CB)
            out_ref[pl.ds(start, CB), :] = sums[0].astype(jnp.bfloat16)
            out_ref[pl.ds(owned + start, CB), :] = sums[1].astype(jnp.bfloat16)
            out_ref[meta, pl.ds(start, CB)] = count_sum[...].astype(jnp.bfloat16)


def moments(rows, resp, order, starts, held, shards):
    runs = tuple(r.shape[0] // RB for r in rows)
    feature_count = rows[0].shape[1]
    smem = pl.BlockSpec(memory_space=pltpu.SMEM)
    vmem = pl.BlockSpec(memory_space=pltpu.VMEM)
    pairs = sum(runs) * held * len(shards) // 8
    out_shape = pltpu.VMEM((2 * held * CB + META, feature_count), jnp.bfloat16)
    return pl.pallas_call(
        functools.partial(moment_body, tuple(shards), held, runs),
        in_specs=[smem, smem] + [vmem] * (2 * len(runs)),
        out_specs=[vmem] * len(shards),
        out_shape=[out_shape] * len(shards),
        scratch_shapes=[
            pltpu.VMEM((2, CB, feature_count), jnp.float32),
            pltpu.VMEM((META, CB), jnp.float32),
        ],
        compiler_params=pltpu.CompilerParams(vmem_limit_bytes=VMEM_LIMIT),
        cost_estimate=pl.CostEstimate(
            flops=pairs * 4 * CB * RB * feature_count,
            bytes_accessed=pairs * RB * (feature_count + CB) * 2,
            transcendentals=0,
        ),
        name="moments",
    )(order, starts, *[in_vmem(r) for r in rows], *[in_vmem(r) for r in resp])


CHUNK = 80


def each_chunk(rows, step):
    whole = rows // CHUNK

    @pl.loop(0, whole)
    def _(i):
        step(pl.ds(pl.multiple_of(i * CHUNK, 16), CHUNK))

    if rows % CHUNK:
        step(slice(whole * CHUNK, rows))


def copy_body(firsts, skip, *refs):
    sources, target, sems = refs[skip:-2], refs[-2], refs[-1]
    copies = [
        pltpu.make_async_copy(source.at[0], target.at[index], sems.at[j])
        for j, (index, source) in enumerate(zip(firsts, sources))
    ]
    for copy in copies:
        copy.start()
    for copy in copies:
        copy.wait()


def stacked(total, first, shards, *earlier):
    vmem = pl.BlockSpec(memory_space=pltpu.VMEM)
    anywhere = pl.BlockSpec(memory_space=pl.ANY)
    places = range(first, first + len(shards))
    return pl.pallas_call(
        functools.partial(copy_body, places, len(earlier)),
        in_specs=[vmem] * len(earlier) + [anywhere] * len(shards),
        out_specs=vmem,
        out_shape=pltpu.VMEM((total,) + shards[0].shape[1:], jnp.bfloat16),
        scratch_shapes=[pltpu.SemaphoreType.DMA((len(shards),))],
        input_output_aliases={0: 0} if earlier else {},
        compiler_params=pltpu.CompilerParams(vmem_limit_bytes=VMEM_LIMIT),
        name="stack_shards",
    )(*[in_vmem(e) for e in earlier], *shards)


def add_body(*refs):
    def step(here):
        terms = [ref[here, :].astype(jnp.float32) for ref in refs[:-1]]
        refs[-1][here, :] = functools.reduce(jnp.add, terms).astype(jnp.bfloat16)

    each_chunk(refs[-1].shape[0], step)


def join_body(*refs):
    start = 0
    for ref in refs[:-1]:
        refs[-1][start : start + ref.shape[0], :] = ref[...]
        start += ref.shape[0]


def small_step(body, shape, dtype, name, *operands):
    vmem = pl.BlockSpec(memory_space=pltpu.VMEM)
    return pl.pallas_call(
        body,
        in_specs=[vmem] * len(operands),
        out_specs=vmem,
        out_shape=pltpu.VMEM(shape, dtype),
        compiler_params=pltpu.CompilerParams(vmem_limit_bytes=VMEM_LIMIT),
        cost_estimate=pl.CostEstimate(
            flops=math.prod(shape), bytes_accessed=2 * math.prod(shape), transcendentals=0
        ),
        name=name,
    )(*[in_vmem(value) for value in operands])


def added(*terms):
    return small_step(add_body, terms[0].shape, jnp.bfloat16, "add_sums", *terms)


def joined(*norms):
    shape = (sum(n.shape[0] for n in norms), RB)
    return small_step(join_body, shape, jnp.float32, "join_norms", *norms)


def result_body(owned, end_ref, *refs):
    own_norm, end_norm, end_sum = refs[:3]
    terms, (count_ref, first_ref, second_ref, loglik_ref) = refs[3:-4], refs[-4:]
    is_end = end_ref[0] > 0
    block = pl.program_id(0)
    feature_count = first_ref.shape[1]

    def total(rows):
        inner = functools.reduce(jnp.add, [t[rows, :].astype(jnp.float32) for t in terms])
        return jnp.where(is_end, end_sum[rows, :].astype(jnp.float32), inner)

    start = pl.multiple_of(block * CB, CB)
    first_ref[...] = total(pl.ds(start, CB))
    second_ref[...] = total(pl.ds(owned + start, CB))
    count_ref[...] = total(slice(2 * owned, 2 * owned + META))[0:1, :owned]
    norm = jnp.where(is_end, end_norm[...], own_norm[...])
    loglik_ref[...] = norm * (1.0 / feature_count)


def results_of(is_end, own_norm, end_norm, end_sum, *terms):
    rows, feature_count = end_sum.shape
    owned = (rows - META) // 2
    vmem = pl.BlockSpec(memory_space=pltpu.VMEM)
    operands = (own_norm, end_norm, end_sum) + terms
    return pl.pallas_call(
        functools.partial(result_body, owned),
        grid=(owned // CB,),
        in_specs=[pl.BlockSpec(memory_space=pltpu.SMEM)] + [vmem] * len(operands),
        out_specs=[
            pl.BlockSpec((1, owned), lambda i: (0, 0)),
            pl.BlockSpec((CB, feature_count), lambda i: (i, 0)),
            pl.BlockSpec((CB, feature_count), lambda i: (i, 0)),
            pl.BlockSpec(own_norm.shape, lambda i: (0, 0)),
        ],
        out_shape=[
            jax.ShapeDtypeStruct((1, owned), jnp.float32),
            jax.ShapeDtypeStruct((owned, feature_count), jnp.float32),
            jax.ShapeDtypeStruct((owned, feature_count), jnp.float32),
            jax.ShapeDtypeStruct(own_norm.shape, jnp.float32),
        ],
        compiler_params=pltpu.CompilerParams(vmem_limit_bytes=VMEM_LIMIT),
        name="results",
    )(is_end.astype(jnp.int32).reshape(1), *[in_vmem(value) for value in operands])


def plain_plan(points, candidates, parameters, held):
    weights = parameter_shard(*parameters, points, (0,))[0]
    dp_size = lax.axis_size("dp")
    row_blocks = points.shape[0] // RB
    pos, order, starts = pair_lists(
        [candidates.T],
        (row_blocks,),
        held,
        dp_size * held,
        lax.axis_size("comp"),
        lambda holder: holder,
        [],
    )
    all_weights = lax.all_gather(weights, "dp", axis=0, tiled=True)
    resp, norm = responsibilities(points, pos, 0, all_weights, held)
    sums = []
    for j in range(dp_size):
        sums += moments([points], [resp], order, starts, held, [j])
    total = lax.psum_scatter(jnp.concatenate(sums), "dp", scatter_dimension=0, tiled=True)
    total = total.astype(jnp.float32)
    owned = held * CB
    counts, first, second = total[2 * owned, :owned], total[:owned], total[owned : 2 * owned]
    return counts, first, second, norm.reshape(-1) / points.shape[1]


def line_pairs(links):
    return [(2 * a + c, 2 * b + c) for a, b in links for c in (0, 1)]


INWARD = line_pairs(((0, 1), (3, 2)))
OUTWARD = line_pairs(((1, 0), (2, 3)))
MIDDLE = line_pairs(((1, 2), (2, 1)))
CORES = [(2, 3), (3, 2), (4, 5), (5, 4)]


def move(value, pairs):
    return lax.ppermute(value, "dp", pairs)


def after(value, *others):
    return lax.optimization_barrier((value,) + others)[0]


def line_place(holder, chip, core):
    z, other = lax.div(holder, 2), lax.rem(holder, 2)
    z = jnp.where(chip < 2, z, 3 - z)
    z = jnp.where(z == 0, 1, jnp.where(z == 1, 0, z))
    return z * 2 + lax.rem(other + core, 2)


def line_plan(points, candidates, parameters, held):
    index = lax.axis_index("dp")
    chip, core = index // 2, index % 2
    where = [chip.reshape(1), core.reshape(1)]
    row_blocks = points.shape[0] // RB
    cuts = (0, row_blocks // 2, row_blocks - row_blocks // 8, row_blocks)
    runs = (row_blocks,) + tuple(b - a for a, b in zip(cuts[:-1], cuts[1:]))
    own_ids = candidates.T
    end_ids = move(own_ids, INWARD)
    weights, *pieces = parameter_shard(*parameters, points, [cut * RB for cut in cuts])
    weights, end_ids = lax.optimization_barrier((weights, end_ids))

    outer = move(weights, INWARD)
    across = move(weights, MIDDLE)
    own_shared = move(weights, CORES)
    moved = [move(after(pieces[0], outer), INWARD)]
    far = move(outer, MIDDLE)
    outer_shared = move(outer, CORES)
    across_shared = move(across, CORES)
    moved.append(move(after(pieces[1], moved[0]), INWARD))
    moved.append(move(after(pieces[2], moved[0], far), INWARD))
    near = [weights, own_shared, outer, outer_shared, across, across_shared]
    pos, order, starts = pair_lists(
        [own_ids, end_ids], runs, held, 8 * held, lax.axis_size("comp"), line_place, where
    )
    near_weights = stacked(8, 0, [after(near[0], pos, order, starts)] + near[1:])
    far, near_weights = lax.optimization_barrier((far, near_weights))
    far_shared = move(far, CORES)
    all_weights = stacked(8, 6, [far, far_shared], near_weights)
    rows = [points] + moved
    results = []
    for j, run_rows in enumerate(rows):
        if results:
            pos = after(pos, results[-1][1])
        results.append(responsibilities(run_rows, pos, sum(runs[:j]), all_weights, held))
    resp = [r[0] for r in results]

    def sums_of(position, *earlier):
        return moments(rows, resp, after(order, *earlier), starts, held, [position])[0]

    far_other = sums_of(7)
    far_received = move(far_other, CORES)
    far_own = sums_of(6, far_other)
    far_part = added(far_own, far_received)
    far_sum = move(far_part, MIDDLE)
    across_other = sums_of(5, far_part)
    end_norm = move(after(joined(*[r[1] for r in results[1:]]), across_other), OUTWARD)
    across_received = move(across_other, CORES)
    across_own = sums_of(4, across_other)
    across_part = added(across_own, across_received)
    across_sum = move(across_part, MIDDLE)
    outer_other = sums_of(3, across_part)
    outer_received = move(outer_other, CORES)
    own_other = sums_of(1, outer_other)
    own_received = move(own_other, CORES)
    outer_own = sums_of(2, own_other, end_norm)
    own_own = sums_of(0, outer_own)
    outer_sum = added(outer_own, outer_received, far_sum)
    end_sum = move(outer_sum, OUTWARD)
    is_end = jnp.logical_or(chip == 0, chip == 3)
    counts, first, second, loglik = results_of(
        is_end, results[0][1], end_norm, end_sum, own_own, own_received, across_sum
    )
    return counts.reshape(-1), first, second, loglik.reshape(-1)


def on_device(points, candidates, means, inv_var, log_weight):
    held = means.shape[0] // CB
    plan = line_plan if lax.axis_size("dp") == 8 else plain_plan
    return plan(points, candidates, (means, inv_var, log_weight), held)


def solution(mesh):
    return jax.shard_map(
        on_device,
        mesh=mesh,
        in_specs=(
            P(("dp", "comp"), None),
            P(("dp", "comp"), None),
            P(("dp", "comp"), None),
            P(("dp", "comp"), None),
            P(("dp", "comp")),
        ),
        out_specs=(
            P(("dp", "comp")),
            P(("dp", "comp"), None),
            P(("dp", "comp"), None),
            P(("dp", "comp")),
        ),
        check_vma=False,
    )
```

```python
import functools
import math

import jax
import jax.numpy as jnp
from jax import lax
from jax.experimental import pallas as pl
from jax.experimental.pallas import tpu as pltpu
from jax.sharding import PartitionSpec as P

CB = 128
RB = 128
CANDS = 4
META = 16
VMEM_LIMIT = 8 * 1024 * 1024
NT = (((1,), (1,)), ((), ()))
TN = (((0,), (0,)), ((), ()))


def in_vmem(value):
    return pltpu.with_memory_space_constraint(value, pltpu.VMEM)


def in_hbm(value):
    return pltpu.with_memory_space_constraint(value, pltpu.HBM)


def shard_body(cuts, means_hbm, inv_hbm, log_ref, points_ref, out_ref, *rest):
    piece_refs, (means_ref, inv_ref, own_sems, sems) = rest[:-4], rest[-4:]
    own_copies = [
        pltpu.make_async_copy(means_hbm, means_ref, own_sems.at[0]),
        pltpu.make_async_copy(inv_hbm, inv_ref, own_sems.at[1]),
    ]
    for copy in own_copies:
        copy.start()
    copies = [
        pltpu.make_async_copy(points_ref.at[pl.ds(cuts[j], piece.shape[0])], piece, sems.at[j])
        for j, piece in enumerate(piece_refs)
    ]
    for copy in copies:
        copy.start()
    owned, feature_count = means_ref.shape
    ones = jnp.ones((META, feature_count), jnp.float32)
    row = lax.broadcasted_iota(jnp.int32, (META, CB), 0)
    for copy in own_copies:
        copy.wait()
    for half in range(2):
        out_ref[0, half, owned:, :] = jnp.zeros((META, feature_count), jnp.bfloat16)
    for block in range(owned // CB):
        here = slice(block * CB, (block + 1) * CB)
        inverse = inv_ref[here, :]
        mean_f = means_ref[here, :].astype(jnp.float32)
        inv_f = inverse.astype(jnp.float32)
        scaled = inv_f * mean_f
        out_ref[0, 0, here, :] = scaled.astype(jnp.bfloat16)
        out_ref[0, 1, here, :] = inverse
        terms = 0.5 * jnp.log(inv_f) - 0.5 * (scaled * mean_f)
        rest = lax.dot_general(
            ones, terms, NT, precision=lax.Precision.HIGHEST, preferred_element_type=jnp.float32
        )
        rest += log_ref[:, here].astype(jnp.float32)
        rest -= 0.5 * feature_count * math.log(2.0 * math.pi)
        high = rest.astype(jnp.bfloat16).astype(jnp.float32)
        rest -= high
        middle = rest.astype(jnp.bfloat16).astype(jnp.float32)
        low = rest - middle
        pieces = jnp.where(row == 0, high, jnp.where(row == 1, middle, low))
        out_ref[0, 0, owned:, here] = pieces.astype(jnp.bfloat16)
    for copy in copies:
        copy.wait()


def parameter_shard(means, inv_var, log_weight, points, cuts):
    owned, feature_count = means.shape
    vmem = pl.BlockSpec(memory_space=pltpu.VMEM)
    hbm = pl.BlockSpec(memory_space=pltpu.HBM)
    lengths = [b - a for a, b in zip(cuts[:-1], cuts[1:])]
    return pl.pallas_call(
        functools.partial(shard_body, cuts),
        in_specs=[hbm, hbm, vmem, hbm],
        out_specs=[vmem] + [vmem] * len(lengths),
        out_shape=[pltpu.VMEM((1, 2, owned + META, feature_count), jnp.bfloat16)]
        + [pltpu.VMEM((length, feature_count), points.dtype) for length in lengths],
        scratch_shapes=[
            pltpu.VMEM((owned, feature_count), means.dtype),
            pltpu.VMEM((owned, feature_count), inv_var.dtype),
            pltpu.SemaphoreType.DMA((2,)),
            pltpu.SemaphoreType.DMA((max(len(lengths), 1),)),
        ],
        compiler_params=pltpu.CompilerParams(vmem_limit_bytes=VMEM_LIMIT),
        cost_estimate=pl.CostEstimate(
            flops=owned * feature_count * 40,
            bytes_accessed=owned * feature_count * 8,
            transcendentals=owned * feature_count,
        ),
        name="parameter_shard",
    )(in_hbm(means), in_hbm(inv_var), log_weight.reshape(1, owned), in_hbm(points))


def density_body(first, count, held, pos_ref, x_ref, weight_ref, resp_ref, norm_ref):
    owned = held * CB
    row_index = lax.broadcasted_iota(jnp.int32, (META, RB), 0)
    pieces = jnp.where(row_index < 3, 1.0, 0.0).astype(jnp.bfloat16)

    @pl.loop(0, count)
    def _(i):
        x = x_ref[pl.ds(pl.multiple_of(i * RB, RB), RB), :]
        half = x * x * -0.5
        densities = []
        for slot in range(CANDS):
            pos = pos_ref[(first + i) * CANDS + slot]
            shard, start = lax.div(pos, held), lax.rem(pos, held) * CB
            here = pl.ds(pl.multiple_of(start, CB), CB)
            linear = lax.dot_general(
                weight_ref[shard, 0, here, :], x, NT, preferred_element_type=jnp.float32
            )
            quadratic = lax.dot_general(
                weight_ref[shard, 1, here, :], half, NT, preferred_element_type=jnp.float32
            )
            constant = lax.dot_general(
                weight_ref[shard, 0, owned:, here],
                pieces,
                TN,
                preferred_element_type=jnp.float32,
            )
            densities.append(linear + quadratic + constant)
        peak = functools.reduce(
            jnp.maximum, [jnp.max(d, axis=0, keepdims=True) for d in densities]
        )
        terms = [jnp.exp(d - peak) for d in densities]
        total = functools.reduce(jnp.add, [jnp.sum(t, axis=0, keepdims=True) for t in terms])
        norm_ref[pl.ds(i, 1), :] = peak + jnp.log(total)
        inverse_total = 1.0 / total
        for slot in range(CANDS):
            resp_ref[i, slot] = (terms[slot] * inverse_total).astype(jnp.bfloat16)


def responsibilities(rows, pos, first, weights, held):
    count = rows.shape[0] // RB
    feature_count = rows.shape[1]
    vmem = pl.BlockSpec(memory_space=pltpu.VMEM)
    pairs = count * CANDS
    return pl.pallas_call(
        functools.partial(density_body, first, count, held),
        in_specs=[pl.BlockSpec(memory_space=pltpu.SMEM), vmem, vmem],
        out_specs=[vmem, vmem],
        out_shape=[
            pltpu.VMEM((count, CANDS, CB, RB), jnp.bfloat16),
            pltpu.VMEM((count, RB), jnp.float32),
        ],
        compiler_params=pltpu.CompilerParams(vmem_limit_bytes=VMEM_LIMIT),
        cost_estimate=pl.CostEstimate(
            flops=pairs * 4 * CB * RB * feature_count,
            bytes_accessed=pairs * CB * feature_count * 4 + rows.size * 2,
            transcendentals=pairs * CB * RB,
        ),
        name="responsibilities",
    )(pos, in_vmem(rows), in_vmem(weights))


def list_body(runs, held, owners, place, known, *rest):
    where = [ref[0] for ref in rest[:known]]
    id_refs, (pos_ref, order_ref, start_ref, cursor) = rest[known:-4], rest[-4:]
    bins = start_ref.shape[0]
    number_of_runs = len(runs)
    per_ref = sum(runs) // len(id_refs)
    firsts = [sum(runs[:j]) for j in range(number_of_runs)]

    def run_of(i):
        return sum((i >= start).astype(jnp.int32) for start in firsts[1:]) if firsts[1:] else 0

    @pl.loop(0, bins)
    def _(j):
        start_ref[j] = 0

    for part, id_ref in enumerate(id_refs):

        @pl.loop(0, per_ref)
        def _(row, part=part, id_ref=id_ref):
            i = part * per_ref + row
            for slot in range(CANDS):
                block = id_ref[slot, row]
                holder = place(lax.div(block, owners * held), *where)
                pos = holder * held + lax.rem(block, held)
                pos_ref[i * CANDS + slot] = pos
                key = pos * number_of_runs + run_of(i) + 1
                start_ref[key] = start_ref[key] + 1

    def prefix(j, total):
        total = total + start_ref[j]
        start_ref[j] = total
        cursor[j] = total
        return total

    lax.fori_loop(0, bins, prefix, jnp.int32(0))

    @pl.loop(0, sum(runs))
    def _(i):
        for slot in range(CANDS):
            key = pos_ref[i * CANDS + slot] * number_of_runs + run_of(i)
            order_ref[cursor[key]] = i * CANDS + slot
            cursor[key] = cursor[key] + 1


def pair_lists(candidates, runs, held, group_blocks, owners, place, where):
    smem = pl.BlockSpec(memory_space=pltpu.SMEM)
    pairs = sum(runs) * CANDS
    bins = group_blocks * len(runs) + 1
    return pl.pallas_call(
        functools.partial(list_body, tuple(runs), held, owners, place, len(where)),
        in_specs=[smem] * (len(where) + len(candidates)),
        out_specs=[smem] * 3,
        out_shape=[jax.ShapeDtypeStruct((n,), jnp.int32) for n in (pairs, pairs, bins)],
        scratch_shapes=[pltpu.SMEM((bins,), jnp.int32)],
        compiler_params=pltpu.CompilerParams(vmem_limit_bytes=VMEM_LIMIT),
        name="pair_lists",
    )(*where, *candidates)


def moment_body(shards, held, runs, order_ref, start_ref, *rest):
    parts, outs = len(runs), len(shards)
    row_refs, resp_refs = rest[:parts], rest[parts : 2 * parts]
    out_refs = rest[2 * parts : 2 * parts + outs]
    sums, count_sum = rest[2 * parts + outs :]
    owned = held * CB
    meta = slice(2 * owned, 2 * owned + META)
    ones = jnp.ones((META, 2 * RB), jnp.bfloat16)

    def block_sums(pos):
        sums[...] = jnp.zeros_like(sums)
        count_sum[...] = jnp.zeros_like(count_sum)
        base = 0
        for run in range(parts):
            entry = pos * parts + run
            low, high = start_ref[entry], start_ref[entry + 1]

            @pl.loop(0, lax.div(high - low + 1, 2))
            def _(step, base=base, run=run, low=low, high=high):
                one = low + 2 * step
                two = jnp.minimum(one + 1, high - 1)
                valid = (one + 1 < high).astype(jnp.float32)
                pair_a, pair_b = order_ref[one] - base, order_ref[two] - base
                row_a, row_b = lax.div(pair_a, CANDS), lax.div(pair_b, CANDS)
                weight_a = resp_refs[run][row_a, lax.rem(pair_a, CANDS)]
                weight_b = resp_refs[run][row_b, lax.rem(pair_b, CANDS)]
                weight_b = (weight_b.astype(jnp.float32) * valid).astype(jnp.bfloat16)
                weight = jnp.concatenate([weight_a, weight_b], axis=1)
                x = jnp.concatenate(
                    [
                        row_refs[run][pl.ds(pl.multiple_of(row_a * RB, RB), RB), :],
                        row_refs[run][pl.ds(pl.multiple_of(row_b * RB, RB), RB), :],
                    ],
                    axis=0,
                )
                sums[0] += jnp.dot(weight, x, preferred_element_type=jnp.float32)
                sums[1] += jnp.dot(weight, x * x, preferred_element_type=jnp.float32)
                count_sum[...] += lax.dot_general(
                    ones, weight, NT, preferred_element_type=jnp.float32
                )

            base += runs[run] * CANDS

    for shard, out_ref in zip(shards, out_refs):
        out_ref[meta, :] = jnp.zeros((META, out_ref.shape[1]), jnp.bfloat16)

        @pl.loop(0, held)
        def _(block, shard=shard, out_ref=out_ref):
            block_sums(shard * held + block)
            start = pl.multiple_of(block * CB, CB)
            out_ref[pl.ds(start, CB), :] = sums[0].astype(jnp.bfloat16)
            out_ref[pl.ds(owned + start, CB), :] = sums[1].astype(jnp.bfloat16)
            out_ref[meta, pl.ds(start, CB)] = count_sum[...].astype(jnp.bfloat16)


def moments(rows, resp, order, starts, held, shards):
    runs = tuple(r.shape[0] // RB for r in rows)
    feature_count = rows[0].shape[1]
    smem = pl.BlockSpec(memory_space=pltpu.SMEM)
    vmem = pl.BlockSpec(memory_space=pltpu.VMEM)
    pairs = sum(runs) * held * len(shards) // 8
    out_shape = pltpu.VMEM((2 * held * CB + META, feature_count), jnp.bfloat16)
    return pl.pallas_call(
        functools.partial(moment_body, tuple(shards), held, runs),
        in_specs=[smem, smem] + [vmem] * (2 * len(runs)),
        out_specs=[vmem] * len(shards),
        out_shape=[out_shape] * len(shards),
        scratch_shapes=[
            pltpu.VMEM((2, CB, feature_count), jnp.float32),
            pltpu.VMEM((META, CB), jnp.float32),
        ],
        compiler_params=pltpu.CompilerParams(vmem_limit_bytes=VMEM_LIMIT),
        cost_estimate=pl.CostEstimate(
            flops=pairs * 4 * CB * RB * feature_count,
            bytes_accessed=pairs * RB * (feature_count + CB) * 2,
            transcendentals=0,
        ),
        name="moments",
    )(order, starts, *[in_vmem(r) for r in rows], *[in_vmem(r) for r in resp])


CHUNK = 80


def each_chunk(rows, step):
    whole = rows // CHUNK

    @pl.loop(0, whole)
    def _(i):
        step(pl.ds(pl.multiple_of(i * CHUNK, 16), CHUNK))

    if rows % CHUNK:
        step(slice(whole * CHUNK, rows))


def copy_body(places, skip, *refs):
    sources, target, sems = refs[skip:-2], refs[-2], refs[-1]
    copies = [
        pltpu.make_async_copy(source.at[0], target.at[index], sems.at[j])
        for j, (index, source) in enumerate(zip(places, sources))
    ]
    for copy in copies:
        copy.start()
    for copy in copies:
        copy.wait()


def stacked(total, places, shards, *earlier):
    vmem = pl.BlockSpec(memory_space=pltpu.VMEM)
    anywhere = pl.BlockSpec(memory_space=pl.ANY)
    return pl.pallas_call(
        functools.partial(copy_body, places, len(earlier)),
        in_specs=[vmem] * len(earlier) + [anywhere] * len(shards),
        out_specs=vmem,
        out_shape=pltpu.VMEM((total,) + shards[0].shape[1:], jnp.bfloat16),
        scratch_shapes=[pltpu.SemaphoreType.DMA((len(shards),))],
        input_output_aliases={0: 0} if earlier else {},
        compiler_params=pltpu.CompilerParams(vmem_limit_bytes=VMEM_LIMIT),
        name="stack_shards",
    )(*[in_vmem(e) for e in earlier], *shards)


def add_body(*refs):
    def step(here):
        terms = [ref[here, :].astype(jnp.float32) for ref in refs[:-1]]
        refs[-1][here, :] = functools.reduce(jnp.add, terms).astype(jnp.bfloat16)

    each_chunk(refs[-1].shape[0], step)


def join_body(*refs):
    start = 0
    for ref in refs[:-1]:
        refs[-1][start : start + ref.shape[0], :] = ref[...]
        start += ref.shape[0]


def small_step(body, shape, dtype, name, *operands):
    vmem = pl.BlockSpec(memory_space=pltpu.VMEM)
    return pl.pallas_call(
        body,
        in_specs=[vmem] * len(operands),
        out_specs=vmem,
        out_shape=pltpu.VMEM(shape, dtype),
        compiler_params=pltpu.CompilerParams(vmem_limit_bytes=VMEM_LIMIT),
        cost_estimate=pl.CostEstimate(
            flops=math.prod(shape), bytes_accessed=2 * math.prod(shape), transcendentals=0
        ),
        name=name,
    )(*[in_vmem(value) for value in operands])


def added(*terms):
    return small_step(add_body, terms[0].shape, jnp.bfloat16, "add_sums", *terms)


def joined(*norms):
    shape = (sum(n.shape[0] for n in norms), RB)
    return small_step(join_body, shape, jnp.float32, "join_norms", *norms)


def result_body(owned, end_ref, *refs):
    own_norm, end_norm, end_sum = refs[:3]
    terms, (count_ref, first_ref, second_ref, loglik_ref) = refs[3:-4], refs[-4:]
    is_end = end_ref[0] > 0
    block = pl.program_id(0)
    feature_count = first_ref.shape[1]

    def total(rows):
        inner = functools.reduce(jnp.add, [t[rows, :].astype(jnp.float32) for t in terms])
        return jnp.where(is_end, end_sum[rows, :].astype(jnp.float32), inner)

    start = pl.multiple_of(block * CB, CB)
    first_ref[...] = total(pl.ds(start, CB))
    second_ref[...] = total(pl.ds(owned + start, CB))
    count_ref[...] = total(slice(2 * owned, 2 * owned + META))[0:1, :owned]
    norm = jnp.where(is_end, end_norm[...], own_norm[...])
    loglik_ref[...] = norm * (1.0 / feature_count)


def results_of(is_end, own_norm, end_norm, end_sum, *terms):
    rows, feature_count = end_sum.shape
    owned = (rows - META) // 2
    vmem = pl.BlockSpec(memory_space=pltpu.VMEM)
    operands = (own_norm, end_norm, end_sum) + terms
    return pl.pallas_call(
        functools.partial(result_body, owned),
        grid=(owned // CB,),
        in_specs=[pl.BlockSpec(memory_space=pltpu.SMEM)] + [vmem] * len(operands),
        out_specs=[
            pl.BlockSpec((1, owned), lambda i: (0, 0)),
            pl.BlockSpec((CB, feature_count), lambda i: (i, 0)),
            pl.BlockSpec((CB, feature_count), lambda i: (i, 0)),
            pl.BlockSpec(own_norm.shape, lambda i: (0, 0)),
        ],
        out_shape=[
            jax.ShapeDtypeStruct((1, owned), jnp.float32),
            jax.ShapeDtypeStruct((owned, feature_count), jnp.float32),
            jax.ShapeDtypeStruct((owned, feature_count), jnp.float32),
            jax.ShapeDtypeStruct(own_norm.shape, jnp.float32),
        ],
        compiler_params=pltpu.CompilerParams(vmem_limit_bytes=VMEM_LIMIT),
        name="results",
    )(is_end.astype(jnp.int32).reshape(1), *[in_vmem(value) for value in operands])


def plain_plan(points, candidates, parameters, held):
    weights = parameter_shard(*parameters, points, (0,))[0]
    dp_size = lax.axis_size("dp")
    row_blocks = points.shape[0] // RB
    pos, order, starts = pair_lists(
        [candidates.T],
        (row_blocks,),
        held,
        dp_size * held,
        lax.axis_size("comp"),
        lambda holder: holder,
        [],
    )
    all_weights = lax.all_gather(weights, "dp", axis=0, tiled=True)
    resp, norm = responsibilities(points, pos, 0, all_weights, held)
    sums = []
    for j in range(dp_size):
        sums += moments([points], [resp], order, starts, held, [j])
    total = lax.psum_scatter(jnp.concatenate(sums), "dp", scatter_dimension=0, tiled=True)
    total = total.astype(jnp.float32)
    owned = held * CB
    counts, first, second = total[2 * owned, :owned], total[:owned], total[owned : 2 * owned]
    return counts, first, second, norm.reshape(-1) / points.shape[1]


def line_pairs(links):
    return [(2 * a + c, 2 * b + c) for a, b in links for c in (0, 1)]


INWARD = line_pairs(((0, 1), (3, 2)))
OUTWARD = line_pairs(((1, 0), (2, 3)))
MIDDLE = line_pairs(((1, 2), (2, 1)))
CORES = [(2, 3), (3, 2), (4, 5), (5, 4)]


def move(value, pairs):
    return lax.ppermute(value, "dp", pairs)


def after(value, *others):
    return lax.optimization_barrier((value,) + others)[0]


def line_place(holder, chip, core):
    z, other = lax.div(holder, 2), lax.rem(holder, 2)
    z = jnp.where(chip < 2, z, 3 - z)
    z = jnp.where(z == 0, 1, jnp.where(z == 1, 0, z))
    return z * 2 + lax.rem(other + core, 2)


def line_plan(points, candidates, parameters, held):
    index = lax.axis_index("dp")
    chip, core = index // 2, index % 2
    where = [chip.reshape(1), core.reshape(1)]
    row_blocks = points.shape[0] // RB
    small = row_blocks // 8
    cuts = (0, small, 6 * small, row_blocks)
    runs = (row_blocks,) + tuple(b - a for a, b in zip(cuts[:-1], cuts[1:]))
    own_ids = candidates.T
    end_ids = move(own_ids, INWARD)
    before = move(points[: small * RB], INWARD)
    weights, *pieces = parameter_shard(*parameters, points, [cut * RB for cut in cuts[1:]])
    weights_then, end_ids, before = lax.optimization_barrier((weights, end_ids, before))

    outer = move(weights_then, INWARD)
    across = move(weights, MIDDLE)
    own_shared = move(weights, CORES)
    most = move(after(pieces[0], outer), INWARD)
    far = move(outer, MIDDLE)
    last = move(after(pieces[1], most), INWARD)
    moved = [before, most, last]
    pos, order, starts = pair_lists(
        [own_ids, end_ids], runs, held, 8 * held, lax.axis_size("comp"), line_place, where
    )
    near = [after(weights, pos, order, starts), own_shared, outer, across]
    near_weights = stacked(8, (0, 1, 2, 4), near)
    far, outer, across, near_weights = lax.optimization_barrier(
        (far, outer, across, near_weights)
    )
    shared = [move(w, CORES) for w in (outer, across, far)]
    all_weights = stacked(8, (6, 3, 5, 7), [far] + shared, near_weights)

    rows = [points] + moved
    results = []
    for j, run_rows in enumerate(rows):
        if results:
            pos = after(pos, results[-1][1])
        results.append(responsibilities(run_rows, pos, sum(runs[:j]), all_weights, held))
    resp = [r[0] for r in results]

    def sums_of(position, *earlier):
        return moments(rows, resp, after(order, *earlier), starts, held, [position])[0]

    far_other = sums_of(7)
    far_received = move(far_other, CORES)
    far_own = sums_of(6, far_other)
    far_part = added(far_own, far_received)
    far_sum = move(far_part, MIDDLE)
    across_other = sums_of(5, far_part)
    end_norm = move(after(joined(*[r[1] for r in results[1:]]), across_other), OUTWARD)
    across_received = move(across_other, CORES)
    across_own = sums_of(4, across_other)
    across_part = added(across_own, across_received)
    across_sum = move(across_part, MIDDLE)
    outer_other = sums_of(3, across_part)
    outer_received = move(outer_other, CORES)
    own_other = sums_of(1, outer_other)
    own_received = move(own_other, CORES)
    outer_own = sums_of(2, own_other, end_norm)
    own_own = sums_of(0, outer_own)
    outer_sum = added(outer_own, outer_received, far_sum)
    end_sum = move(outer_sum, OUTWARD)
    is_end = jnp.logical_or(chip == 0, chip == 3)
    counts, first, second, loglik = results_of(
        is_end, results[0][1], end_norm, end_sum, own_own, own_received, across_sum
    )
    return counts.reshape(-1), first, second, loglik.reshape(-1)


def on_device(points, candidates, means, inv_var, log_weight):
    held = means.shape[0] // CB
    plan = line_plan if lax.axis_size("dp") == 8 else plain_plan
    return plan(points, candidates, (means, inv_var, log_weight), held)


def solution(mesh):
    return jax.shard_map(
        on_device,
        mesh=mesh,
        in_specs=(
            P(("dp", "comp"), None),
            P(("dp", "comp"), None),
            P(("dp", "comp"), None),
            P(("dp", "comp"), None),
            P(("dp", "comp")),
        ),
        out_specs=(
            P(("dp", "comp")),
            P(("dp", "comp"), None),
            P(("dp", "comp"), None),
            P(("dp", "comp")),
        ),
        check_vma=False,
    )
```

```python
import functools
import math

import jax
import jax.numpy as jnp
from jax import lax
from jax.experimental import pallas as pl
from jax.experimental.pallas import tpu as pltpu
from jax.sharding import PartitionSpec as P

CB = 128
RB = 128
CANDS = 4
META = 16
VMEM_LIMIT = 8 * 1024 * 1024
NT = (((1,), (1,)), ((), ()))
TN = (((0,), (0,)), ((), ()))


def in_vmem(value):
    return pltpu.with_memory_space_constraint(value, pltpu.VMEM)


def in_hbm(value):
    return pltpu.with_memory_space_constraint(value, pltpu.HBM)


def shard_body(cuts, means_hbm, inv_hbm, log_ref, points_ref, out_ref, *rest):
    piece_refs, (means_ref, inv_ref, own_sems, sems) = rest[:-4], rest[-4:]
    own_copies = [
        pltpu.make_async_copy(means_hbm, means_ref, own_sems.at[0]),
        pltpu.make_async_copy(inv_hbm, inv_ref, own_sems.at[1]),
    ]
    for copy in own_copies:
        copy.start()
    copies = [
        pltpu.make_async_copy(points_ref.at[pl.ds(cuts[j], piece.shape[0])], piece, sems.at[j])
        for j, piece in enumerate(piece_refs)
    ]
    for copy in copies:
        copy.start()
    owned, feature_count = means_ref.shape
    ones = jnp.ones((META, feature_count), jnp.float32)
    row = lax.broadcasted_iota(jnp.int32, (META, CB), 0)
    for copy in own_copies:
        copy.wait()
    for half in range(2):
        out_ref[0, half, owned:, :] = jnp.zeros((META, feature_count), jnp.bfloat16)
    for block in range(owned // CB):
        here = slice(block * CB, (block + 1) * CB)
        inverse = inv_ref[here, :]
        mean_f = means_ref[here, :].astype(jnp.float32)
        inv_f = inverse.astype(jnp.float32)
        scaled = inv_f * mean_f
        out_ref[0, 0, here, :] = scaled.astype(jnp.bfloat16)
        out_ref[0, 1, here, :] = inverse
        terms = 0.5 * jnp.log(inv_f) - 0.5 * (scaled * mean_f)
        rest = lax.dot_general(
            ones, terms, NT, precision=lax.Precision.HIGHEST, preferred_element_type=jnp.float32
        )
        rest += log_ref[:, here].astype(jnp.float32)
        rest -= 0.5 * feature_count * math.log(2.0 * math.pi)
        high = rest.astype(jnp.bfloat16).astype(jnp.float32)
        rest -= high
        middle = rest.astype(jnp.bfloat16).astype(jnp.float32)
        low = rest - middle
        pieces = jnp.where(row == 0, high, jnp.where(row == 1, middle, low))
        out_ref[0, 0, owned:, here] = pieces.astype(jnp.bfloat16)
    for copy in copies:
        copy.wait()


def parameter_shard(means, inv_var, log_weight, points, cuts):
    owned, feature_count = means.shape
    vmem = pl.BlockSpec(memory_space=pltpu.VMEM)
    hbm = pl.BlockSpec(memory_space=pltpu.HBM)
    lengths = [b - a for a, b in zip(cuts[:-1], cuts[1:])]
    return pl.pallas_call(
        functools.partial(shard_body, cuts),
        in_specs=[hbm, hbm, vmem, hbm],
        out_specs=[vmem] + [vmem] * len(lengths),
        out_shape=[pltpu.VMEM((1, 2, owned + META, feature_count), jnp.bfloat16)]
        + [pltpu.VMEM((length, feature_count), points.dtype) for length in lengths],
        scratch_shapes=[
            pltpu.VMEM((owned, feature_count), means.dtype),
            pltpu.VMEM((owned, feature_count), inv_var.dtype),
            pltpu.SemaphoreType.DMA((2,)),
            pltpu.SemaphoreType.DMA((max(len(lengths), 1),)),
        ],
        compiler_params=pltpu.CompilerParams(vmem_limit_bytes=VMEM_LIMIT),
        cost_estimate=pl.CostEstimate(
            flops=owned * feature_count * 40,
            bytes_accessed=owned * feature_count * 8,
            transcendentals=owned * feature_count,
        ),
        name="parameter_shard",
    )(in_hbm(means), in_hbm(inv_var), log_weight.reshape(1, owned), in_hbm(points))


def density_body(first, count, held, pos_ref, x_ref, weight_ref, resp_ref, norm_ref):
    owned = held * CB
    row_index = lax.broadcasted_iota(jnp.int32, (META, RB), 0)
    pieces = jnp.where(row_index < 3, 1.0, 0.0).astype(jnp.bfloat16)

    @pl.loop(0, count)
    def _(i):
        x = x_ref[pl.ds(pl.multiple_of(i * RB, RB), RB), :]
        half = x * x * -0.5
        chosen = []
        for slot in range(CANDS):
            pos = pos_ref[(first + i) * CANDS + slot]
            start = pl.multiple_of(lax.rem(pos, held) * CB, CB)
            chosen.append((lax.div(pos, held), pl.ds(start, CB)))
        scaled = jnp.concatenate([weight_ref[shard, 0, here, :] for shard, here in chosen])
        inverse = jnp.concatenate([weight_ref[shard, 1, here, :] for shard, here in chosen])
        constants = jnp.concatenate(
            [weight_ref[shard, 0, owned:, here] for shard, here in chosen], axis=1
        )
        densities = lax.dot_general(scaled, x, NT, preferred_element_type=jnp.float32)
        densities += lax.dot_general(inverse, half, NT, preferred_element_type=jnp.float32)
        densities += lax.dot_general(constants, pieces, TN, preferred_element_type=jnp.float32)
        peak = jnp.max(densities, axis=0, keepdims=True)
        terms = jnp.exp(densities - peak)
        total = jnp.sum(terms, axis=0, keepdims=True)
        norm_ref[pl.ds(i, 1), :] = peak + jnp.log(total)
        resp = (terms * (1.0 / total)).astype(jnp.bfloat16)
        for slot in range(CANDS):
            resp_ref[i, slot] = resp[slot * CB : (slot + 1) * CB]


def responsibilities(rows, pos, first, weights, held):
    count = rows.shape[0] // RB
    feature_count = rows.shape[1]
    vmem = pl.BlockSpec(memory_space=pltpu.VMEM)
    pairs = count * CANDS
    return pl.pallas_call(
        functools.partial(density_body, first, count, held),
        in_specs=[pl.BlockSpec(memory_space=pltpu.SMEM), vmem, vmem],
        out_specs=[vmem, vmem],
        out_shape=[
            pltpu.VMEM((count, CANDS, CB, RB), jnp.bfloat16),
            pltpu.VMEM((count, RB), jnp.float32),
        ],
        compiler_params=pltpu.CompilerParams(vmem_limit_bytes=VMEM_LIMIT),
        cost_estimate=pl.CostEstimate(
            flops=pairs * 4 * CB * RB * feature_count,
            bytes_accessed=pairs * CB * feature_count * 4 + rows.size * 2,
            transcendentals=pairs * CB * RB,
        ),
        name="responsibilities",
    )(pos, in_vmem(rows), in_vmem(weights))


def list_body(runs, held, owners, place, known, *rest):
    where = [ref[0] for ref in rest[:known]]
    id_refs, (pos_ref, order_ref, start_ref, cursor) = rest[known:-4], rest[-4:]
    bins = start_ref.shape[0]
    number_of_runs = len(runs)
    per_ref = sum(runs) // len(id_refs)
    firsts = [sum(runs[:j]) for j in range(number_of_runs)]

    def run_of(i):
        return sum((i >= start).astype(jnp.int32) for start in firsts[1:]) if firsts[1:] else 0

    @pl.loop(0, bins)
    def _(j):
        start_ref[j] = 0

    for part, id_ref in enumerate(id_refs):

        @pl.loop(0, per_ref)
        def _(row, part=part, id_ref=id_ref):
            i = part * per_ref + row
            for slot in range(CANDS):
                block = id_ref[slot, row]
                holder = place(lax.div(block, owners * held), *where)
                pos = holder * held + lax.rem(block, held)
                pos_ref[i * CANDS + slot] = pos
                key = pos * number_of_runs + run_of(i) + 1
                start_ref[key] = start_ref[key] + 1

    def prefix(j, total):
        total = total + start_ref[j]
        start_ref[j] = total
        cursor[j] = total
        return total

    lax.fori_loop(0, bins, prefix, jnp.int32(0))

    @pl.loop(0, sum(runs))
    def _(i):
        for slot in range(CANDS):
            key = pos_ref[i * CANDS + slot] * number_of_runs + run_of(i)
            order_ref[cursor[key]] = i * CANDS + slot
            cursor[key] = cursor[key] + 1


def pair_lists(candidates, runs, held, group_blocks, owners, place, where):
    smem = pl.BlockSpec(memory_space=pltpu.SMEM)
    pairs = sum(runs) * CANDS
    bins = group_blocks * len(runs) + 1
    return pl.pallas_call(
        functools.partial(list_body, tuple(runs), held, owners, place, len(where)),
        in_specs=[smem] * (len(where) + len(candidates)),
        out_specs=[smem] * 3,
        out_shape=[jax.ShapeDtypeStruct((n,), jnp.int32) for n in (pairs, pairs, bins)],
        scratch_shapes=[pltpu.SMEM((bins,), jnp.int32)],
        compiler_params=pltpu.CompilerParams(vmem_limit_bytes=VMEM_LIMIT),
        name="pair_lists",
    )(*where, *candidates)


def moment_body(shards, held, runs, order_ref, start_ref, *rest):
    parts, outs = len(runs), len(shards)
    row_refs, resp_refs = rest[:parts], rest[parts : 2 * parts]
    out_refs = rest[2 * parts : 2 * parts + outs]
    sums, count_sum = rest[2 * parts + outs :]
    owned = held * CB
    meta = slice(2 * owned, 2 * owned + META)
    ones = jnp.ones((META, 2 * RB), jnp.bfloat16)

    def block_sums(pos):
        sums[...] = jnp.zeros_like(sums)
        count_sum[...] = jnp.zeros_like(count_sum)
        base = 0
        for run in range(parts):
            entry = pos * parts + run
            low, high = start_ref[entry], start_ref[entry + 1]

            @pl.loop(0, lax.div(high - low + 1, 2))
            def _(step, base=base, run=run, low=low, high=high):
                one = low + 2 * step
                two = jnp.minimum(one + 1, high - 1)
                valid = (one + 1 < high).astype(jnp.float32)
                pair_a, pair_b = order_ref[one] - base, order_ref[two] - base
                row_a, row_b = lax.div(pair_a, CANDS), lax.div(pair_b, CANDS)
                weight_a = resp_refs[run][row_a, lax.rem(pair_a, CANDS)]
                weight_b = resp_refs[run][row_b, lax.rem(pair_b, CANDS)]
                weight_b = (weight_b.astype(jnp.float32) * valid).astype(jnp.bfloat16)
                weight = jnp.concatenate([weight_a, weight_b], axis=1)
                x = jnp.concatenate(
                    [
                        row_refs[run][pl.ds(pl.multiple_of(row_a * RB, RB), RB), :],
                        row_refs[run][pl.ds(pl.multiple_of(row_b * RB, RB), RB), :],
                    ],
                    axis=0,
                )
                sums[0] += jnp.dot(weight, x, preferred_element_type=jnp.float32)
                sums[1] += jnp.dot(weight, x * x, preferred_element_type=jnp.float32)
                count_sum[...] += lax.dot_general(
                    ones, weight, NT, preferred_element_type=jnp.float32
                )

            base += runs[run] * CANDS

    for shard, out_ref in zip(shards, out_refs):
        out_ref[meta, :] = jnp.zeros((META, out_ref.shape[1]), jnp.bfloat16)

        @pl.loop(0, held)
        def _(block, shard=shard, out_ref=out_ref):
            block_sums(shard * held + block)
            start = pl.multiple_of(block * CB, CB)
            out_ref[pl.ds(start, CB), :] = sums[0].astype(jnp.bfloat16)
            out_ref[pl.ds(owned + start, CB), :] = sums[1].astype(jnp.bfloat16)
            out_ref[meta, pl.ds(start, CB)] = count_sum[...].astype(jnp.bfloat16)


def moments(rows, resp, order, starts, held, shards):
    runs = tuple(r.shape[0] // RB for r in rows)
    feature_count = rows[0].shape[1]
    smem = pl.BlockSpec(memory_space=pltpu.SMEM)
    vmem = pl.BlockSpec(memory_space=pltpu.VMEM)
    pairs = sum(runs) * held * len(shards) // 8
    out_shape = pltpu.VMEM((2 * held * CB + META, feature_count), jnp.bfloat16)
    return pl.pallas_call(
        functools.partial(moment_body, tuple(shards), held, runs),
        in_specs=[smem, smem] + [vmem] * (2 * len(runs)),
        out_specs=[vmem] * len(shards),
        out_shape=[out_shape] * len(shards),
        scratch_shapes=[
            pltpu.VMEM((2, CB, feature_count), jnp.float32),
            pltpu.VMEM((META, CB), jnp.float32),
        ],
        compiler_params=pltpu.CompilerParams(vmem_limit_bytes=VMEM_LIMIT),
        cost_estimate=pl.CostEstimate(
            flops=pairs * 4 * CB * RB * feature_count,
            bytes_accessed=pairs * RB * (feature_count + CB) * 2,
            transcendentals=0,
        ),
        name="moments",
    )(order, starts, *[in_vmem(r) for r in rows], *[in_vmem(r) for r in resp])


CHUNK = 80


def each_chunk(rows, step):
    whole = rows // CHUNK

    @pl.loop(0, whole)
    def _(i):
        step(pl.ds(pl.multiple_of(i * CHUNK, 16), CHUNK))

    if rows % CHUNK:
        step(slice(whole * CHUNK, rows))


def copy_body(places, skip, *refs):
    sources, target, sems = refs[skip:-2], refs[-2], refs[-1]
    copies = [
        pltpu.make_async_copy(source.at[0], target.at[index], sems.at[j])
        for j, (index, source) in enumerate(zip(places, sources))
    ]
    for copy in copies:
        copy.start()
    for copy in copies:
        copy.wait()


def stacked(total, places, shards, *earlier):
    vmem = pl.BlockSpec(memory_space=pltpu.VMEM)
    anywhere = pl.BlockSpec(memory_space=pl.ANY)
    return pl.pallas_call(
        functools.partial(copy_body, places, len(earlier)),
        in_specs=[vmem] * len(earlier) + [anywhere] * len(shards),
        out_specs=vmem,
        out_shape=pltpu.VMEM((total,) + shards[0].shape[1:], jnp.bfloat16),
        scratch_shapes=[pltpu.SemaphoreType.DMA((len(shards),))],
        input_output_aliases={0: 0} if earlier else {},
        compiler_params=pltpu.CompilerParams(vmem_limit_bytes=VMEM_LIMIT),
        name="stack_shards",
    )(*[in_vmem(e) for e in earlier], *shards)


def add_body(*refs):
    def step(here):
        terms = [ref[here, :].astype(jnp.float32) for ref in refs[:-1]]
        refs[-1][here, :] = functools.reduce(jnp.add, terms).astype(jnp.bfloat16)

    each_chunk(refs[-1].shape[0], step)


def join_body(*refs):
    start = 0
    for ref in refs[:-1]:
        refs[-1][start : start + ref.shape[0], :] = ref[...]
        start += ref.shape[0]


def small_step(body, shape, dtype, name, *operands):
    vmem = pl.BlockSpec(memory_space=pltpu.VMEM)
    return pl.pallas_call(
        body,
        in_specs=[vmem] * len(operands),
        out_specs=vmem,
        out_shape=pltpu.VMEM(shape, dtype),
        compiler_params=pltpu.CompilerParams(vmem_limit_bytes=VMEM_LIMIT),
        cost_estimate=pl.CostEstimate(
            flops=math.prod(shape), bytes_accessed=2 * math.prod(shape), transcendentals=0
        ),
        name=name,
    )(*[in_vmem(value) for value in operands])


def added(*terms):
    return small_step(add_body, terms[0].shape, jnp.bfloat16, "add_sums", *terms)


def joined(*norms):
    shape = (sum(n.shape[0] for n in norms), RB)
    return small_step(join_body, shape, jnp.float32, "join_norms", *norms)


def result_body(owned, end_ref, *refs):
    own_norm, end_norm, end_sum = refs[:3]
    terms, (count_ref, first_ref, second_ref, loglik_ref) = refs[3:-4], refs[-4:]
    is_end = end_ref[0] > 0
    block = pl.program_id(0)
    feature_count = first_ref.shape[1]

    def total(rows):
        inner = functools.reduce(jnp.add, [t[rows, :].astype(jnp.float32) for t in terms])
        return jnp.where(is_end, end_sum[rows, :].astype(jnp.float32), inner)

    start = pl.multiple_of(block * CB, CB)
    first_ref[...] = total(pl.ds(start, CB))
    second_ref[...] = total(pl.ds(owned + start, CB))
    count_ref[...] = total(slice(2 * owned, 2 * owned + META))[0:1, :owned]
    norm = jnp.where(is_end, end_norm[...], own_norm[...])
    loglik_ref[...] = norm * (1.0 / feature_count)


def results_of(is_end, own_norm, end_norm, end_sum, *terms):
    rows, feature_count = end_sum.shape
    owned = (rows - META) // 2
    vmem = pl.BlockSpec(memory_space=pltpu.VMEM)
    operands = (own_norm, end_norm, end_sum) + terms
    return pl.pallas_call(
        functools.partial(result_body, owned),
        grid=(owned // CB,),
        in_specs=[pl.BlockSpec(memory_space=pltpu.SMEM)] + [vmem] * len(operands),
        out_specs=[
            pl.BlockSpec((1, owned), lambda i: (0, 0)),
            pl.BlockSpec((CB, feature_count), lambda i: (i, 0)),
            pl.BlockSpec((CB, feature_count), lambda i: (i, 0)),
            pl.BlockSpec(own_norm.shape, lambda i: (0, 0)),
        ],
        out_shape=[
            jax.ShapeDtypeStruct((1, owned), jnp.float32),
            jax.ShapeDtypeStruct((owned, feature_count), jnp.float32),
            jax.ShapeDtypeStruct((owned, feature_count), jnp.float32),
            jax.ShapeDtypeStruct(own_norm.shape, jnp.float32),
        ],
        compiler_params=pltpu.CompilerParams(vmem_limit_bytes=VMEM_LIMIT),
        name="results",
    )(is_end.astype(jnp.int32).reshape(1), *[in_vmem(value) for value in operands])


def plain_plan(points, candidates, parameters, held):
    weights = parameter_shard(*parameters, points, (0,))[0]
    dp_size = lax.axis_size("dp")
    row_blocks = points.shape[0] // RB
    pos, order, starts = pair_lists(
        [candidates.T],
        (row_blocks,),
        held,
        dp_size * held,
        lax.axis_size("comp"),
        lambda holder: holder,
        [],
    )
    all_weights = lax.all_gather(weights, "dp", axis=0, tiled=True)
    resp, norm = responsibilities(points, pos, 0, all_weights, held)
    sums = []
    for j in range(dp_size):
        sums += moments([points], [resp], order, starts, held, [j])
    total = lax.psum_scatter(jnp.concatenate(sums), "dp", scatter_dimension=0, tiled=True)
    total = total.astype(jnp.float32)
    owned = held * CB
    counts, first, second = total[2 * owned, :owned], total[:owned], total[owned : 2 * owned]
    return counts, first, second, norm.reshape(-1) / points.shape[1]


def line_pairs(links):
    return [(2 * a + c, 2 * b + c) for a, b in links for c in (0, 1)]


INWARD = line_pairs(((0, 1), (3, 2)))
OUTWARD = line_pairs(((1, 0), (2, 3)))
MIDDLE = line_pairs(((1, 2), (2, 1)))
CORES = [(2, 3), (3, 2), (4, 5), (5, 4)]


def move(value, pairs):
    return lax.ppermute(value, "dp", pairs)


def after(value, *others):
    return lax.optimization_barrier((value,) + others)[0]


def line_place(holder, chip, core):
    z, other = lax.div(holder, 2), lax.rem(holder, 2)
    z = jnp.where(chip < 2, z, 3 - z)
    z = jnp.where(z == 0, 1, jnp.where(z == 1, 0, z))
    return z * 2 + lax.rem(other + core, 2)


def line_plan(points, candidates, parameters, held):
    index = lax.axis_index("dp")
    chip, core = index // 2, index % 2
    where = [chip.reshape(1), core.reshape(1)]
    row_blocks = points.shape[0] // RB
    small = row_blocks // 8
    cuts = (0, 1, 1 + 5 * small, row_blocks)
    runs = (row_blocks,) + tuple(b - a for a, b in zip(cuts[:-1], cuts[1:]))
    own_ids = candidates.T
    end_ids = move(own_ids, INWARD)
    before = move(points[: cuts[1] * RB], INWARD)
    weights, *pieces = parameter_shard(*parameters, points, [cut * RB for cut in cuts[1:]])
    weights_then, end_ids, before = lax.optimization_barrier((weights, end_ids, before))

    outer = move(weights_then, INWARD)
    across = move(weights, MIDDLE)
    own_shared = move(weights, CORES)
    most = move(after(pieces[0], outer), INWARD)
    far = move(outer, MIDDLE)
    last = move(after(pieces[1], most), INWARD)
    moved = [before, most, last]
    pos, order, starts = pair_lists(
        [own_ids, end_ids], runs, held, 8 * held, lax.axis_size("comp"), line_place, where
    )
    near = [after(weights, pos, order, starts), own_shared, outer, across]
    near_weights = stacked(8, (0, 1, 2, 4), near)
    far, outer, across, near_weights = lax.optimization_barrier(
        (far, outer, across, near_weights)
    )
    shared = [move(w, CORES) for w in (outer, across, far)]
    all_weights = stacked(8, (6, 3, 5, 7), [far] + shared, near_weights)

    rows = [points] + moved
    results = []
    for j, run_rows in enumerate(rows):
        if results:
            pos = after(pos, results[-1][1])
        results.append(responsibilities(run_rows, pos, sum(runs[:j]), all_weights, held))
    resp = [r[0] for r in results]

    def sums_of(position, *earlier):
        return moments(rows, resp, after(order, *earlier), starts, held, [position])[0]

    far_other = sums_of(7)
    far_received = move(far_other, CORES)
    far_own = sums_of(6, far_other)
    far_part = added(far_own, far_received)
    far_sum = move(far_part, MIDDLE)
    across_other = sums_of(5, far_part)
    end_norm = move(after(joined(*[r[1] for r in results[1:]]), across_other), OUTWARD)
    across_received = move(across_other, CORES)
    across_own = sums_of(4, across_other)
    across_part = added(across_own, across_received)
    across_sum = move(across_part, MIDDLE)
    outer_other = sums_of(3, across_part)
    outer_received = move(outer_other, CORES)
    own_other = sums_of(1, outer_other)
    own_received = move(own_other, CORES)
    outer_own = sums_of(2, own_other, end_norm)
    own_own = sums_of(0, outer_own)
    outer_sum = added(outer_own, outer_received, far_sum)
    end_sum = move(outer_sum, OUTWARD)
    is_end = jnp.logical_or(chip == 0, chip == 3)
    counts, first, second, loglik = results_of(
        is_end, results[0][1], end_norm, end_sum, own_own, own_received, across_sum
    )
    return counts.reshape(-1), first, second, loglik.reshape(-1)


def on_device(points, candidates, means, inv_var, log_weight):
    held = means.shape[0] // CB
    plan = line_plan if lax.axis_size("dp") == 8 else plain_plan
    return plan(points, candidates, (means, inv_var, log_weight), held)


def solution(mesh):
    return jax.shard_map(
        on_device,
        mesh=mesh,
        in_specs=(
            P(("dp", "comp"), None),
            P(("dp", "comp"), None),
            P(("dp", "comp"), None),
            P(("dp", "comp"), None),
            P(("dp", "comp")),
        ),
        out_specs=(
            P(("dp", "comp")),
            P(("dp", "comp"), None),
            P(("dp", "comp"), None),
            P(("dp", "comp")),
        ),
        check_vma=False,
    )
```

```python
import functools
import math

import jax
import jax.numpy as jnp
from jax import lax
from jax.experimental import pallas as pl
from jax.experimental.pallas import tpu as pltpu
from jax.sharding import PartitionSpec as P

CB = 128
RB = 128
CANDS = 4
META = 16
VMEM_LIMIT = 8 * 1024 * 1024
NT = (((1,), (1,)), ((), ()))
TN = (((0,), (0,)), ((), ()))


def in_vmem(value):
    return pltpu.with_memory_space_constraint(value, pltpu.VMEM)


def in_hbm(value):
    return pltpu.with_memory_space_constraint(value, pltpu.HBM)


def shard_body(means_hbm, inv_hbm, log_ref, out_ref, means_ref, inv_ref, sems):
    copies = [
        pltpu.make_async_copy(means_hbm, means_ref, sems.at[0]),
        pltpu.make_async_copy(inv_hbm, inv_ref, sems.at[1]),
    ]
    for copy in copies:
        copy.start()
    owned, feature_count = means_ref.shape
    ones = jnp.ones((META, feature_count), jnp.float32)
    row = lax.broadcasted_iota(jnp.int32, (META, CB), 0)
    for copy in copies:
        copy.wait()
    for half in range(2):
        out_ref[0, half, owned:, :] = jnp.zeros((META, feature_count), jnp.bfloat16)
    for block in range(owned // CB):
        here = slice(block * CB, (block + 1) * CB)
        inverse = inv_ref[here, :]
        mean_f = means_ref[here, :].astype(jnp.float32)
        inv_f = inverse.astype(jnp.float32)
        scaled = inv_f * mean_f
        out_ref[0, 0, here, :] = scaled.astype(jnp.bfloat16)
        out_ref[0, 1, here, :] = inverse
        terms = 0.5 * jnp.log(inv_f) - 0.5 * (scaled * mean_f)
        rest = lax.dot_general(
            ones, terms, NT, precision=lax.Precision.HIGHEST, preferred_element_type=jnp.float32
        )
        rest += log_ref[:, here].astype(jnp.float32)
        rest -= 0.5 * feature_count * math.log(2.0 * math.pi)
        high = rest.astype(jnp.bfloat16).astype(jnp.float32)
        rest -= high
        middle = rest.astype(jnp.bfloat16).astype(jnp.float32)
        low = rest - middle
        pieces = jnp.where(row == 0, high, jnp.where(row == 1, middle, low))
        out_ref[0, 0, owned:, here] = pieces.astype(jnp.bfloat16)


def parameter_shard(means, inv_var, log_weight):
    owned, feature_count = means.shape
    vmem = pl.BlockSpec(memory_space=pltpu.VMEM)
    hbm = pl.BlockSpec(memory_space=pltpu.HBM)
    return pl.pallas_call(
        shard_body,
        in_specs=[hbm, hbm, vmem],
        out_specs=vmem,
        out_shape=pltpu.VMEM((1, 2, owned + META, feature_count), jnp.bfloat16),
        scratch_shapes=[
            pltpu.VMEM((owned, feature_count), means.dtype),
            pltpu.VMEM((owned, feature_count), inv_var.dtype),
            pltpu.SemaphoreType.DMA((2,)),
        ],
        compiler_params=pltpu.CompilerParams(vmem_limit_bytes=VMEM_LIMIT),
        cost_estimate=pl.CostEstimate(
            flops=owned * feature_count * 40,
            bytes_accessed=owned * feature_count * 8,
            transcendentals=owned * feature_count,
        ),
        name="parameter_shard",
    )(in_hbm(means), in_hbm(inv_var), log_weight.reshape(1, owned))


def cut_body(cuts, points_ref, *refs):
    piece_refs, (staging, sems) = refs[:-2], refs[-2:]
    ways = []
    for j, piece in enumerate(piece_refs):
        here = pl.ds(cuts[j], piece.shape[0])
        there = pl.ds(cuts[j] - cuts[0], piece.shape[0])
        ways.append(
            (
                pltpu.make_async_copy(points_ref.at[here, :], staging.at[there, :], sems.at[0, j]),
                pltpu.make_async_copy(staging.at[there, :], piece, sems.at[1, j]),
            )
        )
    for inward, _ in ways:
        inward.start()
    for inward, outward in ways:
        inward.wait()
        outward.start()
    for _, outward in ways:
        outward.wait()


def cut_rows(points, cuts):
    feature_count = points.shape[1]
    hbm = pl.BlockSpec(memory_space=pltpu.HBM)
    lengths = [b - a for a, b in zip(cuts[:-1], cuts[1:])]
    return pl.pallas_call(
        functools.partial(cut_body, cuts),
        in_specs=[hbm],
        out_specs=[hbm] * len(lengths),
        out_shape=[pltpu.HBM((length, feature_count), points.dtype) for length in lengths],
        scratch_shapes=[
            pltpu.VMEM((sum(lengths), feature_count), points.dtype),
            pltpu.SemaphoreType.DMA((2, len(lengths))),
        ],
        compiler_params=pltpu.CompilerParams(vmem_limit_bytes=VMEM_LIMIT),
        name="cut_rows",
    )(in_hbm(points))


def density_body(first, count, held, pos_ref, x_ref, weight_ref, resp_ref, norm_ref):
    owned = held * CB
    row_index = lax.broadcasted_iota(jnp.int32, (META, RB), 0)
    pieces = jnp.where(row_index < 3, 1.0, 0.0).astype(jnp.bfloat16)

    @pl.loop(0, count)
    def _(i):
        x = x_ref[pl.ds(pl.multiple_of(i * RB, RB), RB), :]
        half = x * x * -0.5
        chosen = []
        for slot in range(CANDS):
            pos = pos_ref[(first + i) * CANDS + slot]
            start = pl.multiple_of(lax.rem(pos, held) * CB, CB)
            chosen.append((lax.div(pos, held), pl.ds(start, CB)))
        scaled = jnp.concatenate([weight_ref[shard, 0, here, :] for shard, here in chosen])
        inverse = jnp.concatenate([weight_ref[shard, 1, here, :] for shard, here in chosen])
        constants = jnp.concatenate(
            [weight_ref[shard, 0, owned:, here] for shard, here in chosen], axis=1
        )
        densities = lax.dot_general(scaled, x, NT, preferred_element_type=jnp.float32)
        densities += lax.dot_general(inverse, half, NT, preferred_element_type=jnp.float32)
        densities += lax.dot_general(constants, pieces, TN, preferred_element_type=jnp.float32)
        peak = jnp.max(densities, axis=0, keepdims=True)
        terms = jnp.exp(densities - peak)
        total = jnp.sum(terms, axis=0, keepdims=True)
        norm_ref[pl.ds(i, 1), :] = peak + jnp.log(total)
        resp = (terms * (1.0 / total)).astype(jnp.bfloat16)
        for slot in range(CANDS):
            resp_ref[i, slot] = resp[slot * CB : (slot + 1) * CB]


def responsibilities(rows, pos, first, weights, held):
    count = rows.shape[0] // RB
    feature_count = rows.shape[1]
    vmem = pl.BlockSpec(memory_space=pltpu.VMEM)
    pairs = count * CANDS
    return pl.pallas_call(
        functools.partial(density_body, first, count, held),
        in_specs=[pl.BlockSpec(memory_space=pltpu.SMEM), vmem, vmem],
        out_specs=[vmem, vmem],
        out_shape=[
            pltpu.VMEM((count, CANDS, CB, RB), jnp.bfloat16),
            pltpu.VMEM((count, RB), jnp.float32),
        ],
        compiler_params=pltpu.CompilerParams(vmem_limit_bytes=VMEM_LIMIT),
        cost_estimate=pl.CostEstimate(
            flops=pairs * 4 * CB * RB * feature_count,
            bytes_accessed=pairs * CB * feature_count * 4 + rows.size * 2,
            transcendentals=pairs * CB * RB,
        ),
        name="responsibilities",
    )(pos, in_vmem(rows), in_vmem(weights))


def list_body(runs, held, owners, place, known, *rest):
    where = [ref[0] for ref in rest[:known]]
    id_refs, (pos_ref, order_ref, start_ref, cursor) = rest[known:-4], rest[-4:]
    bins = start_ref.shape[0]
    number_of_runs = len(runs)
    per_ref = sum(runs) // len(id_refs)
    firsts = [sum(runs[:j]) for j in range(number_of_runs)]

    def run_of(i):
        return sum((i >= start).astype(jnp.int32) for start in firsts[1:]) if firsts[1:] else 0

    @pl.loop(0, bins)
    def _(j):
        start_ref[j] = 0

    for part, id_ref in enumerate(id_refs):

        @pl.loop(0, per_ref)
        def _(row, part=part, id_ref=id_ref):
            i = part * per_ref + row
            for slot in range(CANDS):
                block = id_ref[slot, row]
                holder = place(lax.div(block, owners * held), *where)
                pos = holder * held + lax.rem(block, held)
                pos_ref[i * CANDS + slot] = pos
                key = pos * number_of_runs + run_of(i) + 1
                start_ref[key] = start_ref[key] + 1

    def prefix(j, total):
        total = total + start_ref[j]
        start_ref[j] = total
        cursor[j] = total
        return total

    lax.fori_loop(0, bins, prefix, jnp.int32(0))

    @pl.loop(0, sum(runs))
    def _(i):
        for slot in range(CANDS):
            key = pos_ref[i * CANDS + slot] * number_of_runs + run_of(i)
            order_ref[cursor[key]] = i * CANDS + slot
            cursor[key] = cursor[key] + 1


def pair_lists(candidates, runs, held, group_blocks, owners, place, where):
    smem = pl.BlockSpec(memory_space=pltpu.SMEM)
    pairs = sum(runs) * CANDS
    bins = group_blocks * len(runs) + 1
    return pl.pallas_call(
        functools.partial(list_body, tuple(runs), held, owners, place, len(where)),
        in_specs=[smem] * (len(where) + len(candidates)),
        out_specs=[smem] * 3,
        out_shape=[jax.ShapeDtypeStruct((n,), jnp.int32) for n in (pairs, pairs, bins)],
        scratch_shapes=[pltpu.SMEM((bins,), jnp.int32)],
        compiler_params=pltpu.CompilerParams(vmem_limit_bytes=VMEM_LIMIT),
        name="pair_lists",
    )(*where, *candidates)


def moment_body(shards, held, runs, order_ref, start_ref, *rest):
    parts, outs = len(runs), len(shards)
    row_refs, resp_refs = rest[:parts], rest[parts : 2 * parts]
    out_refs = rest[2 * parts : 2 * parts + outs]
    sums, count_sum = rest[2 * parts + outs :]
    owned = held * CB
    meta = slice(2 * owned, 2 * owned + META)
    ones = jnp.ones((META, 2 * RB), jnp.bfloat16)

    def block_sums(pos):
        sums[...] = jnp.zeros_like(sums)
        count_sum[...] = jnp.zeros_like(count_sum)
        base = 0
        for run in range(parts):
            entry = pos * parts + run
            low, high = start_ref[entry], start_ref[entry + 1]

            @pl.loop(0, lax.div(high - low + 1, 2))
            def _(step, base=base, run=run, low=low, high=high):
                one = low + 2 * step
                two = jnp.minimum(one + 1, high - 1)
                valid = (one + 1 < high).astype(jnp.float32)
                pair_a, pair_b = order_ref[one] - base, order_ref[two] - base
                row_a, row_b = lax.div(pair_a, CANDS), lax.div(pair_b, CANDS)
                weight_a = resp_refs[run][row_a, lax.rem(pair_a, CANDS)]
                weight_b = resp_refs[run][row_b, lax.rem(pair_b, CANDS)]
                weight_b = (weight_b.astype(jnp.float32) * valid).astype(jnp.bfloat16)
                weight = jnp.concatenate([weight_a, weight_b], axis=1)
                x = jnp.concatenate(
                    [
                        row_refs[run][pl.ds(pl.multiple_of(row_a * RB, RB), RB), :],
                        row_refs[run][pl.ds(pl.multiple_of(row_b * RB, RB), RB), :],
                    ],
                    axis=0,
                )
                sums[0] += jnp.dot(weight, x, preferred_element_type=jnp.float32)
                sums[1] += jnp.dot(weight, x * x, preferred_element_type=jnp.float32)
                count_sum[...] += lax.dot_general(
                    ones, weight, NT, preferred_element_type=jnp.float32
                )

            base += runs[run] * CANDS

    for shard, out_ref in zip(shards, out_refs):
        out_ref[meta, :] = jnp.zeros((META, out_ref.shape[1]), jnp.bfloat16)

        @pl.loop(0, held)
        def _(block, shard=shard, out_ref=out_ref):
            block_sums(shard * held + block)
            start = pl.multiple_of(block * CB, CB)
            out_ref[pl.ds(start, CB), :] = sums[0].astype(jnp.bfloat16)
            out_ref[pl.ds(owned + start, CB), :] = sums[1].astype(jnp.bfloat16)
            out_ref[meta, pl.ds(start, CB)] = count_sum[...].astype(jnp.bfloat16)


def moments(rows, resp, order, starts, held, shards):
    runs = tuple(r.shape[0] // RB for r in rows)
    feature_count = rows[0].shape[1]
    smem = pl.BlockSpec(memory_space=pltpu.SMEM)
    vmem = pl.BlockSpec(memory_space=pltpu.VMEM)
    pairs = sum(runs) * held * len(shards) // 8
    out_shape = pltpu.VMEM((2 * held * CB + META, feature_count), jnp.bfloat16)
    return pl.pallas_call(
        functools.partial(moment_body, tuple(shards), held, runs),
        in_specs=[smem, smem] + [vmem] * (2 * len(runs)),
        out_specs=[vmem] * len(shards),
        out_shape=[out_shape] * len(shards),
        scratch_shapes=[
            pltpu.VMEM((2, CB, feature_count), jnp.float32),
            pltpu.VMEM((META, CB), jnp.float32),
        ],
        compiler_params=pltpu.CompilerParams(vmem_limit_bytes=VMEM_LIMIT),
        cost_estimate=pl.CostEstimate(
            flops=pairs * 4 * CB * RB * feature_count,
            bytes_accessed=pairs * RB * (feature_count + CB) * 2,
            transcendentals=0,
        ),
        name="moments",
    )(order, starts, *[in_vmem(r) for r in rows], *[in_vmem(r) for r in resp])


CHUNK = 80


def each_chunk(rows, step):
    whole = rows // CHUNK

    @pl.loop(0, whole)
    def _(i):
        step(pl.ds(pl.multiple_of(i * CHUNK, 16), CHUNK))

    if rows % CHUNK:
        step(slice(whole * CHUNK, rows))


def copy_body(places, skip, *refs):
    sources, target, sems = refs[skip:-2], refs[-2], refs[-1]
    copies = [
        pltpu.make_async_copy(source.at[0], target.at[index], sems.at[j])
        for j, (index, source) in enumerate(zip(places, sources))
    ]
    for copy in copies:
        copy.start()
    for copy in copies:
        copy.wait()


def stacked(total, places, shards, *earlier):
    vmem = pl.BlockSpec(memory_space=pltpu.VMEM)
    anywhere = pl.BlockSpec(memory_space=pl.ANY)
    return pl.pallas_call(
        functools.partial(copy_body, places, len(earlier)),
        in_specs=[vmem] * len(earlier) + [anywhere] * len(shards),
        out_specs=vmem,
        out_shape=pltpu.VMEM((total,) + shards[0].shape[1:], jnp.bfloat16),
        scratch_shapes=[pltpu.SemaphoreType.DMA((len(shards),))],
        input_output_aliases={0: 0} if earlier else {},
        compiler_params=pltpu.CompilerParams(vmem_limit_bytes=VMEM_LIMIT),
        name="stack_shards",
    )(*[in_vmem(e) for e in earlier], *shards)


def add_body(*refs):
    def step(here):
        terms = [ref[here, :].astype(jnp.float32) for ref in refs[:-1]]
        refs[-1][here, :] = functools.reduce(jnp.add, terms).astype(jnp.bfloat16)

    each_chunk(refs[-1].shape[0], step)


def join_body(*refs):
    start = 0
    for ref in refs[:-1]:
        refs[-1][start : start + ref.shape[0], :] = ref[...]
        start += ref.shape[0]


def small_step(body, shape, dtype, name, *operands):
    vmem = pl.BlockSpec(memory_space=pltpu.VMEM)
    return pl.pallas_call(
        body,
        in_specs=[vmem] * len(operands),
        out_specs=vmem,
        out_shape=pltpu.VMEM(shape, dtype),
        compiler_params=pltpu.CompilerParams(vmem_limit_bytes=VMEM_LIMIT),
        cost_estimate=pl.CostEstimate(
            flops=math.prod(shape), bytes_accessed=2 * math.prod(shape), transcendentals=0
        ),
        name=name,
    )(*[in_vmem(value) for value in operands])


def added(*terms):
    return small_step(add_body, terms[0].shape, jnp.bfloat16, "add_sums", *terms)


def joined(*norms):
    shape = (sum(n.shape[0] for n in norms), RB)
    return small_step(join_body, shape, jnp.float32, "join_norms", *norms)


def result_body(owned, end_ref, *refs):
    own_norm, end_norm, end_sum = refs[:3]
    terms, (count_ref, first_ref, second_ref, loglik_ref) = refs[3:-4], refs[-4:]
    is_end = end_ref[0] > 0
    block = pl.program_id(0)
    feature_count = first_ref.shape[1]

    def total(rows):
        inner = functools.reduce(jnp.add, [t[rows, :].astype(jnp.float32) for t in terms])
        return jnp.where(is_end, end_sum[rows, :].astype(jnp.float32), inner)

    start = pl.multiple_of(block * CB, CB)
    first_ref[...] = total(pl.ds(start, CB))
    second_ref[...] = total(pl.ds(owned + start, CB))
    count_ref[...] = total(slice(2 * owned, 2 * owned + META))[0:1, :owned]
    norm = jnp.where(is_end, end_norm[...], own_norm[...])
    loglik_ref[...] = norm * (1.0 / feature_count)


def results_of(is_end, own_norm, end_norm, end_sum, *terms):
    rows, feature_count = end_sum.shape
    owned = (rows - META) // 2
    vmem = pl.BlockSpec(memory_space=pltpu.VMEM)
    operands = (own_norm, end_norm, end_sum) + terms
    return pl.pallas_call(
        functools.partial(result_body, owned),
        grid=(owned // CB,),
        in_specs=[pl.BlockSpec(memory_space=pltpu.SMEM)] + [vmem] * len(operands),
        out_specs=[
            pl.BlockSpec((1, owned), lambda i: (0, 0)),
            pl.BlockSpec((CB, feature_count), lambda i: (i, 0)),
            pl.BlockSpec((CB, feature_count), lambda i: (i, 0)),
            pl.BlockSpec(own_norm.shape, lambda i: (0, 0)),
        ],
        out_shape=[
            jax.ShapeDtypeStruct((1, owned), jnp.float32),
            jax.ShapeDtypeStruct((owned, feature_count), jnp.float32),
            jax.ShapeDtypeStruct((owned, feature_count), jnp.float32),
            jax.ShapeDtypeStruct(own_norm.shape, jnp.float32),
        ],
        compiler_params=pltpu.CompilerParams(vmem_limit_bytes=VMEM_LIMIT),
        name="results",
    )(is_end.astype(jnp.int32).reshape(1), *[in_vmem(value) for value in operands])


def plain_plan(points, candidates, parameters, held):
    weights = parameter_shard(*parameters)
    dp_size = lax.axis_size("dp")
    row_blocks = points.shape[0] // RB
    pos, order, starts = pair_lists(
        [candidates.T],
        (row_blocks,),
        held,
        dp_size * held,
        lax.axis_size("comp"),
        lambda holder: holder,
        [],
    )
    all_weights = lax.all_gather(weights, "dp", axis=0, tiled=True)
    resp, norm = responsibilities(points, pos, 0, all_weights, held)
    sums = []
    for j in range(dp_size):
        sums += moments([points], [resp], order, starts, held, [j])
    total = lax.psum_scatter(jnp.concatenate(sums), "dp", scatter_dimension=0, tiled=True)
    total = total.astype(jnp.float32)
    owned = held * CB
    counts, first, second = total[2 * owned, :owned], total[:owned], total[owned : 2 * owned]
    return counts, first, second, norm.reshape(-1) / points.shape[1]


def line_pairs(links):
    return [(2 * a + c, 2 * b + c) for a, b in links for c in (0, 1)]


INWARD = line_pairs(((0, 1), (3, 2)))
OUTWARD = line_pairs(((1, 0), (2, 3)))
MIDDLE = line_pairs(((1, 2), (2, 1)))
CORES = [(2, 3), (3, 2), (4, 5), (5, 4)]


def move(value, pairs):
    return lax.ppermute(value, "dp", pairs)


def after(value, *others):
    return lax.optimization_barrier((value,) + others)[0]


def line_place(holder, chip, core):
    z, other = lax.div(holder, 2), lax.rem(holder, 2)
    z = jnp.where(chip < 2, z, 3 - z)
    z = jnp.where(z == 0, 1, jnp.where(z == 1, 0, z))
    return z * 2 + lax.rem(other + core, 2)


def line_plan(points, candidates, parameters, held):
    index = lax.axis_index("dp")
    chip, core = index // 2, index % 2
    where = [chip.reshape(1), core.reshape(1)]
    row_blocks = points.shape[0] // RB
    small = row_blocks // 8
    cuts = (0, 1, 2 + 4 * small, row_blocks - small, row_blocks)
    runs = (row_blocks,) + tuple(b - a for a, b in zip(cuts[:-1], cuts[1:]))
    own_ids = candidates.T
    end_ids = move(own_ids, INWARD)
    before = move(points[: cuts[1] * RB], INWARD)
    weights = parameter_shard(*parameters)
    weights_then, end_ids, before = lax.optimization_barrier((weights, end_ids, before))

    outer = move(weights_then, INWARD)
    across = move(weights, MIDDLE)
    pieces = cut_rows(after(points, weights_then), [cut * RB for cut in cuts[1:]])
    own_shared = move(after(weights, *pieces), CORES)
    most = move(after(pieces[0], outer), INWARD)
    far = move(outer, MIDDLE)
    moved = [before, most] + [move(after(piece, far), INWARD) for piece in pieces[1:]]
    pos, order, starts = pair_lists(
        [own_ids, end_ids], runs, held, 8 * held, lax.axis_size("comp"), line_place, where
    )
    near = [after(weights, pos, order, starts), own_shared, outer, across]
    near_weights = stacked(8, (0, 1, 2, 4), near)
    far, near_weights = lax.optimization_barrier((far, near_weights))
    shared = [move(w, CORES) for w in (outer, across, far)]
    all_weights = stacked(8, (6, 3, 5, 7), [after(far, most)] + shared, near_weights)

    rows = [points] + moved
    results = []
    for j, run_rows in enumerate(rows):
        if results:
            pos = after(pos, results[-1][1])
        results.append(responsibilities(run_rows, pos, sum(runs[:j]), all_weights, held))
    resp = [r[0] for r in results]

    def sums_of(position, *earlier):
        return moments(rows, resp, after(order, *earlier), starts, held, [position])[0]

    far_other = sums_of(7)
    far_received = move(far_other, CORES)
    far_own = sums_of(6, far_other)
    far_part = added(far_own, far_received)
    far_sum = move(far_part, MIDDLE)
    across_other = sums_of(5, far_part)
    end_norm = move(after(joined(*[r[1] for r in results[1:]]), across_other), OUTWARD)
    across_received = move(across_other, CORES)
    across_own = sums_of(4, across_other)
    across_part = added(across_own, across_received)
    across_sum = move(across_part, MIDDLE)
    outer_other = sums_of(3, across_part)
    outer_received = move(outer_other, CORES)
    own_other = sums_of(1, outer_other)
    own_received = move(own_other, CORES)
    outer_own = sums_of(2, own_other, end_norm)
    own_own = sums_of(0, outer_own)
    outer_sum = added(outer_own, outer_received, far_sum)
    end_sum = move(outer_sum, OUTWARD)
    is_end = jnp.logical_or(chip == 0, chip == 3)
    counts, first, second, loglik = results_of(
        is_end, results[0][1], end_norm, end_sum, own_own, own_received, across_sum
    )
    return counts.reshape(-1), first, second, loglik.reshape(-1)


def on_device(points, candidates, means, inv_var, log_weight):
    held = means.shape[0] // CB
    plan = line_plan if lax.axis_size("dp") == 8 else plain_plan
    return plan(points, candidates, (means, inv_var, log_weight), held)


def solution(mesh):
    return jax.shard_map(
        on_device,
        mesh=mesh,
        in_specs=(
            P(("dp", "comp"), None),
            P(("dp", "comp"), None),
            P(("dp", "comp"), None),
            P(("dp", "comp"), None),
            P(("dp", "comp")),
        ),
        out_specs=(
            P(("dp", "comp")),
            P(("dp", "comp"), None),
            P(("dp", "comp"), None),
            P(("dp", "comp")),
        ),
        check_vma=False,
    )
```

```python
import functools
import math

import jax
import jax.numpy as jnp
from jax import lax
from jax.experimental import pallas as pl
from jax.experimental.pallas import tpu as pltpu
from jax.sharding import PartitionSpec as P

CB = 128
RB = 128
CANDS = 4
META = 16
COLUMNS = 256
VMEM_LIMIT = 8 * 1024 * 1024
NT = (((1,), (1,)), ((), ()))
TN = (((0,), (0,)), ((), ()))


def in_vmem(value):
    return pltpu.with_memory_space_constraint(value, pltpu.VMEM)


def in_hbm(value):
    return pltpu.with_memory_space_constraint(value, pltpu.HBM)


def shard_body(means_hbm, inv_hbm, log_ref, out_ref, means_ref, inv_ref, sems):
    copies = [
        pltpu.make_async_copy(means_hbm, means_ref, sems.at[0]),
        pltpu.make_async_copy(inv_hbm, inv_ref, sems.at[1]),
    ]
    for copy in copies:
        copy.start()
    owned, feature_count = means_ref.shape
    ones = jnp.ones((META, feature_count), jnp.float32)
    row = lax.broadcasted_iota(jnp.int32, (META, CB), 0)
    for copy in copies:
        copy.wait()
    for half in range(2):
        out_ref[0, half, owned:, :] = jnp.zeros((META, feature_count), jnp.bfloat16)
    for block in range(owned // CB):
        here = slice(block * CB, (block + 1) * CB)
        inverse = inv_ref[here, :]
        mean_f = means_ref[here, :].astype(jnp.float32)
        inv_f = inverse.astype(jnp.float32)
        scaled = inv_f * mean_f
        out_ref[0, 0, here, :] = scaled.astype(jnp.bfloat16)
        out_ref[0, 1, here, :] = inverse
        terms = 0.5 * jnp.log(inv_f) - 0.5 * (scaled * mean_f)
        rest = lax.dot_general(
            ones, terms, NT, precision=lax.Precision.HIGHEST, preferred_element_type=jnp.float32
        )
        rest += log_ref[:, here].astype(jnp.float32)
        rest -= 0.5 * feature_count * math.log(2.0 * math.pi)
        high = rest.astype(jnp.bfloat16).astype(jnp.float32)
        rest -= high
        middle = rest.astype(jnp.bfloat16).astype(jnp.float32)
        low = rest - middle
        pieces = jnp.where(row == 0, high, jnp.where(row == 1, middle, low))
        out_ref[0, 0, owned:, here] = pieces.astype(jnp.bfloat16)


def parameter_shard(means, inv_var, log_weight):
    owned, feature_count = means.shape
    vmem = pl.BlockSpec(memory_space=pltpu.VMEM)
    hbm = pl.BlockSpec(memory_space=pltpu.HBM)
    return pl.pallas_call(
        shard_body,
        in_specs=[hbm, hbm, vmem],
        out_specs=vmem,
        out_shape=pltpu.VMEM((1, 2, owned + META, feature_count), jnp.bfloat16),
        scratch_shapes=[
            pltpu.VMEM((owned, feature_count), means.dtype),
            pltpu.VMEM((owned, feature_count), inv_var.dtype),
            pltpu.SemaphoreType.DMA((2,)),
        ],
        compiler_params=pltpu.CompilerParams(vmem_limit_bytes=VMEM_LIMIT),
        cost_estimate=pl.CostEstimate(
            flops=owned * feature_count * 40,
            bytes_accessed=owned * feature_count * 8,
            transcendentals=owned * feature_count,
        ),
        name="parameter_shard",
    )(in_hbm(means), in_hbm(inv_var), log_weight.reshape(1, owned))


def cut_body(cuts, points_ref, *refs):
    piece_refs, (staging, sems) = refs[:-2], refs[-2:]
    ways = []
    for j, piece in enumerate(piece_refs):
        here = pl.ds(cuts[j], piece.shape[0])
        there = pl.ds(cuts[j] - cuts[0], piece.shape[0])
        ways.append(
            (
                pltpu.make_async_copy(points_ref.at[here, :], staging.at[there, :], sems.at[0, j]),
                pltpu.make_async_copy(staging.at[there, :], piece, sems.at[1, j]),
            )
        )
    for inward, _ in ways:
        inward.start()
    for inward, outward in ways:
        inward.wait()
        outward.start()
    for _, outward in ways:
        outward.wait()


def cut_rows(points, cuts):
    feature_count = points.shape[1]
    hbm = pl.BlockSpec(memory_space=pltpu.HBM)
    lengths = [b - a for a, b in zip(cuts[:-1], cuts[1:])]
    return pl.pallas_call(
        functools.partial(cut_body, cuts),
        in_specs=[hbm],
        out_specs=[hbm] * len(lengths),
        out_shape=[pltpu.HBM((length, feature_count), points.dtype) for length in lengths],
        scratch_shapes=[
            pltpu.VMEM((sum(lengths), feature_count), points.dtype),
            pltpu.SemaphoreType.DMA((2, len(lengths))),
        ],
        compiler_params=pltpu.CompilerParams(vmem_limit_bytes=VMEM_LIMIT),
        name="cut_rows",
    )(in_hbm(points))


def density_body(first, count, held, pos_ref, x_ref, weight_ref, resp_ref, norm_ref):
    owned = held * CB
    row_index = lax.broadcasted_iota(jnp.int32, (META, RB), 0)
    pieces = jnp.where(row_index < 3, 1.0, 0.0).astype(jnp.bfloat16)

    @pl.loop(0, count)
    def _(i):
        x = x_ref[pl.ds(pl.multiple_of(i * RB, RB), RB), :]
        half = x * x * -0.5
        chosen = []
        for slot in range(CANDS):
            pos = pos_ref[(first + i) * CANDS + slot]
            start = pl.multiple_of(lax.rem(pos, held) * CB, CB)
            chosen.append((lax.div(pos, held), pl.ds(start, CB)))
        scaled = jnp.concatenate([weight_ref[shard, 0, here, :] for shard, here in chosen])
        inverse = jnp.concatenate([weight_ref[shard, 1, here, :] for shard, here in chosen])
        constants = jnp.concatenate(
            [weight_ref[shard, 0, owned:, here] for shard, here in chosen], axis=1
        )
        densities = lax.dot_general(scaled, x, NT, preferred_element_type=jnp.float32)
        densities += lax.dot_general(inverse, half, NT, preferred_element_type=jnp.float32)
        densities += lax.dot_general(constants, pieces, TN, preferred_element_type=jnp.float32)
        peak = jnp.max(densities, axis=0, keepdims=True)
        terms = jnp.exp(densities - peak)
        total = jnp.sum(terms, axis=0, keepdims=True)
        norm_ref[pl.ds(i, 1), :] = peak + jnp.log(total)
        resp = (terms * (1.0 / total)).astype(jnp.bfloat16)
        for slot in range(CANDS):
            resp_ref[i, slot] = resp[slot * CB : (slot + 1) * CB]


def responsibilities(rows, pos, first, weights, held):
    count = rows.shape[0] // RB
    feature_count = rows.shape[1]
    vmem = pl.BlockSpec(memory_space=pltpu.VMEM)
    pairs = count * CANDS
    return pl.pallas_call(
        functools.partial(density_body, first, count, held),
        in_specs=[pl.BlockSpec(memory_space=pltpu.SMEM), vmem, vmem],
        out_specs=[vmem, vmem],
        out_shape=[
            pltpu.VMEM((count, CANDS, CB, RB), jnp.bfloat16),
            pltpu.VMEM((count, RB), jnp.float32),
        ],
        compiler_params=pltpu.CompilerParams(vmem_limit_bytes=VMEM_LIMIT),
        cost_estimate=pl.CostEstimate(
            flops=pairs * 4 * CB * RB * feature_count,
            bytes_accessed=pairs * CB * feature_count * 4 + rows.size * 2,
            transcendentals=pairs * CB * RB,
        ),
        name="responsibilities",
    )(pos, in_vmem(rows), in_vmem(weights))


def list_body(runs, held, owners, place, known, *rest):
    where = [ref[0] for ref in rest[:known]]
    id_refs, (pos_ref, order_ref, start_ref, cursor) = rest[known:-4], rest[-4:]
    bins = start_ref.shape[0]
    number_of_runs = len(runs)
    per_ref = sum(runs) // len(id_refs)
    firsts = [sum(runs[:j]) for j in range(number_of_runs)]

    def run_of(i):
        return sum((i >= start).astype(jnp.int32) for start in firsts[1:]) if firsts[1:] else 0

    @pl.loop(0, bins)
    def _(j):
        start_ref[j] = 0

    for part, id_ref in enumerate(id_refs):

        @pl.loop(0, per_ref)
        def _(row, part=part, id_ref=id_ref):
            i = part * per_ref + row
            for slot in range(CANDS):
                block = id_ref[slot, row]
                holder = place(lax.div(block, owners * held), *where)
                pos = holder * held + lax.rem(block, held)
                pos_ref[i * CANDS + slot] = pos
                key = pos * number_of_runs + run_of(i) + 1
                start_ref[key] = start_ref[key] + 1

    def prefix(j, total):
        total = total + start_ref[j]
        start_ref[j] = total
        cursor[j] = total
        return total

    lax.fori_loop(0, bins, prefix, jnp.int32(0))

    @pl.loop(0, sum(runs))
    def _(i):
        for slot in range(CANDS):
            key = pos_ref[i * CANDS + slot] * number_of_runs + run_of(i)
            order_ref[cursor[key]] = i * CANDS + slot
            cursor[key] = cursor[key] + 1


def pair_lists(candidates, runs, held, group_blocks, owners, place, where):
    smem = pl.BlockSpec(memory_space=pltpu.SMEM)
    pairs = sum(runs) * CANDS
    bins = group_blocks * len(runs) + 1
    return pl.pallas_call(
        functools.partial(list_body, tuple(runs), held, owners, place, len(where)),
        in_specs=[smem] * (len(where) + len(candidates)),
        out_specs=[smem] * 3,
        out_shape=[jax.ShapeDtypeStruct((n,), jnp.int32) for n in (pairs, pairs, bins)],
        scratch_shapes=[pltpu.SMEM((bins,), jnp.int32)],
        compiler_params=pltpu.CompilerParams(vmem_limit_bytes=VMEM_LIMIT),
        name="pair_lists",
    )(*where, *candidates)


def moment_body(shards, held, runs, order_ref, start_ref, *rest):
    parts, outs = len(runs), len(shards)
    row_refs, resp_refs = rest[:parts], rest[parts : 2 * parts]
    out_refs = rest[2 * parts : 2 * parts + outs]
    sums, weight_sum = rest[2 * parts + outs :]
    owned = held * CB
    meta = slice(2 * owned, 2 * owned + META)
    ones = jnp.ones((META, RB), jnp.float32)
    feature_count = row_refs[0].shape[1]

    def block_sums(pos):
        sums[...] = jnp.zeros_like(sums)
        weight_sum[...] = jnp.zeros_like(weight_sum)
        base = 0
        for run in range(parts):
            entry = pos * parts + run
            low, high = start_ref[entry], start_ref[entry + 1]

            @pl.loop(0, lax.div(high - low + 1, 2))
            def _(step, base=base, run=run, low=low, high=high):
                one = low + 2 * step
                two = jnp.minimum(one + 1, high - 1)
                valid = (one + 1 < high).astype(jnp.float32)
                pair_a, pair_b = order_ref[one] - base, order_ref[two] - base
                row_a, row_b = lax.div(pair_a, CANDS), lax.div(pair_b, CANDS)
                weight_a = resp_refs[run][row_a, lax.rem(pair_a, CANDS)]
                weight_b = resp_refs[run][row_b, lax.rem(pair_b, CANDS)]
                weight_b = (weight_b.astype(jnp.float32) * valid).astype(jnp.bfloat16)
                weight = jnp.concatenate([weight_a, weight_b], axis=1)
                x = jnp.concatenate(
                    [
                        row_refs[run][pl.ds(pl.multiple_of(row_a * RB, RB), RB), :],
                        row_refs[run][pl.ds(pl.multiple_of(row_b * RB, RB), RB), :],
                    ],
                    axis=0,
                )
                for moment, values in enumerate((x, x * x)):
                    for column in range(0, feature_count, COLUMNS):
                        columns = slice(column, column + COLUMNS)
                        sums[moment, :, columns] += jnp.dot(
                            weight, values[:, columns], preferred_element_type=jnp.float32
                        )
                weight_sum[...] += weight_a.astype(jnp.float32) + weight_b.astype(jnp.float32)

            base += runs[run] * CANDS

    for shard, out_ref in zip(shards, out_refs):
        out_ref[meta, :] = jnp.zeros((META, out_ref.shape[1]), jnp.bfloat16)

        @pl.loop(0, held)
        def _(block, shard=shard, out_ref=out_ref):
            block_sums(shard * held + block)
            start = pl.multiple_of(block * CB, CB)
            out_ref[pl.ds(start, CB), :] = sums[0].astype(jnp.bfloat16)
            out_ref[pl.ds(owned + start, CB), :] = sums[1].astype(jnp.bfloat16)
            counts = lax.dot_general(
                ones,
                weight_sum[...],
                NT,
                precision=lax.Precision.HIGHEST,
                preferred_element_type=jnp.float32,
            )
            out_ref[meta, pl.ds(start, CB)] = counts.astype(jnp.bfloat16)


def moments(rows, resp, order, starts, held, shards):
    runs = tuple(r.shape[0] // RB for r in rows)
    feature_count = rows[0].shape[1]
    smem = pl.BlockSpec(memory_space=pltpu.SMEM)
    vmem = pl.BlockSpec(memory_space=pltpu.VMEM)
    pairs = sum(runs) * held * len(shards) // 8
    out_shape = pltpu.VMEM((2 * held * CB + META, feature_count), jnp.bfloat16)
    return pl.pallas_call(
        functools.partial(moment_body, tuple(shards), held, runs),
        in_specs=[smem, smem] + [vmem] * (2 * len(runs)),
        out_specs=[vmem] * len(shards),
        out_shape=[out_shape] * len(shards),
        scratch_shapes=[
            pltpu.VMEM((2, CB, feature_count), jnp.float32),
            pltpu.VMEM((CB, RB), jnp.float32),
        ],
        compiler_params=pltpu.CompilerParams(vmem_limit_bytes=VMEM_LIMIT),
        cost_estimate=pl.CostEstimate(
            flops=pairs * 4 * CB * RB * feature_count,
            bytes_accessed=pairs * RB * (feature_count + CB) * 2,
            transcendentals=0,
        ),
        name="moments",
    )(order, starts, *[in_vmem(r) for r in rows], *[in_vmem(r) for r in resp])


CHUNK = 80


def each_chunk(rows, step):
    whole = rows // CHUNK

    @pl.loop(0, whole)
    def _(i):
        step(pl.ds(pl.multiple_of(i * CHUNK, 16), CHUNK))

    if rows % CHUNK:
        step(slice(whole * CHUNK, rows))


def copy_body(places, skip, *refs):
    sources, target, sems = refs[skip:-2], refs[-2], refs[-1]
    copies = [
        pltpu.make_async_copy(source.at[0], target.at[index], sems.at[j])
        for j, (index, source) in enumerate(zip(places, sources))
    ]
    for copy in copies:
        copy.start()
    for copy in copies:
        copy.wait()


def stacked(total, places, shards, *earlier):
    vmem = pl.BlockSpec(memory_space=pltpu.VMEM)
    anywhere = pl.BlockSpec(memory_space=pl.ANY)
    return pl.pallas_call(
        functools.partial(copy_body, places, len(earlier)),
        in_specs=[vmem] * len(earlier) + [anywhere] * len(shards),
        out_specs=vmem,
        out_shape=pltpu.VMEM((total,) + shards[0].shape[1:], jnp.bfloat16),
        scratch_shapes=[pltpu.SemaphoreType.DMA((len(shards),))],
        input_output_aliases={0: 0} if earlier else {},
        compiler_params=pltpu.CompilerParams(vmem_limit_bytes=VMEM_LIMIT),
        name="stack_shards",
    )(*[in_vmem(e) for e in earlier], *shards)


def add_body(*refs):
    def step(here):
        terms = [ref[here, :].astype(jnp.float32) for ref in refs[:-1]]
        refs[-1][here, :] = functools.reduce(jnp.add, terms).astype(jnp.bfloat16)

    each_chunk(refs[-1].shape[0], step)


def join_body(*refs):
    start = 0
    for ref in refs[:-1]:
        refs[-1][start : start + ref.shape[0], :] = ref[...]
        start += ref.shape[0]


def small_step(body, shape, dtype, name, *operands):
    vmem = pl.BlockSpec(memory_space=pltpu.VMEM)
    return pl.pallas_call(
        body,
        in_specs=[vmem] * len(operands),
        out_specs=vmem,
        out_shape=pltpu.VMEM(shape, dtype),
        compiler_params=pltpu.CompilerParams(vmem_limit_bytes=VMEM_LIMIT),
        cost_estimate=pl.CostEstimate(
            flops=math.prod(shape), bytes_accessed=2 * math.prod(shape), transcendentals=0
        ),
        name=name,
    )(*[in_vmem(value) for value in operands])


def added(*terms):
    return small_step(add_body, terms[0].shape, jnp.bfloat16, "add_sums", *terms)


def joined(*norms):
    shape = (sum(n.shape[0] for n in norms), RB)
    return small_step(join_body, shape, jnp.float32, "join_norms", *norms)


def result_body(
    held,
    end_ref,
    own_norm,
    end_norm,
    end_sum,
    own_sum,
    moved_sum,
    count_ref,
    first_ref,
    second_ref,
    loglik_ref,
    main,
    more,
    staging,
    main_sems,
    more_sems,
    out_sems,
):
    is_end = end_ref[0] > 0
    owned = held * CB
    feature_count = main.shape[1]
    pieces = [(j * CB, CB) for j in range(2 * held)] + [(2 * owned, META)]

    def copy_in(source, target, sems, j):
        here = pl.ds(*pieces[j])
        return pltpu.make_async_copy(source.at[here, :], target.at[here, :], sems.at[j])

    @pl.when(is_end)
    def _():
        for j in range(len(pieces)):
            copy_in(end_sum, main, main_sems, j).start()

    @pl.when(jnp.logical_not(is_end))
    def _():
        for j in range(len(pieces)):
            copy_in(moved_sum, main, main_sems, j).start()
            copy_in(own_sum, more, more_sems, j).start()

    norm = jnp.where(is_end, end_norm[...], own_norm[...])
    loglik_ref[...] = norm * (1.0 / feature_count)
    outward = []
    for j, (start, length) in enumerate(pieces):
        copy_in(end_sum, main, main_sems, j).wait()

        @pl.when(jnp.logical_not(is_end))
        def _(j=j):
            copy_in(own_sum, more, more_sems, j).wait()

        here = slice(start, start + length)
        value = main[here, :].astype(jnp.float32)
        value = jnp.where(is_end, value, value + more[here, :].astype(jnp.float32))
        if start == 2 * owned:
            count_ref[...] = value[0:1, :owned]
            break
        if j >= 2:
            outward[j - 2].wait()
        staging[j % 2] = value
        target = first_ref if start < owned else second_ref
        rows = pl.ds(start % owned, CB)
        outward.append(
            pltpu.make_async_copy(staging.at[j % 2], target.at[rows, :], out_sems.at[j % 2])
        )
        outward[-1].start()
    for copy in outward[-2:]:
        copy.wait()


def results_of(held, is_end, own_norm, end_norm, end_sum, own_sum, moved_sum):
    rows, feature_count = end_sum.shape
    owned = held * CB
    vmem = pl.BlockSpec(memory_space=pltpu.VMEM)
    anywhere = pl.BlockSpec(memory_space=pl.ANY)
    pieces = 2 * held + 1
    moments_shape = jax.ShapeDtypeStruct((owned, feature_count), jnp.float32)
    return pl.pallas_call(
        functools.partial(result_body, held),
        in_specs=[pl.BlockSpec(memory_space=pltpu.SMEM), vmem, vmem] + [anywhere] * 3,
        out_specs=[vmem, anywhere, anywhere, vmem],
        out_shape=[
            jax.ShapeDtypeStruct((1, owned), jnp.float32),
            moments_shape,
            moments_shape,
            jax.ShapeDtypeStruct(own_norm.shape, jnp.float32),
        ],
        scratch_shapes=[
            pltpu.VMEM((rows, feature_count), jnp.bfloat16),
            pltpu.VMEM((rows, feature_count), jnp.bfloat16),
            pltpu.VMEM((2, CB, feature_count), jnp.float32),
            pltpu.SemaphoreType.DMA((pieces,)),
            pltpu.SemaphoreType.DMA((pieces,)),
            pltpu.SemaphoreType.DMA((2,)),
        ],
        compiler_params=pltpu.CompilerParams(vmem_limit_bytes=VMEM_LIMIT),
        name="results",
    )(is_end.astype(jnp.int32).reshape(1), own_norm, end_norm, end_sum, own_sum, moved_sum)


def plain_plan(points, candidates, parameters, held):
    weights = parameter_shard(*parameters)
    dp_size = lax.axis_size("dp")
    row_blocks = points.shape[0] // RB
    pos, order, starts = pair_lists(
        [candidates.T],
        (row_blocks,),
        held,
        dp_size * held,
        lax.axis_size("comp"),
        lambda holder: holder,
        [],
    )
    all_weights = lax.all_gather(weights, "dp", axis=0, tiled=True)
    resp, norm = responsibilities(points, pos, 0, all_weights, held)
    sums = []
    for j in range(dp_size):
        sums += moments([points], [resp], order, starts, held, [j])
    total = lax.psum_scatter(jnp.concatenate(sums), "dp", scatter_dimension=0, tiled=True)
    total = total.astype(jnp.float32)
    owned = held * CB
    counts, first, second = total[2 * owned, :owned], total[:owned], total[owned : 2 * owned]
    return counts, first, second, norm.reshape(-1) / points.shape[1]


def line_pairs(links):
    return [(2 * a + c, 2 * b + c) for a, b in links for c in (0, 1)]


INWARD = line_pairs(((0, 1), (3, 2)))
OUTWARD = line_pairs(((1, 0), (2, 3)))
MIDDLE = line_pairs(((1, 2), (2, 1)))
CORES = [(2, 3), (3, 2), (4, 5), (5, 4)]


def move(value, pairs):
    return lax.ppermute(value, "dp", pairs)


def after(value, *others):
    return lax.optimization_barrier((value,) + others)[0]


def line_place(holder, chip, core):
    z, other = lax.div(holder, 2), lax.rem(holder, 2)
    z = jnp.where(chip < 2, z, 3 - z)
    z = jnp.where(z == 0, 1, jnp.where(z == 1, 0, z))
    return z * 2 + lax.rem(other + core, 2)


def line_plan(points, candidates, parameters, held):
    index = lax.axis_index("dp")
    chip, core = index // 2, index % 2
    where = [chip.reshape(1), core.reshape(1)]
    row_blocks = points.shape[0] // RB
    small = row_blocks // 8
    cuts = (0, 1, 2 + 4 * small, row_blocks - small, row_blocks)
    runs = (row_blocks,) + tuple(b - a for a, b in zip(cuts[:-1], cuts[1:]))
    own_ids = candidates.T
    end_ids = move(own_ids, INWARD)
    before = move(points[: cuts[1] * RB], INWARD)
    weights = parameter_shard(*parameters)
    weights_then, end_ids, before = lax.optimization_barrier((weights, end_ids, before))

    outer = move(weights_then, INWARD)
    across = move(weights, MIDDLE)
    pieces = cut_rows(after(points, weights_then), [cut * RB for cut in cuts[1:]])
    own_shared = move(after(weights, *pieces), CORES)
    most = move(after(pieces[0], outer), INWARD)
    far = move(outer, MIDDLE)
    moved = [before, most] + [move(after(piece, far), INWARD) for piece in pieces[1:]]
    pos, order, starts = pair_lists(
        [own_ids, end_ids], runs, held, 8 * held, lax.axis_size("comp"), line_place, where
    )
    near = [after(weights, pos, order, starts), own_shared, outer, across]
    near_weights = stacked(8, (0, 1, 2, 4), near)
    far, near_weights = lax.optimization_barrier((far, near_weights))
    shared = [move(w, CORES) for w in (outer, across, far)]
    all_weights = stacked(8, (6, 3, 5, 7), [after(far, most)] + shared, near_weights)

    rows = [points] + moved
    results = []
    for j, run_rows in enumerate(rows):
        if results:
            pos = after(pos, results[-1][1])
        results.append(responsibilities(run_rows, pos, sum(runs[:j]), all_weights, held))
    resp = [r[0] for r in results]

    def sums_of(position, *earlier):
        return moments(rows, resp, after(order, *earlier), starts, held, [position])[0]

    far_other = sums_of(7)
    far_received = move(far_other, CORES)
    far_own = sums_of(6, far_other)
    far_part = added(far_own, far_received)
    far_sum = move(far_part, MIDDLE)
    across_other = sums_of(5, far_part)
    end_norm = move(after(joined(*[r[1] for r in results[1:]]), across_other), OUTWARD)
    across_received = move(across_other, CORES)
    across_own = sums_of(4, across_other)
    across_part = added(across_own, across_received)
    across_sum = move(across_part, MIDDLE)
    outer_other = sums_of(3, across_part)
    outer_received = move(outer_other, CORES)
    own_other = sums_of(1, outer_other)
    own_received = move(own_other, CORES)
    outer_own = sums_of(2, own_other, end_norm)
    own_own = sums_of(0, outer_own)
    outer_sum = added(outer_own, outer_received, far_sum)
    end_sum = move(outer_sum, OUTWARD)
    is_end = jnp.logical_or(chip == 0, chip == 3)
    own_sum = added(own_own, own_received)
    counts, first, second, loglik = results_of(
        held, is_end, results[0][1], end_norm, end_sum, own_sum, across_sum
    )
    return counts.reshape(-1), first, second, loglik.reshape(-1)


def on_device(points, candidates, means, inv_var, log_weight):
    held = means.shape[0] // CB
    plan = line_plan if lax.axis_size("dp") == 8 else plain_plan
    return plan(points, candidates, (means, inv_var, log_weight), held)


def solution(mesh):
    return jax.shard_map(
        on_device,
        mesh=mesh,
        in_specs=(
            P(("dp", "comp"), None),
            P(("dp", "comp"), None),
            P(("dp", "comp"), None),
            P(("dp", "comp"), None),
            P(("dp", "comp")),
        ),
        out_specs=(
            P(("dp", "comp")),
            P(("dp", "comp"), None),
            P(("dp", "comp"), None),
            P(("dp", "comp")),
        ),
        check_vma=False,
    )
```

```python
import functools
import math

import jax
import jax.numpy as jnp
from jax import lax
from jax.experimental import pallas as pl
from jax.experimental.pallas import tpu as pltpu
from jax.sharding import PartitionSpec as P

CB = 128
RB = 128
CANDS = 4
META = 16
VMEM_LIMIT = 8 * 1024 * 1024
NT = (((1,), (1,)), ((), ()))
TN = (((0,), (0,)), ((), ()))


def in_vmem(value):
    return pltpu.with_memory_space_constraint(value, pltpu.VMEM)


def in_hbm(value):
    return pltpu.with_memory_space_constraint(value, pltpu.HBM)


def shard_body(means_hbm, inv_hbm, log_ref, out_ref, means_ref, inv_ref, sems):
    copies = [
        pltpu.make_async_copy(means_hbm, means_ref, sems.at[0]),
        pltpu.make_async_copy(inv_hbm, inv_ref, sems.at[1]),
    ]
    for copy in copies:
        copy.start()
    owned, feature_count = means_ref.shape
    ones = jnp.ones((META, feature_count), jnp.float32)
    row = lax.broadcasted_iota(jnp.int32, (META, CB), 0)
    for copy in copies:
        copy.wait()
    for half in range(2):
        out_ref[0, half, owned:, :] = jnp.zeros((META, feature_count), jnp.bfloat16)
    for block in range(owned // CB):
        here = slice(block * CB, (block + 1) * CB)
        inverse = inv_ref[here, :]
        mean_f = means_ref[here, :].astype(jnp.float32)
        inv_f = inverse.astype(jnp.float32)
        scaled = inv_f * mean_f
        out_ref[0, 0, here, :] = scaled.astype(jnp.bfloat16)
        out_ref[0, 1, here, :] = inverse
        terms = 0.5 * jnp.log(inv_f) - 0.5 * (scaled * mean_f)
        rest = lax.dot_general(
            ones, terms, NT, precision=lax.Precision.HIGHEST, preferred_element_type=jnp.float32
        )
        rest += log_ref[:, here].astype(jnp.float32)
        rest -= 0.5 * feature_count * math.log(2.0 * math.pi)
        high = rest.astype(jnp.bfloat16).astype(jnp.float32)
        rest -= high
        middle = rest.astype(jnp.bfloat16).astype(jnp.float32)
        low = rest - middle
        pieces = jnp.where(row == 0, high, jnp.where(row == 1, middle, low))
        out_ref[0, 0, owned:, here] = pieces.astype(jnp.bfloat16)


def parameter_shard(means, inv_var, log_weight):
    owned, feature_count = means.shape
    vmem = pl.BlockSpec(memory_space=pltpu.VMEM)
    hbm = pl.BlockSpec(memory_space=pltpu.HBM)
    return pl.pallas_call(
        shard_body,
        in_specs=[hbm, hbm, vmem],
        out_specs=vmem,
        out_shape=pltpu.VMEM((1, 2, owned + META, feature_count), jnp.bfloat16),
        scratch_shapes=[
            pltpu.VMEM((owned, feature_count), means.dtype),
            pltpu.VMEM((owned, feature_count), inv_var.dtype),
            pltpu.SemaphoreType.DMA((2,)),
        ],
        compiler_params=pltpu.CompilerParams(vmem_limit_bytes=VMEM_LIMIT),
        cost_estimate=pl.CostEstimate(
            flops=owned * feature_count * 40,
            bytes_accessed=owned * feature_count * 8,
            transcendentals=owned * feature_count,
        ),
        name="parameter_shard",
    )(in_hbm(means), in_hbm(inv_var), log_weight.reshape(1, owned))


def cut_body(cuts, points_ref, *refs):
    piece_refs, (staging, sems) = refs[:-2], refs[-2:]
    ways = []
    for j, piece in enumerate(piece_refs):
        here = pl.ds(cuts[j], piece.shape[0])
        there = pl.ds(cuts[j] - cuts[0], piece.shape[0])
        ways.append(
            (
                pltpu.make_async_copy(points_ref.at[here, :], staging.at[there, :], sems.at[0, j]),
                pltpu.make_async_copy(staging.at[there, :], piece, sems.at[1, j]),
            )
        )
    for inward, _ in ways:
        inward.start()
    for inward, outward in ways:
        inward.wait()
        outward.start()
    for _, outward in ways:
        outward.wait()


def cut_rows(points, cuts):
    feature_count = points.shape[1]
    hbm = pl.BlockSpec(memory_space=pltpu.HBM)
    lengths = [b - a for a, b in zip(cuts[:-1], cuts[1:])]
    return pl.pallas_call(
        functools.partial(cut_body, cuts),
        in_specs=[hbm],
        out_specs=[hbm] * len(lengths),
        out_shape=[pltpu.HBM((length, feature_count), points.dtype) for length in lengths],
        scratch_shapes=[
            pltpu.VMEM((sum(lengths), feature_count), points.dtype),
            pltpu.SemaphoreType.DMA((2, len(lengths))),
        ],
        compiler_params=pltpu.CompilerParams(vmem_limit_bytes=VMEM_LIMIT),
        name="cut_rows",
    )(in_hbm(points))


def density_body(first, count, held, pos_ref, x_ref, weight_ref, resp_ref, norm_ref):
    owned = held * CB
    row_index = lax.broadcasted_iota(jnp.int32, (META, RB), 0)
    pieces = jnp.where(row_index < 3, 1.0, 0.0).astype(jnp.bfloat16)

    @pl.loop(0, count)
    def _(i):
        x = x_ref[pl.ds(pl.multiple_of(i * RB, RB), RB), :]
        half = x * x * -0.5
        chosen = []
        for slot in range(CANDS):
            pos = pos_ref[(first + i) * CANDS + slot]
            start = pl.multiple_of(lax.rem(pos, held) * CB, CB)
            chosen.append((lax.div(pos, held), pl.ds(start, CB)))
        scaled = jnp.concatenate([weight_ref[shard, 0, here, :] for shard, here in chosen])
        inverse = jnp.concatenate([weight_ref[shard, 1, here, :] for shard, here in chosen])
        constants = jnp.concatenate(
            [weight_ref[shard, 0, owned:, here] for shard, here in chosen], axis=1
        )
        densities = lax.dot_general(scaled, x, NT, preferred_element_type=jnp.float32)
        densities += lax.dot_general(inverse, half, NT, preferred_element_type=jnp.float32)
        densities += lax.dot_general(constants, pieces, TN, preferred_element_type=jnp.float32)
        peak = jnp.max(densities, axis=0, keepdims=True)
        terms = jnp.exp(densities - peak)
        total = jnp.sum(terms, axis=0, keepdims=True)
        norm_ref[pl.ds(i, 1), :] = peak + jnp.log(total)
        resp = (terms * (1.0 / total)).astype(jnp.bfloat16)
        for slot in range(CANDS):
            resp_ref[i, slot] = resp[slot * CB : (slot + 1) * CB]


def is_one_of(shard, shards):
    return functools.reduce(jnp.logical_or, [shard == j for j in shards])


def slot_density(weight_ref, pos, held, x, half, pieces):
    owned = held * CB
    shard = lax.div(pos, held)
    here = pl.ds(pl.multiple_of(lax.rem(pos, held) * CB, CB), CB)
    linear = lax.dot_general(
        weight_ref[shard, 0, here, :], x, NT, preferred_element_type=jnp.float32
    )
    quadratic = lax.dot_general(
        weight_ref[shard, 1, here, :], half, NT, preferred_element_type=jnp.float32
    )
    constant = lax.dot_general(
        weight_ref[shard, 0, owned:, here], pieces, TN, preferred_element_type=jnp.float32
    )
    return linear + quadratic + constant


def piece_mask():
    row_index = lax.broadcasted_iota(jnp.int32, (META, RB), 0)
    return jnp.where(row_index < 3, 1.0, 0.0).astype(jnp.bfloat16)


def early_body(count, held, near, pos_ref, x_ref, weight_ref, density_ref):
    pieces = piece_mask()

    @pl.loop(0, count)
    def _(i):
        x = x_ref[pl.ds(pl.multiple_of(i * RB, RB), RB), :]
        half = x * x * -0.5
        for slot in range(CANDS):
            pos = pos_ref[i * CANDS + slot]

            @pl.when(is_one_of(lax.div(pos, held), near))
            def _(pos=pos, slot=slot):
                density_ref[i, slot] = slot_density(weight_ref, pos, held, x, half, pieces)


def late_body(count, held, near, pos_ref, x_ref, weight_ref, _, density_ref, resp_ref, norm_ref):
    pieces = piece_mask()

    @pl.loop(0, count)
    def _(i):
        x = x_ref[pl.ds(pl.multiple_of(i * RB, RB), RB), :]
        half = x * x * -0.5
        for slot in range(CANDS):
            pos = pos_ref[i * CANDS + slot]

            @pl.when(jnp.logical_not(is_one_of(lax.div(pos, held), near)))
            def _(pos=pos, slot=slot):
                density_ref[i, slot] = slot_density(weight_ref, pos, held, x, half, pieces)

        densities = [density_ref[i, slot] for slot in range(CANDS)]
        peak = functools.reduce(
            jnp.maximum, [jnp.max(d, axis=0, keepdims=True) for d in densities]
        )
        terms = [jnp.exp(d - peak) for d in densities]
        total = functools.reduce(jnp.add, [jnp.sum(t, axis=0, keepdims=True) for t in terms])
        norm_ref[pl.ds(i, 1), :] = peak + jnp.log(total)
        inverse_total = 1.0 / total
        for slot in range(CANDS):
            resp_ref[i, slot] = (terms[slot] * inverse_total).astype(jnp.bfloat16)


def early_densities(rows, pos, weights, held, near):
    count = rows.shape[0] // RB
    vmem = pl.BlockSpec(memory_space=pltpu.VMEM)
    return pl.pallas_call(
        functools.partial(early_body, count, held, near),
        in_specs=[pl.BlockSpec(memory_space=pltpu.SMEM), vmem, vmem],
        out_specs=vmem,
        out_shape=pltpu.VMEM((count, CANDS, CB, RB), jnp.float32),
        compiler_params=pltpu.CompilerParams(vmem_limit_bytes=VMEM_LIMIT),
        name="early_densities",
    )(pos, in_vmem(rows), in_vmem(weights))


def late_responsibilities(rows, pos, weights, held, near, densities):
    count = rows.shape[0] // RB
    vmem = pl.BlockSpec(memory_space=pltpu.VMEM)
    outs = pl.pallas_call(
        functools.partial(late_body, count, held, near),
        in_specs=[pl.BlockSpec(memory_space=pltpu.SMEM), vmem, vmem, vmem],
        out_specs=[vmem] * 3,
        out_shape=[
            pltpu.VMEM(densities.shape, jnp.float32),
            pltpu.VMEM((count, CANDS, CB, RB), jnp.bfloat16),
            pltpu.VMEM((count, RB), jnp.float32),
        ],
        input_output_aliases={3: 0},
        compiler_params=pltpu.CompilerParams(vmem_limit_bytes=VMEM_LIMIT),
        name="late_responsibilities",
    )(pos, in_vmem(rows), in_vmem(weights), in_vmem(densities))
    return outs[1:]


def responsibilities(rows, pos, first, weights, held):
    count = rows.shape[0] // RB
    feature_count = rows.shape[1]
    vmem = pl.BlockSpec(memory_space=pltpu.VMEM)
    pairs = count * CANDS
    return pl.pallas_call(
        functools.partial(density_body, first, count, held),
        in_specs=[pl.BlockSpec(memory_space=pltpu.SMEM), vmem, vmem],
        out_specs=[vmem, vmem],
        out_shape=[
            pltpu.VMEM((count, CANDS, CB, RB), jnp.bfloat16),
            pltpu.VMEM((count, RB), jnp.float32),
        ],
        compiler_params=pltpu.CompilerParams(vmem_limit_bytes=VMEM_LIMIT),
        cost_estimate=pl.CostEstimate(
            flops=pairs * 4 * CB * RB * feature_count,
            bytes_accessed=pairs * CB * feature_count * 4 + rows.size * 2,
            transcendentals=pairs * CB * RB,
        ),
        name="responsibilities",
    )(pos, in_vmem(rows), in_vmem(weights))


def list_body(runs, held, owners, place, known, *rest):
    where = [ref[0] for ref in rest[:known]]
    id_refs, (pos_ref, order_ref, start_ref, cursor) = rest[known:-4], rest[-4:]
    bins = start_ref.shape[0]
    number_of_runs = len(runs)
    per_ref = sum(runs) // len(id_refs)
    firsts = [sum(runs[:j]) for j in range(number_of_runs)]

    def run_of(i):
        return sum((i >= start).astype(jnp.int32) for start in firsts[1:]) if firsts[1:] else 0

    @pl.loop(0, bins)
    def _(j):
        start_ref[j] = 0

    for part, id_ref in enumerate(id_refs):

        @pl.loop(0, per_ref)
        def _(row, part=part, id_ref=id_ref):
            i = part * per_ref + row
            for slot in range(CANDS):
                block = id_ref[slot, row]
                holder = place(lax.div(block, owners * held), *where)
                pos = holder * held + lax.rem(block, held)
                pos_ref[i * CANDS + slot] = pos
                key = pos * number_of_runs + run_of(i) + 1
                start_ref[key] = start_ref[key] + 1

    def prefix(j, total):
        total = total + start_ref[j]
        start_ref[j] = total
        cursor[j] = total
        return total

    lax.fori_loop(0, bins, prefix, jnp.int32(0))

    @pl.loop(0, sum(runs))
    def _(i):
        for slot in range(CANDS):
            key = pos_ref[i * CANDS + slot] * number_of_runs + run_of(i)
            order_ref[cursor[key]] = i * CANDS + slot
            cursor[key] = cursor[key] + 1


def pair_lists(candidates, runs, held, group_blocks, owners, place, where):
    smem = pl.BlockSpec(memory_space=pltpu.SMEM)
    pairs = sum(runs) * CANDS
    bins = group_blocks * len(runs) + 1
    return pl.pallas_call(
        functools.partial(list_body, tuple(runs), held, owners, place, len(where)),
        in_specs=[smem] * (len(where) + len(candidates)),
        out_specs=[smem] * 3,
        out_shape=[jax.ShapeDtypeStruct((n,), jnp.int32) for n in (pairs, pairs, bins)],
        scratch_shapes=[pltpu.SMEM((bins,), jnp.int32)],
        compiler_params=pltpu.CompilerParams(vmem_limit_bytes=VMEM_LIMIT),
        name="pair_lists",
    )(*where, *candidates)


def moment_body(shards, held, runs, order_ref, start_ref, *rest):
    parts, outs = len(runs), len(shards)
    row_refs, resp_refs = rest[:parts], rest[parts : 2 * parts]
    out_refs = rest[2 * parts : 2 * parts + outs]
    sums, count_sum = rest[2 * parts + outs :]
    owned = held * CB
    meta = slice(2 * owned, 2 * owned + META)
    ones = jnp.ones((META, 2 * RB), jnp.bfloat16)

    def block_sums(pos):
        sums[...] = jnp.zeros_like(sums)
        count_sum[...] = jnp.zeros_like(count_sum)
        base = 0
        for run in range(parts):
            entry = pos * parts + run
            low, high = start_ref[entry], start_ref[entry + 1]

            @pl.loop(0, lax.div(high - low + 1, 2))
            def _(step, base=base, run=run, low=low, high=high):
                one = low + 2 * step
                two = jnp.minimum(one + 1, high - 1)
                valid = (one + 1 < high).astype(jnp.float32)
                pair_a, pair_b = order_ref[one] - base, order_ref[two] - base
                row_a, row_b = lax.div(pair_a, CANDS), lax.div(pair_b, CANDS)
                weight_a = resp_refs[run][row_a, lax.rem(pair_a, CANDS)]
                weight_b = resp_refs[run][row_b, lax.rem(pair_b, CANDS)]
                weight_b = (weight_b.astype(jnp.float32) * valid).astype(jnp.bfloat16)
                weight = jnp.concatenate([weight_a, weight_b], axis=1)
                x = jnp.concatenate(
                    [
                        row_refs[run][pl.ds(pl.multiple_of(row_a * RB, RB), RB), :],
                        row_refs[run][pl.ds(pl.multiple_of(row_b * RB, RB), RB), :],
                    ],
                    axis=0,
                )
                sums[0] += jnp.dot(weight, x, preferred_element_type=jnp.float32)
                sums[1] += jnp.dot(weight, x * x, preferred_element_type=jnp.float32)
                count_sum[...] += lax.dot_general(
                    ones, weight, NT, preferred_element_type=jnp.float32
                )

            base += runs[run] * CANDS

    for shard, out_ref in zip(shards, out_refs):
        out_ref[meta, :] = jnp.zeros((META, out_ref.shape[1]), jnp.bfloat16)

        @pl.loop(0, held)
        def _(block, shard=shard, out_ref=out_ref):
            block_sums(shard * held + block)
            start = pl.multiple_of(block * CB, CB)
            out_ref[pl.ds(start, CB), :] = sums[0].astype(jnp.bfloat16)
            out_ref[pl.ds(owned + start, CB), :] = sums[1].astype(jnp.bfloat16)
            out_ref[meta, pl.ds(start, CB)] = count_sum[...].astype(jnp.bfloat16)


def moments(rows, resp, order, starts, held, shards):
    runs = tuple(r.shape[0] // RB for r in rows)
    feature_count = rows[0].shape[1]
    smem = pl.BlockSpec(memory_space=pltpu.SMEM)
    vmem = pl.BlockSpec(memory_space=pltpu.VMEM)
    pairs = sum(runs) * held * len(shards) // 8
    out_shape = pltpu.VMEM((2 * held * CB + META, feature_count), jnp.bfloat16)
    return pl.pallas_call(
        functools.partial(moment_body, tuple(shards), held, runs),
        in_specs=[smem, smem] + [vmem] * (2 * len(runs)),
        out_specs=[vmem] * len(shards),
        out_shape=[out_shape] * len(shards),
        scratch_shapes=[
            pltpu.VMEM((2, CB, feature_count), jnp.float32),
            pltpu.VMEM((META, CB), jnp.float32),
        ],
        compiler_params=pltpu.CompilerParams(vmem_limit_bytes=VMEM_LIMIT),
        cost_estimate=pl.CostEstimate(
            flops=pairs * 4 * CB * RB * feature_count,
            bytes_accessed=pairs * RB * (feature_count + CB) * 2,
            transcendentals=0,
        ),
        name="moments",
    )(order, starts, *[in_vmem(r) for r in rows], *[in_vmem(r) for r in resp])


CHUNK = 80


def each_chunk(rows, step):
    whole = rows // CHUNK

    @pl.loop(0, whole)
    def _(i):
        step(pl.ds(pl.multiple_of(i * CHUNK, 16), CHUNK))

    if rows % CHUNK:
        step(slice(whole * CHUNK, rows))


def copy_body(places, skip, *refs):
    sources, target, sems = refs[skip:-2], refs[-2], refs[-1]
    copies = [
        pltpu.make_async_copy(source.at[0], target.at[index], sems.at[j])
        for j, (index, source) in enumerate(zip(places, sources))
    ]
    for copy in copies:
        copy.start()
    for copy in copies:
        copy.wait()


def stacked(total, places, shards, *earlier):
    vmem = pl.BlockSpec(memory_space=pltpu.VMEM)
    anywhere = pl.BlockSpec(memory_space=pl.ANY)
    return pl.pallas_call(
        functools.partial(copy_body, places, len(earlier)),
        in_specs=[vmem] * len(earlier) + [anywhere] * len(shards),
        out_specs=vmem,
        out_shape=pltpu.VMEM((total,) + shards[0].shape[1:], jnp.bfloat16),
        scratch_shapes=[pltpu.SemaphoreType.DMA((len(shards),))],
        input_output_aliases={0: 0} if earlier else {},
        compiler_params=pltpu.CompilerParams(vmem_limit_bytes=VMEM_LIMIT),
        name="stack_shards",
    )(*[in_vmem(e) for e in earlier], *shards)


def add_body(*refs):
    def step(here):
        terms = [ref[here, :].astype(jnp.float32) for ref in refs[:-1]]
        refs[-1][here, :] = functools.reduce(jnp.add, terms).astype(jnp.bfloat16)

    each_chunk(refs[-1].shape[0], step)


def join_body(*refs):
    start = 0
    for ref in refs[:-1]:
        refs[-1][start : start + ref.shape[0], :] = ref[...]
        start += ref.shape[0]


def small_step(body, shape, dtype, name, *operands):
    vmem = pl.BlockSpec(memory_space=pltpu.VMEM)
    return pl.pallas_call(
        body,
        in_specs=[vmem] * len(operands),
        out_specs=vmem,
        out_shape=pltpu.VMEM(shape, dtype),
        compiler_params=pltpu.CompilerParams(vmem_limit_bytes=VMEM_LIMIT),
        cost_estimate=pl.CostEstimate(
            flops=math.prod(shape), bytes_accessed=2 * math.prod(shape), transcendentals=0
        ),
        name=name,
    )(*[in_vmem(value) for value in operands])


def added(*terms):
    return small_step(add_body, terms[0].shape, jnp.bfloat16, "add_sums", *terms)


def joined(*norms):
    shape = (sum(n.shape[0] for n in norms), RB)
    return small_step(join_body, shape, jnp.float32, "join_norms", *norms)


def result_body(owned, end_ref, *refs):
    own_norm, end_norm, end_sum = refs[:3]
    terms, (count_ref, first_ref, second_ref, loglik_ref) = refs[3:-4], refs[-4:]
    is_end = end_ref[0] > 0
    block = pl.program_id(0)
    feature_count = first_ref.shape[1]

    def total(rows):
        inner = functools.reduce(jnp.add, [t[rows, :].astype(jnp.float32) for t in terms])
        return jnp.where(is_end, end_sum[rows, :].astype(jnp.float32), inner)

    start = pl.multiple_of(block * CB, CB)
    first_ref[...] = total(pl.ds(start, CB))
    second_ref[...] = total(pl.ds(owned + start, CB))
    count_ref[...] = total(slice(2 * owned, 2 * owned + META))[0:1, :owned]
    norm = jnp.where(is_end, end_norm[...], own_norm[...])
    loglik_ref[...] = norm * (1.0 / feature_count)


def results_of(is_end, own_norm, end_norm, end_sum, *terms):
    rows, feature_count = end_sum.shape
    owned = (rows - META) // 2
    vmem = pl.BlockSpec(memory_space=pltpu.VMEM)
    operands = (own_norm, end_norm, end_sum) + terms
    return pl.pallas_call(
        functools.partial(result_body, owned),
        grid=(owned // CB,),
        in_specs=[pl.BlockSpec(memory_space=pltpu.SMEM)] + [vmem] * len(operands),
        out_specs=[
            pl.BlockSpec((1, owned), lambda i: (0, 0)),
            pl.BlockSpec((CB, feature_count), lambda i: (i, 0)),
            pl.BlockSpec((CB, feature_count), lambda i: (i, 0)),
            pl.BlockSpec(own_norm.shape, lambda i: (0, 0)),
        ],
        out_shape=[
            jax.ShapeDtypeStruct((1, owned), jnp.float32),
            jax.ShapeDtypeStruct((owned, feature_count), jnp.float32),
            jax.ShapeDtypeStruct((owned, feature_count), jnp.float32),
            jax.ShapeDtypeStruct(own_norm.shape, jnp.float32),
        ],
        compiler_params=pltpu.CompilerParams(vmem_limit_bytes=VMEM_LIMIT),
        name="results",
    )(is_end.astype(jnp.int32).reshape(1), *[in_vmem(value) for value in operands])


def plain_plan(points, candidates, parameters, held):
    weights = parameter_shard(*parameters)
    dp_size = lax.axis_size("dp")
    row_blocks = points.shape[0] // RB
    pos, order, starts = pair_lists(
        [candidates.T],
        (row_blocks,),
        held,
        dp_size * held,
        lax.axis_size("comp"),
        lambda holder: holder,
        [],
    )
    all_weights = lax.all_gather(weights, "dp", axis=0, tiled=True)
    resp, norm = responsibilities(points, pos, 0, all_weights, held)
    sums = []
    for j in range(dp_size):
        sums += moments([points], [resp], order, starts, held, [j])
    total = lax.psum_scatter(jnp.concatenate(sums), "dp", scatter_dimension=0, tiled=True)
    total = total.astype(jnp.float32)
    owned = held * CB
    counts, first, second = total[2 * owned, :owned], total[:owned], total[owned : 2 * owned]
    return counts, first, second, norm.reshape(-1) / points.shape[1]


def line_pairs(links):
    return [(2 * a + c, 2 * b + c) for a, b in links for c in (0, 1)]


INWARD = line_pairs(((0, 1), (3, 2)))
OUTWARD = line_pairs(((1, 0), (2, 3)))
MIDDLE = line_pairs(((1, 2), (2, 1)))
CORES = [(2, 3), (3, 2), (4, 5), (5, 4)]


def move(value, pairs):
    return lax.ppermute(value, "dp", pairs)


def after(value, *others):
    return lax.optimization_barrier((value,) + others)[0]


def line_place(holder, chip, core):
    z, other = lax.div(holder, 2), lax.rem(holder, 2)
    z = jnp.where(chip < 2, z, 3 - z)
    z = jnp.where(z == 0, 1, jnp.where(z == 1, 0, z))
    return z * 2 + lax.rem(other + core, 2)


def line_plan(points, candidates, parameters, held):
    index = lax.axis_index("dp")
    chip, core = index // 2, index % 2
    where = [chip.reshape(1), core.reshape(1)]
    row_blocks = points.shape[0] // RB
    small = row_blocks // 8
    cuts = (0, 1, 2 + 4 * small, row_blocks - small, row_blocks)
    runs = (row_blocks,) + tuple(b - a for a, b in zip(cuts[:-1], cuts[1:]))
    own_ids = candidates.T
    end_ids = move(own_ids, INWARD)
    before = move(points[: cuts[1] * RB], INWARD)
    weights = parameter_shard(*parameters)
    weights_then, end_ids, before = lax.optimization_barrier((weights, end_ids, before))

    outer = move(weights_then, INWARD)
    across = move(weights, MIDDLE)
    pieces = cut_rows(after(points, weights_then), [cut * RB for cut in cuts[1:]])
    own_shared = move(after(weights, *pieces), CORES)
    most = move(after(pieces[0], outer), INWARD)
    far = move(outer, MIDDLE)
    moved = [before, most] + [move(after(piece, far), INWARD) for piece in pieces[1:]]
    pos, order, starts = pair_lists(
        [own_ids, end_ids], runs, held, 8 * held, lax.axis_size("comp"), line_place, where
    )
    near = [after(weights, pos, order, starts), own_shared, outer, across]
    near_weights = stacked(8, (0, 1, 2, 4), near)
    near_places = (0, 1, 2, 4)
    densities = early_densities(points, pos, near_weights, held, near_places)
    far, near_weights, densities = lax.optimization_barrier((far, near_weights, densities))
    shared = [move(w, CORES) for w in (outer, across, far)]
    all_weights = stacked(8, (6, 3, 5, 7), [after(far, most)] + shared, near_weights)

    rows = [points] + moved
    results = [late_responsibilities(points, pos, all_weights, held, near_places, densities)]
    for j, run_rows in enumerate(rows[1:], 1):
        pos = after(pos, results[-1][1])
        results.append(responsibilities(run_rows, pos, sum(runs[:j]), all_weights, held))
    resp = [r[0] for r in results]

    def sums_of(position, *earlier):
        return moments(rows, resp, after(order, *earlier), starts, held, [position])[0]

    far_other = sums_of(7)
    far_received = move(far_other, CORES)
    far_own = sums_of(6, far_other)
    far_part = added(far_own, far_received)
    far_sum = move(far_part, MIDDLE)
    across_other = sums_of(5, far_part)
    end_norm = move(after(joined(*[r[1] for r in results[1:]]), across_other), OUTWARD)
    across_received = move(across_other, CORES)
    across_own = sums_of(4, across_other)
    across_part = added(across_own, across_received)
    across_sum = move(across_part, MIDDLE)
    outer_other = sums_of(3, across_part)
    outer_received = move(outer_other, CORES)
    own_other = sums_of(1, outer_other)
    own_received = move(own_other, CORES)
    outer_own = sums_of(2, own_other, end_norm)
    own_own = sums_of(0, outer_own)
    outer_sum = added(added(outer_own, outer_received), far_sum)
    end_sum = move(outer_sum, OUTWARD)
    is_end = jnp.logical_or(chip == 0, chip == 3)
    counts, first, second, loglik = results_of(
        is_end, results[0][1], end_norm, end_sum, added(own_own, own_received), across_sum
    )
    return counts.reshape(-1), first, second, loglik.reshape(-1)


def on_device(points, candidates, means, inv_var, log_weight):
    held = means.shape[0] // CB
    plan = line_plan if lax.axis_size("dp") == 8 else plain_plan
    return plan(points, candidates, (means, inv_var, log_weight), held)


def solution(mesh):
    return jax.shard_map(
        on_device,
        mesh=mesh,
        in_specs=(
            P(("dp", "comp"), None),
            P(("dp", "comp"), None),
            P(("dp", "comp"), None),
            P(("dp", "comp"), None),
            P(("dp", "comp")),
        ),
        out_specs=(
            P(("dp", "comp")),
            P(("dp", "comp"), None),
            P(("dp", "comp"), None),
            P(("dp", "comp")),
        ),
        check_vma=False,
    )
```

```python
import functools
import math

import jax
import jax.numpy as jnp
from jax import lax
from jax.experimental import pallas as pl
from jax.experimental.pallas import tpu as pltpu
from jax.sharding import PartitionSpec as P

CB = 128
RB = 128
CANDS = 4
META = 16
VMEM_LIMIT = 8 * 1024 * 1024
NT = (((1,), (1,)), ((), ()))
TN = (((0,), (0,)), ((), ()))


def in_vmem(value):
    return pltpu.with_memory_space_constraint(value, pltpu.VMEM)


def in_hbm(value):
    return pltpu.with_memory_space_constraint(value, pltpu.HBM)


def shard_body(means_hbm, inv_hbm, log_ref, out_ref, means_ref, inv_ref, sems):
    copies = [
        pltpu.make_async_copy(means_hbm, means_ref, sems.at[0]),
        pltpu.make_async_copy(inv_hbm, inv_ref, sems.at[1]),
    ]
    for copy in copies:
        copy.start()
    owned, feature_count = means_ref.shape
    ones = jnp.ones((META, feature_count), jnp.float32)
    row = lax.broadcasted_iota(jnp.int32, (META, CB), 0)
    for copy in copies:
        copy.wait()
    for half in range(2):
        out_ref[0, half, owned:, :] = jnp.zeros((META, feature_count), jnp.bfloat16)
    for block in range(owned // CB):
        here = slice(block * CB, (block + 1) * CB)
        inverse = inv_ref[here, :]
        mean_f = means_ref[here, :].astype(jnp.float32)
        inv_f = inverse.astype(jnp.float32)
        scaled = inv_f * mean_f
        out_ref[0, 0, here, :] = scaled.astype(jnp.bfloat16)
        out_ref[0, 1, here, :] = inverse
        terms = 0.5 * jnp.log(inv_f) - 0.5 * (scaled * mean_f)
        rest = lax.dot_general(
            ones, terms, NT, precision=lax.Precision.HIGHEST, preferred_element_type=jnp.float32
        )
        rest += log_ref[:, here].astype(jnp.float32)
        rest -= 0.5 * feature_count * math.log(2.0 * math.pi)
        high = rest.astype(jnp.bfloat16).astype(jnp.float32)
        rest -= high
        middle = rest.astype(jnp.bfloat16).astype(jnp.float32)
        low = rest - middle
        pieces = jnp.where(row == 0, high, jnp.where(row == 1, middle, low))
        out_ref[0, 0, owned:, here] = pieces.astype(jnp.bfloat16)


def parameter_shard(means, inv_var, log_weight):
    owned, feature_count = means.shape
    vmem = pl.BlockSpec(memory_space=pltpu.VMEM)
    hbm = pl.BlockSpec(memory_space=pltpu.HBM)
    return pl.pallas_call(
        shard_body,
        in_specs=[hbm, hbm, vmem],
        out_specs=vmem,
        out_shape=pltpu.VMEM((1, 2, owned + META, feature_count), jnp.bfloat16),
        scratch_shapes=[
            pltpu.VMEM((owned, feature_count), means.dtype),
            pltpu.VMEM((owned, feature_count), inv_var.dtype),
            pltpu.SemaphoreType.DMA((2,)),
        ],
        compiler_params=pltpu.CompilerParams(vmem_limit_bytes=VMEM_LIMIT),
        cost_estimate=pl.CostEstimate(
            flops=owned * feature_count * 40,
            bytes_accessed=owned * feature_count * 8,
            transcendentals=owned * feature_count,
        ),
        name="parameter_shard",
    )(in_hbm(means), in_hbm(inv_var), log_weight.reshape(1, owned))


def cut_body(cuts, points_ref, *refs):
    piece_refs, (staging, sems) = refs[:-2], refs[-2:]
    ways = []
    for j, piece in enumerate(piece_refs):
        here = pl.ds(cuts[j], piece.shape[0])
        there = pl.ds(cuts[j] - cuts[0], piece.shape[0])
        ways.append(
            (
                pltpu.make_async_copy(points_ref.at[here, :], staging.at[there, :], sems.at[0, j]),
                pltpu.make_async_copy(staging.at[there, :], piece, sems.at[1, j]),
            )
        )
    for inward, _ in ways:
        inward.start()
    for inward, outward in ways:
        inward.wait()
        outward.start()
    for _, outward in ways:
        outward.wait()


def cut_rows(points, cuts):
    feature_count = points.shape[1]
    hbm = pl.BlockSpec(memory_space=pltpu.HBM)
    lengths = [b - a for a, b in zip(cuts[:-1], cuts[1:])]
    return pl.pallas_call(
        functools.partial(cut_body, cuts),
        in_specs=[hbm],
        out_specs=[hbm] * len(lengths),
        out_shape=[pltpu.HBM((length, feature_count), points.dtype) for length in lengths],
        scratch_shapes=[
            pltpu.VMEM((sum(lengths), feature_count), points.dtype),
            pltpu.SemaphoreType.DMA((2, len(lengths))),
        ],
        compiler_params=pltpu.CompilerParams(vmem_limit_bytes=VMEM_LIMIT),
        name="cut_rows",
    )(in_hbm(points))


def density_body(first, count, held, pos_ref, x_ref, weight_ref, resp_ref, norm_ref):
    owned = held * CB
    row_index = lax.broadcasted_iota(jnp.int32, (META, RB), 0)
    pieces = jnp.where(row_index < 3, 1.0, 0.0).astype(jnp.bfloat16)

    @pl.loop(0, count)
    def _(i):
        x = x_ref[pl.ds(pl.multiple_of(i * RB, RB), RB), :]
        half = x * x * -0.5
        chosen = []
        for slot in range(CANDS):
            pos = pos_ref[(first + i) * CANDS + slot]
            start = pl.multiple_of(lax.rem(pos, held) * CB, CB)
            chosen.append((lax.div(pos, held), pl.ds(start, CB)))
        scaled = jnp.concatenate([weight_ref[shard, 0, here, :] for shard, here in chosen])
        inverse = jnp.concatenate([weight_ref[shard, 1, here, :] for shard, here in chosen])
        constants = jnp.concatenate(
            [weight_ref[shard, 0, owned:, here] for shard, here in chosen], axis=1
        )
        densities = lax.dot_general(scaled, x, NT, preferred_element_type=jnp.float32)
        densities += lax.dot_general(inverse, half, NT, preferred_element_type=jnp.float32)
        densities += lax.dot_general(constants, pieces, TN, preferred_element_type=jnp.float32)
        peak = jnp.max(densities, axis=0, keepdims=True)
        terms = jnp.exp(densities - peak)
        total = jnp.sum(terms, axis=0, keepdims=True)
        norm_ref[pl.ds(i, 1), :] = peak + jnp.log(total)
        resp = (terms * (1.0 / total)).astype(jnp.bfloat16)
        for slot in range(CANDS):
            resp_ref[i, slot] = resp[slot * CB : (slot + 1) * CB]


def responsibilities(rows, pos, first, weights, held):
    count = rows.shape[0] // RB
    feature_count = rows.shape[1]
    vmem = pl.BlockSpec(memory_space=pltpu.VMEM)
    pairs = count * CANDS
    return pl.pallas_call(
        functools.partial(density_body, first, count, held),
        in_specs=[pl.BlockSpec(memory_space=pltpu.SMEM), vmem, vmem],
        out_specs=[vmem, vmem],
        out_shape=[
            pltpu.VMEM((count, CANDS, CB, RB), jnp.bfloat16),
            pltpu.VMEM((count, RB), jnp.float32),
        ],
        compiler_params=pltpu.CompilerParams(vmem_limit_bytes=VMEM_LIMIT),
        cost_estimate=pl.CostEstimate(
            flops=pairs * 4 * CB * RB * feature_count,
            bytes_accessed=pairs * CB * feature_count * 4 + rows.size * 2,
            transcendentals=pairs * CB * RB,
        ),
        name="responsibilities",
    )(pos, in_vmem(rows), in_vmem(weights))


def list_body(runs, held, owners, place, known, *rest):
    where = [ref[0] for ref in rest[:known]]
    id_refs, (pos_ref, order_ref, start_ref, cursor) = rest[known:-4], rest[-4:]
    bins = start_ref.shape[0]
    number_of_runs = len(runs)
    per_ref = sum(runs) // len(id_refs)
    firsts = [sum(runs[:j]) for j in range(number_of_runs)]

    def run_of(i):
        return sum((i >= start).astype(jnp.int32) for start in firsts[1:]) if firsts[1:] else 0

    @pl.loop(0, bins)
    def _(j):
        start_ref[j] = 0

    for part, id_ref in enumerate(id_refs):

        @pl.loop(0, per_ref)
        def _(row, part=part, id_ref=id_ref):
            i = part * per_ref + row
            for slot in range(CANDS):
                block = id_ref[slot, row]
                holder = place(lax.div(block, owners * held), *where)
                pos = holder * held + lax.rem(block, held)
                pos_ref[i * CANDS + slot] = pos
                key = pos * number_of_runs + run_of(i) + 1
                start_ref[key] = start_ref[key] + 1

    def prefix(j, total):
        total = total + start_ref[j]
        start_ref[j] = total
        cursor[j] = total
        return total

    lax.fori_loop(0, bins, prefix, jnp.int32(0))

    @pl.loop(0, sum(runs))
    def _(i):
        for slot in range(CANDS):
            key = pos_ref[i * CANDS + slot] * number_of_runs + run_of(i)
            order_ref[cursor[key]] = i * CANDS + slot
            cursor[key] = cursor[key] + 1


def pair_lists(candidates, runs, held, group_blocks, owners, place, where):
    smem = pl.BlockSpec(memory_space=pltpu.SMEM)
    pairs = sum(runs) * CANDS
    bins = group_blocks * len(runs) + 1
    return pl.pallas_call(
        functools.partial(list_body, tuple(runs), held, owners, place, len(where)),
        in_specs=[smem] * (len(where) + len(candidates)),
        out_specs=[smem] * 3,
        out_shape=[jax.ShapeDtypeStruct((n,), jnp.int32) for n in (pairs, pairs, bins)],
        scratch_shapes=[pltpu.SMEM((bins,), jnp.int32)],
        compiler_params=pltpu.CompilerParams(vmem_limit_bytes=VMEM_LIMIT),
        name="pair_lists",
    )(*where, *candidates)


def moment_body(shards, held, runs, order_ref, start_ref, *rest):
    parts, outs = len(runs), len(shards)
    row_refs, resp_refs = rest[:parts], rest[parts : 2 * parts]
    out_refs = rest[2 * parts : 2 * parts + outs]
    sums, count_sum = rest[2 * parts + outs :]
    owned = held * CB
    meta = slice(2 * owned, 2 * owned + META)
    ones = jnp.ones((META, 2 * RB), jnp.bfloat16)

    def block_sums(pos):
        sums[...] = jnp.zeros_like(sums)
        count_sum[...] = jnp.zeros_like(count_sum)
        base = 0
        for run in range(parts):
            entry = pos * parts + run
            low, high = start_ref[entry], start_ref[entry + 1]

            @pl.loop(0, lax.div(high - low + 1, 2))
            def _(step, base=base, run=run, low=low, high=high):
                one = low + 2 * step
                two = jnp.minimum(one + 1, high - 1)
                valid = (one + 1 < high).astype(jnp.float32)
                pair_a, pair_b = order_ref[one] - base, order_ref[two] - base
                row_a, row_b = lax.div(pair_a, CANDS), lax.div(pair_b, CANDS)
                weight_a = resp_refs[run][row_a, lax.rem(pair_a, CANDS)]
                weight_b = resp_refs[run][row_b, lax.rem(pair_b, CANDS)]
                weight_b = (weight_b.astype(jnp.float32) * valid).astype(jnp.bfloat16)
                weight = jnp.concatenate([weight_a, weight_b], axis=1)
                x = jnp.concatenate(
                    [
                        row_refs[run][pl.ds(pl.multiple_of(row_a * RB, RB), RB), :],
                        row_refs[run][pl.ds(pl.multiple_of(row_b * RB, RB), RB), :],
                    ],
                    axis=0,
                )
                sums[0] += jnp.dot(weight, x, preferred_element_type=jnp.float32)
                sums[1] += jnp.dot(weight, x * x, preferred_element_type=jnp.float32)
                count_sum[...] += lax.dot_general(
                    ones, weight, NT, preferred_element_type=jnp.float32
                )

            base += runs[run] * CANDS

    for shard, out_ref in zip(shards, out_refs):
        out_ref[meta, :] = jnp.zeros((META, out_ref.shape[1]), jnp.bfloat16)

        @pl.loop(0, held)
        def _(block, shard=shard, out_ref=out_ref):
            block_sums(shard * held + block)
            start = pl.multiple_of(block * CB, CB)
            out_ref[pl.ds(start, CB), :] = sums[0].astype(jnp.bfloat16)
            out_ref[pl.ds(owned + start, CB), :] = sums[1].astype(jnp.bfloat16)
            out_ref[meta, pl.ds(start, CB)] = count_sum[...].astype(jnp.bfloat16)


def moments(rows, resp, order, starts, held, shards):
    runs = tuple(r.shape[0] // RB for r in rows)
    feature_count = rows[0].shape[1]
    smem = pl.BlockSpec(memory_space=pltpu.SMEM)
    vmem = pl.BlockSpec(memory_space=pltpu.VMEM)
    pairs = sum(runs) * held * len(shards) // 8
    out_shape = pltpu.VMEM((2 * held * CB + META, feature_count), jnp.bfloat16)
    return pl.pallas_call(
        functools.partial(moment_body, tuple(shards), held, runs),
        in_specs=[smem, smem] + [vmem] * (2 * len(runs)),
        out_specs=[vmem] * len(shards),
        out_shape=[out_shape] * len(shards),
        scratch_shapes=[
            pltpu.VMEM((2, CB, feature_count), jnp.float32),
            pltpu.VMEM((META, CB), jnp.float32),
        ],
        compiler_params=pltpu.CompilerParams(vmem_limit_bytes=VMEM_LIMIT),
        cost_estimate=pl.CostEstimate(
            flops=pairs * 4 * CB * RB * feature_count,
            bytes_accessed=pairs * RB * (feature_count + CB) * 2,
            transcendentals=0,
        ),
        name="moments",
    )(order, starts, *[in_vmem(r) for r in rows], *[in_vmem(r) for r in resp])


CHUNK = 80


def each_chunk(rows, step):
    whole = rows // CHUNK

    @pl.loop(0, whole)
    def _(i):
        step(pl.ds(pl.multiple_of(i * CHUNK, 16), CHUNK))

    if rows % CHUNK:
        step(slice(whole * CHUNK, rows))


def copy_body(places, skip, *refs):
    sources, target, sems = refs[skip:-2], refs[-2], refs[-1]
    copies = [
        pltpu.make_async_copy(source.at[0], target.at[index], sems.at[j])
        for j, (index, source) in enumerate(zip(places, sources))
    ]
    for copy in copies:
        copy.start()
    for copy in copies:
        copy.wait()


def stacked(total, places, shards, *earlier):
    vmem = pl.BlockSpec(memory_space=pltpu.VMEM)
    anywhere = pl.BlockSpec(memory_space=pl.ANY)
    return pl.pallas_call(
        functools.partial(copy_body, places, len(earlier)),
        in_specs=[vmem] * len(earlier) + [anywhere] * len(shards),
        out_specs=vmem,
        out_shape=pltpu.VMEM((total,) + shards[0].shape[1:], jnp.bfloat16),
        scratch_shapes=[pltpu.SemaphoreType.DMA((len(shards),))],
        input_output_aliases={0: 0} if earlier else {},
        compiler_params=pltpu.CompilerParams(vmem_limit_bytes=VMEM_LIMIT),
        name="stack_shards",
    )(*[in_vmem(e) for e in earlier], *shards)


def add_body(*refs):
    def step(here):
        terms = [ref[here, :].astype(jnp.float32) for ref in refs[:-1]]
        refs[-1][here, :] = functools.reduce(jnp.add, terms).astype(jnp.bfloat16)

    each_chunk(refs[-1].shape[0], step)


def add_two_body(a_ref, b_ref, c_ref, d_ref, e_ref, first_ref, second_ref):
    def step(here):
        first = a_ref[here, :].astype(jnp.float32) + b_ref[here, :].astype(jnp.float32)
        first_ref[here, :] = first.astype(jnp.bfloat16)
        second = c_ref[here, :].astype(jnp.float32) + d_ref[here, :].astype(jnp.float32)
        second_ref[here, :] = (second + e_ref[here, :].astype(jnp.float32)).astype(jnp.bfloat16)

    each_chunk(first_ref.shape[0], step)


def added_two(*terms):
    vmem = pl.BlockSpec(memory_space=pltpu.VMEM)
    shape = terms[0].shape
    return pl.pallas_call(
        add_two_body,
        in_specs=[vmem] * 5,
        out_specs=[vmem] * 2,
        out_shape=[pltpu.VMEM(shape, jnp.bfloat16)] * 2,
        compiler_params=pltpu.CompilerParams(vmem_limit_bytes=12 * 1024 * 1024),
        name="add_both_sums",
    )(*[in_vmem(value) for value in terms])


def join_body(*refs):
    start = 0
    for ref in refs[:-1]:
        refs[-1][start : start + ref.shape[0], :] = ref[...]
        start += ref.shape[0]


def small_step(body, shape, dtype, name, *operands):
    vmem = pl.BlockSpec(memory_space=pltpu.VMEM)
    return pl.pallas_call(
        body,
        in_specs=[vmem] * len(operands),
        out_specs=vmem,
        out_shape=pltpu.VMEM(shape, dtype),
        compiler_params=pltpu.CompilerParams(vmem_limit_bytes=VMEM_LIMIT),
        cost_estimate=pl.CostEstimate(
            flops=math.prod(shape), bytes_accessed=2 * math.prod(shape), transcendentals=0
        ),
        name=name,
    )(*[in_vmem(value) for value in operands])


def added(*terms):
    return small_step(add_body, terms[0].shape, jnp.bfloat16, "add_sums", *terms)


def joined(*norms):
    shape = (sum(n.shape[0] for n in norms), RB)
    return small_step(join_body, shape, jnp.float32, "join_norms", *norms)


def result_body(owned, end_ref, *refs):
    own_norm, end_norm, end_sum = refs[:3]
    terms, (count_ref, first_ref, second_ref, loglik_ref) = refs[3:-4], refs[-4:]
    is_end = end_ref[0] > 0
    block = pl.program_id(0)
    feature_count = first_ref.shape[1]

    def total(rows):
        inner = functools.reduce(jnp.add, [t[rows, :].astype(jnp.float32) for t in terms])
        return jnp.where(is_end, end_sum[rows, :].astype(jnp.float32), inner)

    start = pl.multiple_of(block * CB, CB)
    first_ref[...] = total(pl.ds(start, CB))
    second_ref[...] = total(pl.ds(owned + start, CB))
    count_ref[...] = total(slice(2 * owned, 2 * owned + META))[0:1, :owned]
    norm = jnp.where(is_end, end_norm[...], own_norm[...])
    loglik_ref[...] = norm * (1.0 / feature_count)


def results_of(is_end, own_norm, end_norm, end_sum, *terms):
    rows, feature_count = end_sum.shape
    owned = (rows - META) // 2
    vmem = pl.BlockSpec(memory_space=pltpu.VMEM)
    operands = (own_norm, end_norm, end_sum) + terms
    return pl.pallas_call(
        functools.partial(result_body, owned),
        grid=(owned // CB,),
        in_specs=[pl.BlockSpec(memory_space=pltpu.SMEM)] + [vmem] * len(operands),
        out_specs=[
            pl.BlockSpec((1, owned), lambda i: (0, 0)),
            pl.BlockSpec((CB, feature_count), lambda i: (i, 0)),
            pl.BlockSpec((CB, feature_count), lambda i: (i, 0)),
            pl.BlockSpec(own_norm.shape, lambda i: (0, 0)),
        ],
        out_shape=[
            jax.ShapeDtypeStruct((1, owned), jnp.float32),
            jax.ShapeDtypeStruct((owned, feature_count), jnp.float32),
            jax.ShapeDtypeStruct((owned, feature_count), jnp.float32),
            jax.ShapeDtypeStruct(own_norm.shape, jnp.float32),
        ],
        compiler_params=pltpu.CompilerParams(vmem_limit_bytes=VMEM_LIMIT),
        name="results",
    )(is_end.astype(jnp.int32).reshape(1), *[in_vmem(value) for value in operands])


def plain_plan(points, candidates, parameters, held):
    weights = parameter_shard(*parameters)
    dp_size = lax.axis_size("dp")
    row_blocks = points.shape[0] // RB
    pos, order, starts = pair_lists(
        [candidates.T],
        (row_blocks,),
        held,
        dp_size * held,
        lax.axis_size("comp"),
        lambda holder: holder,
        [],
    )
    all_weights = lax.all_gather(weights, "dp", axis=0, tiled=True)
    resp, norm = responsibilities(points, pos, 0, all_weights, held)
    sums = []
    for j in range(dp_size):
        sums += moments([points], [resp], order, starts, held, [j])
    total = lax.psum_scatter(jnp.concatenate(sums), "dp", scatter_dimension=0, tiled=True)
    total = total.astype(jnp.float32)
    owned = held * CB
    counts, first, second = total[2 * owned, :owned], total[:owned], total[owned : 2 * owned]
    return counts, first, second, norm.reshape(-1) / points.shape[1]


def line_pairs(links):
    return [(2 * a + c, 2 * b + c) for a, b in links for c in (0, 1)]


INWARD = line_pairs(((0, 1), (3, 2)))
OUTWARD = line_pairs(((1, 0), (2, 3)))
MIDDLE = line_pairs(((1, 2), (2, 1)))
CORES = [(2, 3), (3, 2), (4, 5), (5, 4)]


def move(value, pairs):
    return lax.ppermute(value, "dp", pairs)


def after(value, *others):
    return lax.optimization_barrier((value,) + others)[0]


def line_place(holder, chip, core):
    z, other = lax.div(holder, 2), lax.rem(holder, 2)
    z = jnp.where(chip < 2, z, 3 - z)
    z = jnp.where(z == 0, 1, jnp.where(z == 1, 0, z))
    return z * 2 + lax.rem(other + core, 2)


def line_plan(points, candidates, parameters, held):
    index = lax.axis_index("dp")
    chip, core = index // 2, index % 2
    where = [chip.reshape(1), core.reshape(1)]
    row_blocks = points.shape[0] // RB
    small = row_blocks // 8
    cuts = (0, 1, 2 + 4 * small, row_blocks - small, row_blocks)
    runs = (row_blocks,) + tuple(b - a for a, b in zip(cuts[:-1], cuts[1:]))
    own_ids = candidates.T
    end_ids = move(own_ids, INWARD)
    before = move(points[: cuts[1] * RB], INWARD)
    weights = parameter_shard(*parameters)
    weights_then, end_ids, before = lax.optimization_barrier((weights, end_ids, before))

    outer = move(weights_then, INWARD)
    across = move(weights, MIDDLE)
    pieces = cut_rows(after(points, weights_then), [cut * RB for cut in cuts[1:]])
    own_shared = move(after(weights, *pieces), CORES)
    most = move(after(pieces[0], outer), INWARD)
    far = move(outer, MIDDLE)
    moved = [before, most] + [move(after(piece, far), INWARD) for piece in pieces[1:]]
    pos, order, starts = pair_lists(
        [own_ids, end_ids], runs, held, 8 * held, lax.axis_size("comp"), line_place, where
    )
    near = [after(weights, pos, order, starts), own_shared, outer, across]
    near_weights = stacked(8, (0, 1, 2, 4), near)
    far, near_weights = lax.optimization_barrier((far, near_weights))
    shared = [move(w, CORES) for w in (outer, across, far)]
    all_weights = stacked(8, (6, 3, 5, 7), [after(far, most)] + shared, near_weights)

    rows = [points] + moved
    results = []
    for j, run_rows in enumerate(rows):
        if results:
            pos = after(pos, results[-1][1])
        results.append(responsibilities(run_rows, pos, sum(runs[:j]), all_weights, held))
    resp = [r[0] for r in results]

    def sums_of(position, *earlier):
        return moments(rows, resp, after(order, *earlier), starts, held, [position])[0]

    far_other = sums_of(7)
    far_received = move(far_other, CORES)
    far_own = sums_of(6, far_other)
    far_part = added(far_own, far_received)
    far_sum = move(far_part, MIDDLE)
    across_other = sums_of(5, far_part)
    across_received = move(across_other, CORES)
    outer_other = sums_of(3, across_other)
    outer_received = move(outer_other, CORES)
    own_other = sums_of(1, outer_other)
    own_received = move(own_other, CORES)
    end_norm = move(after(joined(*[r[1] for r in results[1:]]), across_other), OUTWARD)
    across_own = sums_of(4, own_other)
    outer_own = sums_of(2, across_own, end_norm)
    far_sum, outer_own, across_own = lax.optimization_barrier((far_sum, outer_own, across_own))
    across_part, outer_sum = added_two(
        across_own, across_received, outer_own, outer_received, far_sum
    )
    across_sum = move(across_part, MIDDLE)
    end_sum = move(outer_sum, OUTWARD)
    own_own = sums_of(0, across_part, outer_sum)
    is_end = jnp.logical_or(chip == 0, chip == 3)
    counts, first, second, loglik = results_of(
        is_end, results[0][1], end_norm, end_sum, added(own_own, own_received), across_sum
    )
    return counts.reshape(-1), first, second, loglik.reshape(-1)


def on_device(points, candidates, means, inv_var, log_weight):
    held = means.shape[0] // CB
    plan = line_plan if lax.axis_size("dp") == 8 else plain_plan
    return plan(points, candidates, (means, inv_var, log_weight), held)


def solution(mesh):
    return jax.shard_map(
        on_device,
        mesh=mesh,
        in_specs=(
            P(("dp", "comp"), None),
            P(("dp", "comp"), None),
            P(("dp", "comp"), None),
            P(("dp", "comp"), None),
            P(("dp", "comp")),
        ),
        out_specs=(
            P(("dp", "comp")),
            P(("dp", "comp"), None),
            P(("dp", "comp"), None),
            P(("dp", "comp")),
        ),
        check_vma=False,
    )
```

```python
import functools
import math

import jax
import jax.numpy as jnp
from jax import lax
from jax.experimental import pallas as pl
from jax.experimental.pallas import tpu as pltpu
from jax.sharding import PartitionSpec as P

CB = 128
RB = 128
CANDS = 4
META = 16
VMEM_LIMIT = 8 * 1024 * 1024
NT = (((1,), (1,)), ((), ()))
TN = (((0,), (0,)), ((), ()))


def in_vmem(value):
    return pltpu.with_memory_space_constraint(value, pltpu.VMEM)


def in_hbm(value):
    return pltpu.with_memory_space_constraint(value, pltpu.HBM)


def shard_body(means_hbm, inv_hbm, log_ref, out_ref, means_ref, inv_ref, sems):
    copies = [
        pltpu.make_async_copy(means_hbm, means_ref, sems.at[0]),
        pltpu.make_async_copy(inv_hbm, inv_ref, sems.at[1]),
    ]
    for copy in copies:
        copy.start()
    owned, feature_count = means_ref.shape
    ones = jnp.ones((META, feature_count), jnp.float32)
    row = lax.broadcasted_iota(jnp.int32, (META, CB), 0)
    for copy in copies:
        copy.wait()
    for half in range(2):
        out_ref[0, half, owned:, :] = jnp.zeros((META, feature_count), jnp.bfloat16)
    for block in range(owned // CB):
        here = slice(block * CB, (block + 1) * CB)
        inverse = inv_ref[here, :]
        mean_f = means_ref[here, :].astype(jnp.float32)
        inv_f = inverse.astype(jnp.float32)
        scaled = inv_f * mean_f
        out_ref[0, 0, here, :] = scaled.astype(jnp.bfloat16)
        out_ref[0, 1, here, :] = inverse
        terms = 0.5 * jnp.log(inv_f) - 0.5 * (scaled * mean_f)
        rest = lax.dot_general(
            ones, terms, NT, precision=lax.Precision.HIGHEST, preferred_element_type=jnp.float32
        )
        rest += log_ref[:, here].astype(jnp.float32)
        rest -= 0.5 * feature_count * math.log(2.0 * math.pi)
        high = rest.astype(jnp.bfloat16).astype(jnp.float32)
        rest -= high
        middle = rest.astype(jnp.bfloat16).astype(jnp.float32)
        low = rest - middle
        pieces = jnp.where(row == 0, high, jnp.where(row == 1, middle, low))
        out_ref[0, 0, owned:, here] = pieces.astype(jnp.bfloat16)


def parameter_shard(means, inv_var, log_weight):
    owned, feature_count = means.shape
    vmem = pl.BlockSpec(memory_space=pltpu.VMEM)
    hbm = pl.BlockSpec(memory_space=pltpu.HBM)
    return pl.pallas_call(
        shard_body,
        in_specs=[hbm, hbm, vmem],
        out_specs=vmem,
        out_shape=pltpu.VMEM((1, 2, owned + META, feature_count), jnp.bfloat16),
        scratch_shapes=[
            pltpu.VMEM((owned, feature_count), means.dtype),
            pltpu.VMEM((owned, feature_count), inv_var.dtype),
            pltpu.SemaphoreType.DMA((2,)),
        ],
        compiler_params=pltpu.CompilerParams(vmem_limit_bytes=VMEM_LIMIT),
        cost_estimate=pl.CostEstimate(
            flops=owned * feature_count * 40,
            bytes_accessed=owned * feature_count * 8,
            transcendentals=owned * feature_count,
        ),
        name="parameter_shard",
    )(in_hbm(means), in_hbm(inv_var), log_weight.reshape(1, owned))


def cut_body(cuts, points_ref, *refs):
    piece_refs, (staging, sems) = refs[:-2], refs[-2:]
    ways = []
    for j, piece in enumerate(piece_refs):
        here = pl.ds(cuts[j], piece.shape[0])
        there = pl.ds(cuts[j] - cuts[0], piece.shape[0])
        ways.append(
            (
                pltpu.make_async_copy(points_ref.at[here, :], staging.at[there, :], sems.at[0, j]),
                pltpu.make_async_copy(staging.at[there, :], piece, sems.at[1, j]),
            )
        )
    for inward, _ in ways:
        inward.start()
    for inward, outward in ways:
        inward.wait()
        outward.start()
    for _, outward in ways:
        outward.wait()


def cut_rows(points, cuts):
    feature_count = points.shape[1]
    hbm = pl.BlockSpec(memory_space=pltpu.HBM)
    lengths = [b - a for a, b in zip(cuts[:-1], cuts[1:])]
    return pl.pallas_call(
        functools.partial(cut_body, cuts),
        in_specs=[hbm],
        out_specs=[hbm] * len(lengths),
        out_shape=[pltpu.HBM((length, feature_count), points.dtype) for length in lengths],
        scratch_shapes=[
            pltpu.VMEM((sum(lengths), feature_count), points.dtype),
            pltpu.SemaphoreType.DMA((2, len(lengths))),
        ],
        compiler_params=pltpu.CompilerParams(vmem_limit_bytes=VMEM_LIMIT),
        name="cut_rows",
    )(in_hbm(points))


def density_body(first, count, held, pos_ref, x_ref, weight_ref, resp_ref, norm_ref):
    owned = held * CB
    row_index = lax.broadcasted_iota(jnp.int32, (META, RB), 0)
    pieces = jnp.where(row_index < 3, 1.0, 0.0).astype(jnp.bfloat16)

    @pl.loop(0, count)
    def _(i):
        x = x_ref[pl.ds(pl.multiple_of(i * RB, RB), RB), :]
        half = x * x * -0.5
        chosen = []
        for slot in range(CANDS):
            pos = pos_ref[(first + i) * CANDS + slot]
            start = pl.multiple_of(lax.rem(pos, held) * CB, CB)
            chosen.append((lax.div(pos, held), pl.ds(start, CB)))
        scaled = jnp.concatenate([weight_ref[shard, 0, here, :] for shard, here in chosen])
        inverse = jnp.concatenate([weight_ref[shard, 1, here, :] for shard, here in chosen])
        constants = jnp.concatenate(
            [weight_ref[shard, 0, owned:, here] for shard, here in chosen], axis=1
        )
        densities = lax.dot_general(scaled, x, NT, preferred_element_type=jnp.float32)
        densities += lax.dot_general(inverse, half, NT, preferred_element_type=jnp.float32)
        densities += lax.dot_general(constants, pieces, TN, preferred_element_type=jnp.float32)
        peak = jnp.max(densities, axis=0, keepdims=True)
        terms = jnp.exp(densities - peak)
        total = jnp.sum(terms, axis=0, keepdims=True)
        norm_ref[pl.ds(i, 1), :] = peak + jnp.log(total)
        resp = (terms * (1.0 / total)).astype(jnp.bfloat16)
        for slot in range(CANDS):
            resp_ref[i, slot] = resp[slot * CB : (slot + 1) * CB]


def responsibilities(rows, pos, first, weights, held):
    count = rows.shape[0] // RB
    feature_count = rows.shape[1]
    vmem = pl.BlockSpec(memory_space=pltpu.VMEM)
    pairs = count * CANDS
    return pl.pallas_call(
        functools.partial(density_body, first, count, held),
        in_specs=[pl.BlockSpec(memory_space=pltpu.SMEM), vmem, vmem],
        out_specs=[vmem, vmem],
        out_shape=[
            pltpu.VMEM((count, CANDS, CB, RB), jnp.bfloat16),
            pltpu.VMEM((count, RB), jnp.float32),
        ],
        compiler_params=pltpu.CompilerParams(vmem_limit_bytes=VMEM_LIMIT),
        cost_estimate=pl.CostEstimate(
            flops=pairs * 4 * CB * RB * feature_count,
            bytes_accessed=pairs * CB * feature_count * 4 + rows.size * 2,
            transcendentals=pairs * CB * RB,
        ),
        name="responsibilities",
    )(pos, in_vmem(rows), in_vmem(weights))


def list_body(runs, held, owners, place, known, *rest):
    where = [ref[0] for ref in rest[:known]]
    id_refs, (pos_ref, order_ref, start_ref, cursor) = rest[known:-4], rest[-4:]
    bins = start_ref.shape[0]
    number_of_runs = len(runs)
    per_ref = sum(runs) // len(id_refs)
    firsts = [sum(runs[:j]) for j in range(number_of_runs)]

    def run_of(i):
        return sum((i >= start).astype(jnp.int32) for start in firsts[1:]) if firsts[1:] else 0

    @pl.loop(0, bins)
    def _(j):
        start_ref[j] = 0

    for part, id_ref in enumerate(id_refs):

        @pl.loop(0, per_ref)
        def _(row, part=part, id_ref=id_ref):
            i = part * per_ref + row
            for slot in range(CANDS):
                block = id_ref[slot, row]
                holder = place(lax.div(block, owners * held), *where)
                pos = holder * held + lax.rem(block, held)
                pos_ref[i * CANDS + slot] = pos
                key = pos * number_of_runs + run_of(i) + 1
                start_ref[key] = start_ref[key] + 1

    def prefix(j, total):
        total = total + start_ref[j]
        start_ref[j] = total
        cursor[j] = total
        return total

    lax.fori_loop(0, bins, prefix, jnp.int32(0))

    @pl.loop(0, sum(runs))
    def _(i):
        for slot in range(CANDS):
            key = pos_ref[i * CANDS + slot] * number_of_runs + run_of(i)
            order_ref[cursor[key]] = i * CANDS + slot
            cursor[key] = cursor[key] + 1


def pair_lists(candidates, runs, held, group_blocks, owners, place, where):
    smem = pl.BlockSpec(memory_space=pltpu.SMEM)
    pairs = sum(runs) * CANDS
    bins = group_blocks * len(runs) + 1
    return pl.pallas_call(
        functools.partial(list_body, tuple(runs), held, owners, place, len(where)),
        in_specs=[smem] * (len(where) + len(candidates)),
        out_specs=[smem] * 3,
        out_shape=[jax.ShapeDtypeStruct((n,), jnp.int32) for n in (pairs, pairs, bins)],
        scratch_shapes=[pltpu.SMEM((bins,), jnp.int32)],
        compiler_params=pltpu.CompilerParams(vmem_limit_bytes=VMEM_LIMIT),
        name="pair_lists",
    )(*where, *candidates)


def moment_body(shards, held, runs, order_ref, start_ref, *rest):
    parts, outs = len(runs), len(shards)
    row_refs, resp_refs = rest[:parts], rest[parts : 2 * parts]
    out_refs = rest[2 * parts : 2 * parts + outs]
    sums, count_sum = rest[2 * parts + outs :]
    owned = held * CB
    meta = slice(2 * owned, 2 * owned + META)
    ones = jnp.ones((META, 2 * RB), jnp.bfloat16)

    def block_sums(pos):
        sums[...] = jnp.zeros_like(sums)
        count_sum[...] = jnp.zeros_like(count_sum)
        base = 0
        for run in range(parts):
            entry = pos * parts + run
            low, high = start_ref[entry], start_ref[entry + 1]

            @pl.loop(0, lax.div(high - low + 1, 2))
            def _(step, base=base, run=run, low=low, high=high):
                one = low + 2 * step
                two = jnp.minimum(one + 1, high - 1)
                valid = (one + 1 < high).astype(jnp.float32)
                pair_a, pair_b = order_ref[one] - base, order_ref[two] - base
                row_a, row_b = lax.div(pair_a, CANDS), lax.div(pair_b, CANDS)
                weight_a = resp_refs[run][row_a, lax.rem(pair_a, CANDS)]
                weight_b = resp_refs[run][row_b, lax.rem(pair_b, CANDS)]
                weight_b = (weight_b.astype(jnp.float32) * valid).astype(jnp.bfloat16)
                weight = jnp.concatenate([weight_a, weight_b], axis=1)
                x = jnp.concatenate(
                    [
                        row_refs[run][pl.ds(pl.multiple_of(row_a * RB, RB), RB), :],
                        row_refs[run][pl.ds(pl.multiple_of(row_b * RB, RB), RB), :],
                    ],
                    axis=0,
                )
                sums[0] += jnp.dot(weight, x, preferred_element_type=jnp.float32)
                sums[1] += jnp.dot(weight, x * x, preferred_element_type=jnp.float32)
                count_sum[...] += lax.dot_general(
                    ones, weight, NT, preferred_element_type=jnp.float32
                )

            base += runs[run] * CANDS

    for shard, out_ref in zip(shards, out_refs):
        out_ref[meta, :] = jnp.zeros((META, out_ref.shape[1]), jnp.bfloat16)

        @pl.loop(0, held)
        def _(block, shard=shard, out_ref=out_ref):
            block_sums(shard * held + block)
            start = pl.multiple_of(block * CB, CB)
            out_ref[pl.ds(start, CB), :] = sums[0].astype(jnp.bfloat16)
            out_ref[pl.ds(owned + start, CB), :] = sums[1].astype(jnp.bfloat16)
            out_ref[meta, pl.ds(start, CB)] = count_sum[...].astype(jnp.bfloat16)


def moments(rows, resp, order, starts, held, shards):
    runs = tuple(r.shape[0] // RB for r in rows)
    feature_count = rows[0].shape[1]
    smem = pl.BlockSpec(memory_space=pltpu.SMEM)
    vmem = pl.BlockSpec(memory_space=pltpu.VMEM)
    pairs = sum(runs) * held * len(shards) // 8
    out_shape = pltpu.VMEM((2 * held * CB + META, feature_count), jnp.bfloat16)
    return pl.pallas_call(
        functools.partial(moment_body, tuple(shards), held, runs),
        in_specs=[smem, smem] + [vmem] * (2 * len(runs)),
        out_specs=[vmem] * len(shards),
        out_shape=[out_shape] * len(shards),
        scratch_shapes=[
            pltpu.VMEM((2, CB, feature_count), jnp.float32),
            pltpu.VMEM((META, CB), jnp.float32),
        ],
        compiler_params=pltpu.CompilerParams(vmem_limit_bytes=VMEM_LIMIT),
        cost_estimate=pl.CostEstimate(
            flops=pairs * 4 * CB * RB * feature_count,
            bytes_accessed=pairs * RB * (feature_count + CB) * 2,
            transcendentals=0,
        ),
        name="moments",
    )(order, starts, *[in_vmem(r) for r in rows], *[in_vmem(r) for r in resp])


CHUNK = 80


def each_chunk(rows, step):
    whole = rows // CHUNK

    @pl.loop(0, whole)
    def _(i):
        step(pl.ds(pl.multiple_of(i * CHUNK, 16), CHUNK))

    if rows % CHUNK:
        step(slice(whole * CHUNK, rows))


def copy_body(places, skip, *refs):
    sources, target, sems = refs[skip:-2], refs[-2], refs[-1]
    copies = [
        pltpu.make_async_copy(source.at[0], target.at[index], sems.at[j])
        for j, (index, source) in enumerate(zip(places, sources))
    ]
    for copy in copies:
        copy.start()
    for copy in copies:
        copy.wait()


def stacked(total, places, shards, *earlier):
    vmem = pl.BlockSpec(memory_space=pltpu.VMEM)
    anywhere = pl.BlockSpec(memory_space=pl.ANY)
    return pl.pallas_call(
        functools.partial(copy_body, places, len(earlier)),
        in_specs=[vmem] * len(earlier) + [anywhere] * len(shards),
        out_specs=vmem,
        out_shape=pltpu.VMEM((total,) + shards[0].shape[1:], jnp.bfloat16),
        scratch_shapes=[pltpu.SemaphoreType.DMA((len(shards),))],
        input_output_aliases={0: 0} if earlier else {},
        compiler_params=pltpu.CompilerParams(vmem_limit_bytes=VMEM_LIMIT),
        name="stack_shards",
    )(*[in_vmem(e) for e in earlier], *shards)


def add_body(*refs):
    def step(here):
        terms = [ref[here, :].astype(jnp.float32) for ref in refs[:-1]]
        refs[-1][here, :] = functools.reduce(jnp.add, terms).astype(jnp.bfloat16)

    each_chunk(refs[-1].shape[0], step)


def add_two_body(a_ref, b_ref, c_ref, d_ref, e_ref, first_ref, second_ref):
    def step(here):
        first = a_ref[here, :].astype(jnp.float32) + b_ref[here, :].astype(jnp.float32)
        first_ref[here, :] = first.astype(jnp.bfloat16)
        second = c_ref[here, :].astype(jnp.float32) + d_ref[here, :].astype(jnp.float32)
        second_ref[here, :] = (second + e_ref[here, :].astype(jnp.float32)).astype(jnp.bfloat16)

    each_chunk(first_ref.shape[0], step)


def added_two(*terms):
    vmem = pl.BlockSpec(memory_space=pltpu.VMEM)
    shape = terms[0].shape
    return pl.pallas_call(
        add_two_body,
        in_specs=[vmem] * 5,
        out_specs=[vmem] * 2,
        out_shape=[pltpu.VMEM(shape, jnp.bfloat16)] * 2,
        compiler_params=pltpu.CompilerParams(vmem_limit_bytes=12 * 1024 * 1024),
        name="add_both_sums",
    )(*[in_vmem(value) for value in terms])


def join_body(*refs):
    start = 0
    for ref in refs[:-1]:
        refs[-1][start : start + ref.shape[0], :] = ref[...]
        start += ref.shape[0]


def small_step(body, shape, dtype, name, *operands):
    vmem = pl.BlockSpec(memory_space=pltpu.VMEM)
    return pl.pallas_call(
        body,
        in_specs=[vmem] * len(operands),
        out_specs=vmem,
        out_shape=pltpu.VMEM(shape, dtype),
        compiler_params=pltpu.CompilerParams(vmem_limit_bytes=VMEM_LIMIT),
        cost_estimate=pl.CostEstimate(
            flops=math.prod(shape), bytes_accessed=2 * math.prod(shape), transcendentals=0
        ),
        name=name,
    )(*[in_vmem(value) for value in operands])


def added(*terms):
    return small_step(add_body, terms[0].shape, jnp.bfloat16, "add_sums", *terms)


def joined(*norms):
    shape = (sum(n.shape[0] for n in norms), RB)
    return small_step(join_body, shape, jnp.float32, "join_norms", *norms)


def result_body(owned, end_ref, *refs):
    own_norm, end_norm, end_sum = refs[:3]
    terms, (count_ref, first_ref, second_ref, loglik_ref) = refs[3:-4], refs[-4:]
    is_end = end_ref[0] > 0
    block = pl.program_id(0)
    feature_count = first_ref.shape[1]

    def total(rows):
        inner = functools.reduce(jnp.add, [t[rows, :].astype(jnp.float32) for t in terms])
        return jnp.where(is_end, end_sum[rows, :].astype(jnp.float32), inner)

    start = pl.multiple_of(block * CB, CB)
    first_ref[...] = total(pl.ds(start, CB))
    second_ref[...] = total(pl.ds(owned + start, CB))
    count_ref[...] = total(slice(2 * owned, 2 * owned + META))[0:1, :owned]
    norm = jnp.where(is_end, end_norm[...], own_norm[...])
    loglik_ref[...] = norm * (1.0 / feature_count)


def results_of(is_end, own_norm, end_norm, end_sum, *terms):
    rows, feature_count = end_sum.shape
    owned = (rows - META) // 2
    vmem = pl.BlockSpec(memory_space=pltpu.VMEM)
    operands = (own_norm, end_norm, end_sum) + terms
    return pl.pallas_call(
        functools.partial(result_body, owned),
        grid=(owned // CB,),
        in_specs=[pl.BlockSpec(memory_space=pltpu.SMEM)] + [vmem] * len(operands),
        out_specs=[
            pl.BlockSpec((1, owned), lambda i: (0, 0)),
            pl.BlockSpec((CB, feature_count), lambda i: (i, 0)),
            pl.BlockSpec((CB, feature_count), lambda i: (i, 0)),
            pl.BlockSpec(own_norm.shape, lambda i: (0, 0)),
        ],
        out_shape=[
            jax.ShapeDtypeStruct((1, owned), jnp.float32),
            jax.ShapeDtypeStruct((owned, feature_count), jnp.float32),
            jax.ShapeDtypeStruct((owned, feature_count), jnp.float32),
            jax.ShapeDtypeStruct(own_norm.shape, jnp.float32),
        ],
        compiler_params=pltpu.CompilerParams(vmem_limit_bytes=VMEM_LIMIT),
        name="results",
    )(is_end.astype(jnp.int32).reshape(1), *[in_vmem(value) for value in operands])


def plain_plan(points, candidates, parameters, held):
    weights = parameter_shard(*parameters)
    dp_size = lax.axis_size("dp")
    row_blocks = points.shape[0] // RB
    pos, order, starts = pair_lists(
        [candidates.T],
        (row_blocks,),
        held,
        dp_size * held,
        lax.axis_size("comp"),
        lambda holder: holder,
        [],
    )
    all_weights = lax.all_gather(weights, "dp", axis=0, tiled=True)
    resp, norm = responsibilities(points, pos, 0, all_weights, held)
    sums = []
    for j in range(dp_size):
        sums += moments([points], [resp], order, starts, held, [j])
    total = lax.psum_scatter(jnp.concatenate(sums), "dp", scatter_dimension=0, tiled=True)
    total = total.astype(jnp.float32)
    owned = held * CB
    counts, first, second = total[2 * owned, :owned], total[:owned], total[owned : 2 * owned]
    return counts, first, second, norm.reshape(-1) / points.shape[1]


def line_pairs(links):
    return [(2 * a + c, 2 * b + c) for a, b in links for c in (0, 1)]


INWARD = line_pairs(((0, 1), (3, 2)))
OUTWARD = line_pairs(((1, 0), (2, 3)))
MIDDLE = line_pairs(((1, 2), (2, 1)))
CORES = [(2, 3), (3, 2), (4, 5), (5, 4)]


def move(value, pairs):
    return lax.ppermute(value, "dp", pairs)


def after(value, *others):
    return lax.optimization_barrier((value,) + others)[0]


def line_place(holder, chip, core):
    z, other = lax.div(holder, 2), lax.rem(holder, 2)
    z = jnp.where(chip < 2, z, 3 - z)
    z = jnp.where(z == 0, 1, jnp.where(z == 1, 0, z))
    return z * 2 + lax.rem(other + core, 2)


def line_plan(points, candidates, parameters, held):
    index = lax.axis_index("dp")
    chip, core = index // 2, index % 2
    where = [chip.reshape(1), core.reshape(1)]
    row_blocks = points.shape[0] // RB
    small = row_blocks // 8
    cuts = (0, 1, 2 + 4 * small, row_blocks - small, row_blocks)
    runs = (row_blocks,) + tuple(b - a for a, b in zip(cuts[:-1], cuts[1:]))
    own_ids = candidates.T
    end_ids = move(own_ids, INWARD)
    before = move(points[: cuts[1] * RB], INWARD)
    weights = parameter_shard(*parameters)
    weights_then, end_ids, before = lax.optimization_barrier((weights, end_ids, before))

    outer = move(weights_then, INWARD)
    across = move(weights, MIDDLE)
    pieces = cut_rows(after(points, weights_then), [cut * RB for cut in cuts[1:]])
    own_shared = move(after(weights, *pieces), CORES)
    most = move(after(pieces[0], outer), INWARD)
    far = move(outer, MIDDLE)
    moved = [before, most] + [move(after(piece, far), INWARD) for piece in pieces[1:]]
    pos, order, starts = pair_lists(
        [own_ids, end_ids], runs, held, 8 * held, lax.axis_size("comp"), line_place, where
    )
    near = [after(weights, pos, order, starts), own_shared, outer, across]
    near_weights = stacked(8, (0, 1, 2, 4), near)
    far, near_weights = lax.optimization_barrier((far, near_weights))
    shared = [move(w, CORES) for w in (outer, across, far)]
    all_weights = stacked(8, (6, 3, 5, 7), [after(far, most)] + shared, near_weights)

    rows = [points] + moved
    results = []
    for j, run_rows in enumerate(rows):
        if results:
            pos = after(pos, results[-1][1])
        results.append(responsibilities(run_rows, pos, sum(runs[:j]), all_weights, held))
    resp = [r[0] for r in results]

    def sums_of(position, *earlier):
        return moments(rows, resp, after(order, *earlier), starts, held, [position])[0]

    far_other = sums_of(7)
    far_received = move(far_other, CORES)
    far_own = sums_of(6, far_other)
    far_part = added(far_own, far_received)
    far_sum = move(far_part, MIDDLE)
    across_other = sums_of(5, far_part)
    across_received = move(across_other, CORES)
    outer_other = sums_of(3, across_other)
    outer_received = move(outer_other, CORES)
    end_norm = move(after(joined(*[r[1] for r in results[1:]]), across_other), OUTWARD)
    across_own = sums_of(4, outer_other)
    outer_own = sums_of(2, across_own, end_norm)
    far_sum, outer_own, across_own = lax.optimization_barrier((far_sum, outer_own, across_own))
    across_part, outer_sum = added_two(
        across_own, across_received, outer_own, outer_received, far_sum
    )
    across_sum = move(across_part, MIDDLE)
    end_sum = move(outer_sum, OUTWARD)
    own_other = sums_of(1, across_part, outer_sum)
    own_received = move(own_other, CORES)
    own_own = sums_of(0, own_other)
    across_sum, end_sum, own_own = lax.optimization_barrier((across_sum, end_sum, own_own))
    is_end = jnp.logical_or(chip == 0, chip == 3)
    counts, first, second, loglik = results_of(
        is_end, results[0][1], end_norm, end_sum, own_own, own_received, across_sum
    )
    return counts.reshape(-1), first, second, loglik.reshape(-1)


def on_device(points, candidates, means, inv_var, log_weight):
    held = means.shape[0] // CB
    plan = line_plan if lax.axis_size("dp") == 8 else plain_plan
    return plan(points, candidates, (means, inv_var, log_weight), held)


def solution(mesh):
    return jax.shard_map(
        on_device,
        mesh=mesh,
        in_specs=(
            P(("dp", "comp"), None),
            P(("dp", "comp"), None),
            P(("dp", "comp"), None),
            P(("dp", "comp"), None),
            P(("dp", "comp")),
        ),
        out_specs=(
            P(("dp", "comp")),
            P(("dp", "comp"), None),
            P(("dp", "comp"), None),
            P(("dp", "comp")),
        ),
        check_vma=False,
    )
```

```python
import functools
import math

import jax
import jax.numpy as jnp
from jax import lax
from jax.experimental import pallas as pl
from jax.experimental.pallas import tpu as pltpu
from jax.sharding import PartitionSpec as P

CB = 128
RB = 128
CANDS = 4
META = 16
VMEM_LIMIT = 8 * 1024 * 1024
NT = (((1,), (1,)), ((), ()))
TN = (((0,), (0,)), ((), ()))


def in_vmem(value):
    return pltpu.with_memory_space_constraint(value, pltpu.VMEM)


def in_hbm(value):
    return pltpu.with_memory_space_constraint(value, pltpu.HBM)


def shard_body(means_hbm, inv_hbm, log_ref, out_ref, means_ref, inv_ref, sems):
    copies = [
        pltpu.make_async_copy(means_hbm, means_ref, sems.at[0]),
        pltpu.make_async_copy(inv_hbm, inv_ref, sems.at[1]),
    ]
    for copy in copies:
        copy.start()
    owned, feature_count = means_ref.shape
    ones = jnp.ones((META, feature_count), jnp.float32)
    row = lax.broadcasted_iota(jnp.int32, (META, CB), 0)
    for copy in copies:
        copy.wait()
    for half in range(2):
        out_ref[0, half, owned:, :] = jnp.zeros((META, feature_count), jnp.bfloat16)
    for block in range(owned // CB):
        here = slice(block * CB, (block + 1) * CB)
        inverse = inv_ref[here, :]
        mean_f = means_ref[here, :].astype(jnp.float32)
        inv_f = inverse.astype(jnp.float32)
        scaled = inv_f * mean_f
        out_ref[0, 0, here, :] = scaled.astype(jnp.bfloat16)
        out_ref[0, 1, here, :] = inverse
        terms = 0.5 * jnp.log(inv_f) - 0.5 * (scaled * mean_f)
        rest = lax.dot_general(
            ones, terms, NT, precision=lax.Precision.HIGHEST, preferred_element_type=jnp.float32
        )
        rest += log_ref[:, here].astype(jnp.float32)
        rest -= 0.5 * feature_count * math.log(2.0 * math.pi)
        high = rest.astype(jnp.bfloat16).astype(jnp.float32)
        rest -= high
        middle = rest.astype(jnp.bfloat16).astype(jnp.float32)
        low = rest - middle
        pieces = jnp.where(row == 0, high, jnp.where(row == 1, middle, low))
        out_ref[0, 0, owned:, here] = pieces.astype(jnp.bfloat16)


def parameter_shard(means, inv_var, log_weight):
    owned, feature_count = means.shape
    vmem = pl.BlockSpec(memory_space=pltpu.VMEM)
    hbm = pl.BlockSpec(memory_space=pltpu.HBM)
    return pl.pallas_call(
        shard_body,
        in_specs=[hbm, hbm, vmem],
        out_specs=vmem,
        out_shape=pltpu.VMEM((1, 2, owned + META, feature_count), jnp.bfloat16),
        scratch_shapes=[
            pltpu.VMEM((owned, feature_count), means.dtype),
            pltpu.VMEM((owned, feature_count), inv_var.dtype),
            pltpu.SemaphoreType.DMA((2,)),
        ],
        compiler_params=pltpu.CompilerParams(vmem_limit_bytes=VMEM_LIMIT),
        cost_estimate=pl.CostEstimate(
            flops=owned * feature_count * 40,
            bytes_accessed=owned * feature_count * 8,
            transcendentals=owned * feature_count,
        ),
        name="parameter_shard",
    )(in_hbm(means), in_hbm(inv_var), log_weight.reshape(1, owned))


def cut_body(cuts, points_ref, *refs):
    piece_refs, (staging, sems) = refs[:-2], refs[-2:]
    ways = []
    for j, piece in enumerate(piece_refs):
        here = pl.ds(cuts[j], piece.shape[0])
        there = pl.ds(cuts[j] - cuts[0], piece.shape[0])
        ways.append(
            (
                pltpu.make_async_copy(points_ref.at[here, :], staging.at[there, :], sems.at[0, j]),
                pltpu.make_async_copy(staging.at[there, :], piece, sems.at[1, j]),
            )
        )
    for inward, _ in ways:
        inward.start()
    for inward, outward in ways:
        inward.wait()
        outward.start()
    for _, outward in ways:
        outward.wait()


def cut_rows(points, cuts):
    feature_count = points.shape[1]
    hbm = pl.BlockSpec(memory_space=pltpu.HBM)
    lengths = [b - a for a, b in zip(cuts[:-1], cuts[1:])]
    return pl.pallas_call(
        functools.partial(cut_body, cuts),
        in_specs=[hbm],
        out_specs=[hbm] * len(lengths),
        out_shape=[pltpu.HBM((length, feature_count), points.dtype) for length in lengths],
        scratch_shapes=[
            pltpu.VMEM((sum(lengths), feature_count), points.dtype),
            pltpu.SemaphoreType.DMA((2, len(lengths))),
        ],
        compiler_params=pltpu.CompilerParams(vmem_limit_bytes=VMEM_LIMIT),
        name="cut_rows",
    )(in_hbm(points))


def density_body(first, count, held, pos_ref, x_ref, weight_ref, resp_ref, norm_ref):
    owned = held * CB
    row_index = lax.broadcasted_iota(jnp.int32, (META, RB), 0)
    pieces = jnp.where(row_index < 3, 1.0, 0.0).astype(jnp.bfloat16)

    @pl.loop(0, count)
    def _(i):
        x = x_ref[pl.ds(pl.multiple_of(i * RB, RB), RB), :]
        half = x * x * -0.5
        chosen = []
        for slot in range(CANDS):
            pos = pos_ref[(first + i) * CANDS + slot]
            start = pl.multiple_of(lax.rem(pos, held) * CB, CB)
            chosen.append((lax.div(pos, held), pl.ds(start, CB)))
        scaled = jnp.concatenate([weight_ref[shard, 0, here, :] for shard, here in chosen])
        inverse = jnp.concatenate([weight_ref[shard, 1, here, :] for shard, here in chosen])
        constants = jnp.concatenate(
            [weight_ref[shard, 0, owned:, here] for shard, here in chosen], axis=1
        )
        densities = lax.dot_general(scaled, x, NT, preferred_element_type=jnp.float32)
        densities += lax.dot_general(inverse, half, NT, preferred_element_type=jnp.float32)
        densities += lax.dot_general(constants, pieces, TN, preferred_element_type=jnp.float32)
        peak = jnp.max(densities, axis=0, keepdims=True)
        terms = jnp.exp(densities - peak)
        total = jnp.sum(terms, axis=0, keepdims=True)
        norm_ref[pl.ds(i, 1), :] = peak + jnp.log(total)
        resp = (terms * (1.0 / total)).astype(jnp.bfloat16)
        for slot in range(CANDS):
            resp_ref[i, slot] = resp[slot * CB : (slot + 1) * CB]


def responsibilities(rows, pos, first, weights, held):
    count = rows.shape[0] // RB
    feature_count = rows.shape[1]
    vmem = pl.BlockSpec(memory_space=pltpu.VMEM)
    pairs = count * CANDS
    return pl.pallas_call(
        functools.partial(density_body, first, count, held),
        in_specs=[pl.BlockSpec(memory_space=pltpu.SMEM), vmem, vmem],
        out_specs=[vmem, vmem],
        out_shape=[
            pltpu.VMEM((count, CANDS, CB, RB), jnp.bfloat16),
            pltpu.VMEM((count, RB), jnp.float32),
        ],
        compiler_params=pltpu.CompilerParams(vmem_limit_bytes=VMEM_LIMIT),
        cost_estimate=pl.CostEstimate(
            flops=pairs * 4 * CB * RB * feature_count,
            bytes_accessed=pairs * CB * feature_count * 4 + rows.size * 2,
            transcendentals=pairs * CB * RB,
        ),
        name="responsibilities",
    )(pos, in_vmem(rows), in_vmem(weights))


def list_body(runs, held, owners, place, known, *rest):
    where = [ref[0] for ref in rest[:known]]
    id_refs, (pos_ref, order_ref, start_ref, cursor) = rest[known:-4], rest[-4:]
    bins = start_ref.shape[0]
    number_of_runs = len(runs)
    per_ref = sum(runs) // len(id_refs)
    firsts = [sum(runs[:j]) for j in range(number_of_runs)]

    def run_of(i):
        return sum((i >= start).astype(jnp.int32) for start in firsts[1:]) if firsts[1:] else 0

    @pl.loop(0, bins)
    def _(j):
        start_ref[j] = 0

    for part, id_ref in enumerate(id_refs):

        @pl.loop(0, per_ref)
        def _(row, part=part, id_ref=id_ref):
            i = part * per_ref + row
            for slot in range(CANDS):
                block = id_ref[slot, row]
                holder = place(lax.div(block, owners * held), *where)
                pos = holder * held + lax.rem(block, held)
                pos_ref[i * CANDS + slot] = pos
                key = pos * number_of_runs + run_of(i) + 1
                start_ref[key] = start_ref[key] + 1

    def prefix(j, total):
        total = total + start_ref[j]
        start_ref[j] = total
        cursor[j] = total
        return total

    lax.fori_loop(0, bins, prefix, jnp.int32(0))

    @pl.loop(0, sum(runs))
    def _(i):
        for slot in range(CANDS):
            key = pos_ref[i * CANDS + slot] * number_of_runs + run_of(i)
            order_ref[cursor[key]] = i * CANDS + slot
            cursor[key] = cursor[key] + 1


def pair_lists(candidates, runs, held, group_blocks, owners, place, where):
    smem = pl.BlockSpec(memory_space=pltpu.SMEM)
    pairs = sum(runs) * CANDS
    bins = group_blocks * len(runs) + 1
    return pl.pallas_call(
        functools.partial(list_body, tuple(runs), held, owners, place, len(where)),
        in_specs=[smem] * (len(where) + len(candidates)),
        out_specs=[smem] * 3,
        out_shape=[jax.ShapeDtypeStruct((n,), jnp.int32) for n in (pairs, pairs, bins)],
        scratch_shapes=[pltpu.SMEM((bins,), jnp.int32)],
        compiler_params=pltpu.CompilerParams(vmem_limit_bytes=VMEM_LIMIT),
        name="pair_lists",
    )(*where, *candidates)


def moment_body(shards, held, runs, order_ref, start_ref, *rest):
    parts, outs = len(runs), len(shards)
    row_refs, resp_refs = rest[:parts], rest[parts : 2 * parts]
    out_refs = rest[2 * parts : 2 * parts + outs]
    sums, count_sum = rest[2 * parts + outs :]
    owned = held * CB
    meta = slice(2 * owned, 2 * owned + META)
    ones = jnp.ones((META, 2 * RB), jnp.bfloat16)

    def block_sums(pos):
        sums[...] = jnp.zeros_like(sums)
        count_sum[...] = jnp.zeros_like(count_sum)
        base = 0
        for run in range(parts):
            entry = pos * parts + run
            low, high = start_ref[entry], start_ref[entry + 1]

            @pl.loop(0, lax.div(high - low + 1, 2))
            def _(step, base=base, run=run, low=low, high=high):
                one = low + 2 * step
                two = jnp.minimum(one + 1, high - 1)
                valid = (one + 1 < high).astype(jnp.float32)
                pair_a, pair_b = order_ref[one] - base, order_ref[two] - base
                row_a, row_b = lax.div(pair_a, CANDS), lax.div(pair_b, CANDS)
                weight_a = resp_refs[run][row_a, lax.rem(pair_a, CANDS)]
                weight_b = resp_refs[run][row_b, lax.rem(pair_b, CANDS)]
                weight_b = (weight_b.astype(jnp.float32) * valid).astype(jnp.bfloat16)
                weight = jnp.concatenate([weight_a, weight_b], axis=1)
                x = jnp.concatenate(
                    [
                        row_refs[run][pl.ds(pl.multiple_of(row_a * RB, RB), RB), :],
                        row_refs[run][pl.ds(pl.multiple_of(row_b * RB, RB), RB), :],
                    ],
                    axis=0,
                )
                sums[0] += jnp.dot(weight, x, preferred_element_type=jnp.float32)
                sums[1] += jnp.dot(weight, x * x, preferred_element_type=jnp.float32)
                count_sum[...] += lax.dot_general(
                    ones, weight, NT, preferred_element_type=jnp.float32
                )

            base += runs[run] * CANDS

    for shard, out_ref in zip(shards, out_refs):
        out_ref[meta, :] = jnp.zeros((META, out_ref.shape[1]), jnp.bfloat16)

        @pl.loop(0, held)
        def _(block, shard=shard, out_ref=out_ref):
            block_sums(shard * held + block)
            start = pl.multiple_of(block * CB, CB)
            out_ref[pl.ds(start, CB), :] = sums[0].astype(jnp.bfloat16)
            out_ref[pl.ds(owned + start, CB), :] = sums[1].astype(jnp.bfloat16)
            out_ref[meta, pl.ds(start, CB)] = count_sum[...].astype(jnp.bfloat16)


def moments(rows, resp, order, starts, held, shards):
    runs = tuple(r.shape[0] // RB for r in rows)
    feature_count = rows[0].shape[1]
    smem = pl.BlockSpec(memory_space=pltpu.SMEM)
    vmem = pl.BlockSpec(memory_space=pltpu.VMEM)
    pairs = sum(runs) * held * len(shards) // 8
    out_shape = pltpu.VMEM((2 * held * CB + META, feature_count), jnp.bfloat16)
    return pl.pallas_call(
        functools.partial(moment_body, tuple(shards), held, runs),
        in_specs=[smem, smem] + [vmem] * (2 * len(runs)),
        out_specs=[vmem] * len(shards),
        out_shape=[out_shape] * len(shards),
        scratch_shapes=[
            pltpu.VMEM((2, CB, feature_count), jnp.float32),
            pltpu.VMEM((META, CB), jnp.float32),
        ],
        compiler_params=pltpu.CompilerParams(vmem_limit_bytes=VMEM_LIMIT),
        cost_estimate=pl.CostEstimate(
            flops=pairs * 4 * CB * RB * feature_count,
            bytes_accessed=pairs * RB * (feature_count + CB) * 2,
            transcendentals=0,
        ),
        name="moments",
    )(order, starts, *[in_vmem(r) for r in rows], *[in_vmem(r) for r in resp])


CHUNK = 16


def each_chunk(rows, step):
    whole = rows // CHUNK

    @pl.loop(0, whole)
    def _(i):
        step(pl.ds(pl.multiple_of(i * CHUNK, 16), CHUNK))

    if rows % CHUNK:
        step(slice(whole * CHUNK, rows))


def copy_body(places, skip, *refs):
    sources, target, sems = refs[skip:-2], refs[-2], refs[-1]
    copies = [
        pltpu.make_async_copy(source.at[0], target.at[index], sems.at[j])
        for j, (index, source) in enumerate(zip(places, sources))
    ]
    for copy in copies:
        copy.start()
    for copy in copies:
        copy.wait()


def stacked(total, places, shards, *earlier):
    vmem = pl.BlockSpec(memory_space=pltpu.VMEM)
    anywhere = pl.BlockSpec(memory_space=pl.ANY)
    return pl.pallas_call(
        functools.partial(copy_body, places, len(earlier)),
        in_specs=[vmem] * len(earlier) + [anywhere] * len(shards),
        out_specs=vmem,
        out_shape=pltpu.VMEM((total,) + shards[0].shape[1:], jnp.bfloat16),
        scratch_shapes=[pltpu.SemaphoreType.DMA((len(shards),))],
        input_output_aliases={0: 0} if earlier else {},
        compiler_params=pltpu.CompilerParams(vmem_limit_bytes=VMEM_LIMIT),
        name="stack_shards",
    )(*[in_vmem(e) for e in earlier], *shards)


def add_body(*refs):
    def step(here):
        terms = [ref[here, :].astype(jnp.float32) for ref in refs[:-1]]
        refs[-1][here, :] = functools.reduce(jnp.add, terms).astype(jnp.bfloat16)

    each_chunk(refs[-1].shape[0], step)


def add_two_body(a_ref, b_ref, c_ref, d_ref, e_ref, first_ref, second_ref):
    def step(here):
        first = a_ref[here, :].astype(jnp.float32) + b_ref[here, :].astype(jnp.float32)
        first_ref[here, :] = first.astype(jnp.bfloat16)
        second = c_ref[here, :].astype(jnp.float32) + d_ref[here, :].astype(jnp.float32)
        second_ref[here, :] = (second + e_ref[here, :].astype(jnp.float32)).astype(jnp.bfloat16)

    each_chunk(first_ref.shape[0], step)


def added_two(*terms):
    vmem = pl.BlockSpec(memory_space=pltpu.VMEM)
    shape = terms[0].shape
    return pl.pallas_call(
        add_two_body,
        in_specs=[vmem] * 5,
        out_specs=[vmem] * 2,
        out_shape=[pltpu.VMEM(shape, jnp.bfloat16)] * 2,
        compiler_params=pltpu.CompilerParams(vmem_limit_bytes=12 * 1024 * 1024),
        name="add_both_sums",
    )(*[in_vmem(value) for value in terms])


def join_body(*refs):
    start = 0
    for ref in refs[:-1]:
        refs[-1][start : start + ref.shape[0], :] = ref[...]
        start += ref.shape[0]


def small_step(body, shape, dtype, name, *operands):
    vmem = pl.BlockSpec(memory_space=pltpu.VMEM)
    return pl.pallas_call(
        body,
        in_specs=[vmem] * len(operands),
        out_specs=vmem,
        out_shape=pltpu.VMEM(shape, dtype),
        compiler_params=pltpu.CompilerParams(vmem_limit_bytes=VMEM_LIMIT),
        cost_estimate=pl.CostEstimate(
            flops=math.prod(shape), bytes_accessed=2 * math.prod(shape), transcendentals=0
        ),
        name=name,
    )(*[in_vmem(value) for value in operands])


def added(*terms):
    return small_step(add_body, terms[0].shape, jnp.bfloat16, "add_sums", *terms)


def joined(*norms):
    shape = (sum(n.shape[0] for n in norms), RB)
    return small_step(join_body, shape, jnp.float32, "join_norms", *norms)


def result_body(owned, end_ref, *refs):
    own_norm, end_norm, end_sum = refs[:3]
    terms, (count_ref, first_ref, second_ref, loglik_ref) = refs[3:-4], refs[-4:]
    is_end = end_ref[0] > 0
    block = pl.program_id(0)
    feature_count = first_ref.shape[1]

    def total(rows):
        inner = functools.reduce(jnp.add, [t[rows, :].astype(jnp.float32) for t in terms])
        return jnp.where(is_end, end_sum[rows, :].astype(jnp.float32), inner)

    start = pl.multiple_of(block * CB, CB)
    first_ref[...] = total(pl.ds(start, CB))
    second_ref[...] = total(pl.ds(owned + start, CB))
    count_ref[...] = total(slice(2 * owned, 2 * owned + META))[0:1, :owned]
    norm = jnp.where(is_end, end_norm[...], own_norm[...])
    loglik_ref[...] = norm * (1.0 / feature_count)


def results_of(is_end, own_norm, end_norm, end_sum, *terms):
    rows, feature_count = end_sum.shape
    owned = (rows - META) // 2
    vmem = pl.BlockSpec(memory_space=pltpu.VMEM)
    operands = (own_norm, end_norm, end_sum) + terms
    return pl.pallas_call(
        functools.partial(result_body, owned),
        grid=(owned // CB,),
        in_specs=[pl.BlockSpec(memory_space=pltpu.SMEM)] + [vmem] * len(operands),
        out_specs=[
            pl.BlockSpec((1, owned), lambda i: (0, 0)),
            pl.BlockSpec((CB, feature_count), lambda i: (i, 0)),
            pl.BlockSpec((CB, feature_count), lambda i: (i, 0)),
            pl.BlockSpec(own_norm.shape, lambda i: (0, 0)),
        ],
        out_shape=[
            jax.ShapeDtypeStruct((1, owned), jnp.float32),
            jax.ShapeDtypeStruct((owned, feature_count), jnp.float32),
            jax.ShapeDtypeStruct((owned, feature_count), jnp.float32),
            jax.ShapeDtypeStruct(own_norm.shape, jnp.float32),
        ],
        compiler_params=pltpu.CompilerParams(vmem_limit_bytes=VMEM_LIMIT),
        name="results",
    )(is_end.astype(jnp.int32).reshape(1), *[in_vmem(value) for value in operands])


def plain_plan(points, candidates, parameters, held):
    weights = parameter_shard(*parameters)
    dp_size = lax.axis_size("dp")
    row_blocks = points.shape[0] // RB
    pos, order, starts = pair_lists(
        [candidates.T],
        (row_blocks,),
        held,
        dp_size * held,
        lax.axis_size("comp"),
        lambda holder: holder,
        [],
    )
    all_weights = lax.all_gather(weights, "dp", axis=0, tiled=True)
    resp, norm = responsibilities(points, pos, 0, all_weights, held)
    sums = []
    for j in range(dp_size):
        sums += moments([points], [resp], order, starts, held, [j])
    total = lax.psum_scatter(jnp.concatenate(sums), "dp", scatter_dimension=0, tiled=True)
    total = total.astype(jnp.float32)
    owned = held * CB
    counts, first, second = total[2 * owned, :owned], total[:owned], total[owned : 2 * owned]
    return counts, first, second, norm.reshape(-1) / points.shape[1]


def line_pairs(links):
    return [(2 * a + c, 2 * b + c) for a, b in links for c in (0, 1)]


INWARD = line_pairs(((0, 1), (3, 2)))
OUTWARD = line_pairs(((1, 0), (2, 3)))
MIDDLE = line_pairs(((1, 2), (2, 1)))
CORES = [(2, 3), (3, 2), (4, 5), (5, 4)]


def move(value, pairs):
    return lax.ppermute(value, "dp", pairs)


def after(value, *others):
    return lax.optimization_barrier((value,) + others)[0]


def line_place(holder, chip, core):
    z, other = lax.div(holder, 2), lax.rem(holder, 2)
    z = jnp.where(chip < 2, z, 3 - z)
    z = jnp.where(z == 0, 1, jnp.where(z == 1, 0, z))
    return z * 2 + lax.rem(other + core, 2)


def line_plan(points, candidates, parameters, held):
    index = lax.axis_index("dp")
    chip, core = index // 2, index % 2
    where = [chip.reshape(1), core.reshape(1)]
    row_blocks = points.shape[0] // RB
    small = row_blocks // 8
    cuts = (0, 1 + 4 * small, row_blocks - 1, row_blocks)
    runs = (row_blocks,) + tuple(b - a for a, b in zip(cuts[:-1], cuts[1:]))
    own_ids = candidates.T
    end_ids = move(own_ids, INWARD)
    weights = parameter_shard(*parameters)
    weights_then, end_ids = lax.optimization_barrier((weights, end_ids))

    outer = move(weights_then, INWARD)
    across = move(weights, MIDDLE)
    pieces = cut_rows(after(points, weights_then), [cut * RB for cut in cuts])
    own_shared = move(after(weights, *pieces), CORES)
    most = move(after(pieces[0], outer), INWARD)
    far = move(outer, MIDDLE)
    moved = [most] + [move(after(piece, far), INWARD) for piece in pieces[1:]]
    pos, order, starts = pair_lists(
        [own_ids, end_ids], runs, held, 8 * held, lax.axis_size("comp"), line_place, where
    )
    near = [after(weights, pos, order, starts), own_shared, outer, across]
    near_weights = stacked(8, (0, 1, 2, 4), near)
    far, near_weights = lax.optimization_barrier((far, near_weights))
    shared = [move(w, CORES) for w in (outer, across, far)]
    all_weights = stacked(8, (6, 3, 5, 7), [after(far, most)] + shared, near_weights)

    rows = [points] + moved
    results = []
    for j, run_rows in enumerate(rows):
        if results:
            pos = after(pos, results[-1][1])
        results.append(responsibilities(run_rows, pos, sum(runs[:j]), all_weights, held))
    resp = [r[0] for r in results]

    def sums_of(position, *earlier):
        return moments(rows, resp, after(order, *earlier), starts, held, [position])[0]

    far_other = sums_of(7)
    far_received = move(far_other, CORES)
    far_own = sums_of(6, far_other)
    far_part = added(far_own, far_received)
    far_sum = move(far_part, MIDDLE)
    across_other = sums_of(5, far_part)
    across_received = move(across_other, CORES)
    outer_other = sums_of(3, across_other)
    outer_received = move(outer_other, CORES)
    end_norm = move(after(joined(*[r[1] for r in results[1:]]), across_other), OUTWARD)
    across_own = sums_of(4, outer_other)
    outer_own = sums_of(2, across_own, end_norm)
    far_sum, outer_own, across_own = lax.optimization_barrier((far_sum, outer_own, across_own))
    across_part, outer_sum = added_two(
        across_own, across_received, outer_own, outer_received, far_sum
    )
    across_sum = move(across_part, MIDDLE)
    end_sum = move(outer_sum, OUTWARD)
    own_other = sums_of(1, across_part, outer_sum)
    own_received = move(own_other, CORES)
    own_own = sums_of(0, own_other)
    across_sum, end_sum, own_own = lax.optimization_barrier((across_sum, end_sum, own_own))
    is_end = jnp.logical_or(chip == 0, chip == 3)
    counts, first, second, loglik = results_of(
        is_end, results[0][1], end_norm, end_sum, own_own, own_received, across_sum
    )
    return counts.reshape(-1), first, second, loglik.reshape(-1)


def on_device(points, candidates, means, inv_var, log_weight):
    held = means.shape[0] // CB
    plan = line_plan if lax.axis_size("dp") == 8 else plain_plan
    return plan(points, candidates, (means, inv_var, log_weight), held)


def solution(mesh):
    return jax.shard_map(
        on_device,
        mesh=mesh,
        in_specs=(
            P(("dp", "comp"), None),
            P(("dp", "comp"), None),
            P(("dp", "comp"), None),
            P(("dp", "comp"), None),
            P(("dp", "comp")),
        ),
        out_specs=(
            P(("dp", "comp")),
            P(("dp", "comp"), None),
            P(("dp", "comp"), None),
            P(("dp", "comp")),
        ),
        check_vma=False,
    )
```
